32 devices in a mesh: head: 4 (over y, core), blk: 8 (over z, x).
Axes of the slice: x: 2, y: 2, z: 4, core: 2. Of those that a mesh axis runs over, the one named last changes fastest.
Arguments:
- first_half: bfloat16 [6144, 1024], P(('head', 'blk')), may hold values from -6 to 6
- second_half: bfloat16 [6144, 1024], P(('head', 'blk')), may hold values from -6 to 6
- grad_first: bfloat16 [6144, 1024], P(('head', 'blk')), may hold values from -6 to 6
- grad_second: bfloat16 [6144, 1024], P(('head', 'blk')), may hold values from -6 to 6
- qk_weight: bfloat16 [1024, 1024], P(('head', 'blk')), may hold values from -0.375 to 0.375
- value_weight: bfloat16 [1024, 1024], P(('head', 'blk')), may hold values from -0.1875 to 0.1875
- out_weight: bfloat16 [1024, 1024], P(('head', 'blk')), may hold values from -1.5 to 1.5
- attn_gain: bfloat16 [1024], P(('head', 'blk')), may hold values from 0.5 to 1.5
- ffn_gain: bfloat16 [1024], P(('head', 'blk')), may hold values from 0.5 to 1.5
- up_weight: bfloat16 [1024, 4096], P(None, ('head', 'blk')), may hold values from -0.1875 to 0.1875
- down_weight: bfloat16 [4096, 1024], P(('head', 'blk')), may hold values from -0.09375 to 0.09375
- stretch_ids: int32 [4, 6144], replicated, may hold values from 0 to 95, as said below
Outputs:
- y_first: bfloat16 [6144, 1024], P(('head', 'blk'))
- y_second: bfloat16 [6144, 1024], P(('head', 'blk'))
- grad_first_half: bfloat16 [6144, 1024], P(('head', 'blk'))
- grad_second_half: bfloat16 [6144, 1024], P(('head', 'blk'))
- grad_qk_weight: float32 [1024, 1024], P(('head', 'blk'))
- grad_value_weight: float32 [1024, 1024], P(('head', 'blk'))
- grad_out_weight: float32 [1024, 1024], P(('head', 'blk'))
- grad_attn_gain: float32 [1024], P(('head', 'blk'))
- grad_ffn_gain: float32 [1024], P(('head', 'blk'))
- grad_up_weight: float32 [1024, 4096], P(None, ('head', 'blk'))
- grad_down_weight: float32 [4096, 1024], P(('head', 'blk'))
The draws below stay inside these ranges and needn't reach their ends.
Inputs may be any that keep to these rules, and one draw needn't show every extreme that they name: `stretch_ids`: in each of the 4 rounds every stretch number from 0 to 95 is held by exactly 64 tokens. In each round, of the tokens k * 192 to (k + 1) * 192 - 1 at most 6 have stretch numbers in any one range m * 3 to (m + 1) * 3 - 1, and some range holds exactly 6 of them.
All inputs are finite; a program needn't handle non-finite values.
Results may differ from the reference program's by a relative error of at most 0.017.
Values may be sent and summed in bfloat16 or wider, within the bound.
No kernel may reach another device: no remote copies, remote signals or barrier semaphores. Data moves between devices by JAX's collectives and lax.ppermute only.
A program may use at most 128 MiB of HBM per device.

```python
import math
import jax
import jax.numpy as jnp
from jax import lax

D = 1024
FF = 4096
NH = 8
DH = 128
ROUNDS = 4
STRETCH = 64
TOK_DEV = 192
TOKENS = 6144


def draw_stretch_ids(key, part):
    devices = TOKENS // TOK_DEV
    local = jnp.arange(TOK_DEV, dtype=jnp.int32)
    ranked = []
    for hashing in range(ROUNDS):
        round_key = jax.random.fold_in(key, hashing + 11)
        subkeys = jax.random.split(round_key, 5)
        starts = jax.random.randint(subkeys[0], (devices,), 0, TOK_DEV).astype(jnp.int32)
        spread = jax.random.permutation(subkeys[1], devices).astype(jnp.int32)
        target_order = jax.random.permutation(subkeys[2], devices).astype(jnp.int32)
        source_order = jax.random.permutation(subkeys[3], devices).astype(jnp.int32)
        slots = jax.random.permutation(subkeys[4], TOK_DEV).astype(jnp.int32)
        offset_index = (local[None, :] + starts[:, None]) % TOK_DEV
        offsets = spread[offset_index % devices]
        target = target_order[(source_order[:, None] + offsets) % devices]
        position = target * TOK_DEV + slots[offset_index]
        ranked.append((position // STRETCH).reshape(TOKENS).astype(jnp.int32))
    return jnp.stack(ranked)


def levels(rng, shape, pieces, low, top_value):
    loudness, own = 1.0, jax.random.fold_in(rng, 6)
    for dim, shards_of in pieces:
        draws = jnp.exp(jax.random.uniform(jax.random.fold_in(own, dim), (shards_of,), jnp.float32, low / len(pieces), top_value / len(pieces)))
        loudness = loudness * jnp.repeat(draws, shape[dim] // shards_of).reshape([-1 if axis == dim else 1 for axis in range(len(shape))])
    return loudness


def normal_values(own_key, dims, width, reach, pieces=(), held_as=jnp.bfloat16):
    factor_of = levels(own_key, dims, pieces, -0.22, 0.18) if pieces else 1.0
    entries = jax.random.normal(own_key, dims, jnp.float32) * width * factor_of
    return jnp.minimum(jnp.maximum(entries, -reach), reach).astype(held_as)


def setup_inputs(seed: int = 0) -> dict:
    key_of = jax.random.split(jax.random.key(seed), 13)
    return {
        "first_half": normal_values(key_of[0], (TOKENS, D), 1.0, 6.0, ((0, 32),)),
        "second_half": normal_values(key_of[1], (TOKENS, D), 1.0, 6.0, ((0, 32),)),
        "grad_first": normal_values(key_of[2], (TOKENS, D), 1.0, 6.0, ((0, 32),)),
        "grad_second": normal_values(key_of[3], (TOKENS, D), 1.0, 6.0, ((0, 32),)),
        "qk_weight": normal_values(key_of[4], (D, D), (D // 4) ** -0.5, 0.375, ((0, 32),)),
        "value_weight": normal_values(key_of[5], (D, D), D ** -0.5, 0.1875, ((0, 32),)),
        "out_weight": normal_values(key_of[6], (D, D), (D // 64) ** -0.5, 1.5, ((0, 32),)),
        "attn_gain": jnp.clip(1.0 + 0.1 * jax.random.normal(key_of[7], (D,), jnp.float32), 0.5, 1.5).astype(jnp.bfloat16),
        "ffn_gain": jnp.clip(1.0 + 0.1 * jax.random.normal(key_of[8], (D,), jnp.float32), 0.5, 1.5).astype(jnp.bfloat16),
        "up_weight": normal_values(key_of[9], (D, FF), D ** -0.5, 0.1875, ((1, 32),)),
        "down_weight": normal_values(key_of[10], (FF, D), FF ** -0.5, 0.09375, ((0, 32),)),
        "stretch_ids": draw_stretch_ids(jax.random.fold_in(key_of[12], 71), 0),
    }


@jax.custom_vjp
def low(v):
    return lax.optimization_barrier(v.astype(jnp.bfloat16)).astype(jnp.float32)

@jax.custom_vjp
def low_back(v):
    return v

def low_keep(v):
    return (low(v), None)

def low_pass(kept, grad):
    return (grad,)

def back_keep(v):
    return (v, None)

def back_low(kept, grad):
    return (low(grad),)
low.defvjp(low_keep, low_pass)
low_back.defvjp(back_keep, back_low)

def layer_norm(values, gains):
    average = lax.optimization_barrier(jnp.mean(values, axis=-1, keepdims=True))
    centred = values - average
    variance = lax.optimization_barrier(jnp.mean(centred * centred, axis=-1, keepdims=True))
    return centred * lax.rsqrt(variance + 1e-05) * gains

def key_norm(queries):
    return queries * lax.rsqrt(lax.optimization_barrier(jnp.mean(queries * queries, axis=-1, keepdims=True)) + 1e-06) * queries.shape[-1] ** (-0.5)

def row_norm(queries):
    return jnp.sqrt(lax.optimization_barrier(jnp.sum(queries * queries, axis=-1)) + 1e-06)

def matmul(left, right):
    return jnp.dot(left, right, precision=lax.Precision.HIGHEST, preferred_element_type=jnp.float32)

def forward(first_half, second_half, qk_weight, value_weight, out_weight, attn_gain, ffn_gain, up_weight, down_weight, stretch_ids):
    tokens = first_half.shape[0]
    normed = low(layer_norm(second_half, attn_gain))
    queries = low(low_back(matmul(normed, qk_weight))).reshape(tokens, NH, DH)
    values = low(low_back(matmul(normed, value_weight))).reshape(tokens, NH, DH)
    keys = low(key_norm(queries))
    query_norms = row_norm(queries)
    nchunk = tokens // STRETCH
    positions = jnp.arange(tokens, dtype=jnp.int32)
    block_rows = math.gcd(tokens, 512)

    def attend(start_row):
        query_block = lax.dynamic_slice_in_dim(queries, start_row, block_rows, 0)
        norm_block = lax.dynamic_slice_in_dim(query_norms, start_row, block_rows, 0)
        own_ids = lax.dynamic_slice_in_dim(stretch_ids, start_row, block_rows, 1)
        previous = (own_ids + nchunk - 1) % nchunk
        same_stretch = stretch_ids[:, None, :] == own_ids[:, :, None]
        before = stretch_ids[:, None, :] == previous[:, :, None]
        counts = lax.optimization_barrier(jnp.sum((same_stretch | before).astype(jnp.float32), axis=0))
        own_places = start_row + jnp.arange(block_rows, dtype=jnp.int32)
        counts = counts * (own_places[:, None] != positions[None, :]).astype(jnp.float32)
        scores = low_back(jnp.einsum('qhd,khd->hqk', query_block, keys, precision=lax.Precision.HIGHEST))
        weights = counts[None] * jnp.exp(scores - norm_block.T[:, :, None])
        totals = lax.optimization_barrier(jnp.sum(weights, axis=-1))
        summed = low_back(jnp.einsum('hqk,khd->qhd', low(weights), values, precision=lax.Precision.HIGHEST))
        return summed / totals.T[:, :, None]
    starts = jnp.arange(tokens // block_rows, dtype=jnp.int32) * block_rows
    outputs = lax.map(jax.checkpoint(attend), starts)
    attn = low(low_back(outputs.reshape(tokens, D)))
    first_out = first_half + low_back(matmul(attn, out_weight))
    normed_ffn = low(layer_norm(first_out, ffn_gain))
    hidden = low(jax.nn.gelu(low_back(matmul(normed_ffn, up_weight))))
    second_out = second_half + matmul(hidden, down_weight)
    return (first_out, second_out)

def reference(first_half, second_half, grad_first, grad_second, qk_weight, value_weight, out_weight, attn_gain, ffn_gain, up_weight, down_weight, stretch_ids):
    floats = [array.astype(jnp.float32) for array in (first_half, second_half, qk_weight, value_weight, out_weight, attn_gain, ffn_gain, up_weight, down_weight)]

    def wrapped(*arrays):
        return forward(*arrays, stretch_ids)
    outputs, pullback = jax.vjp(wrapped, *floats)
    gradients = pullback((grad_first.astype(jnp.float32), grad_second.astype(jnp.float32)))
    return (outputs[0].astype(jnp.bfloat16), outputs[1].astype(jnp.bfloat16), gradients[0].astype(jnp.bfloat16), gradients[1].astype(jnp.bfloat16), gradients[2], gradients[3], gradients[4], gradients[5], gradients[6], gradients[7], gradients[8])
```

```python
import functools

import jax
import jax.numpy as jnp
from jax import lax
from jax.experimental import pallas as pl
from jax.experimental.pallas import tpu as pltpu
from jax.sharding import PartitionSpec as P

NH = 8
DH = 128
STRETCH = 64


def shifted(value, axis, by):
    devices = lax.axis_size(axis)
    return lax.ppermute(value, axis, [(i, (i + by) % devices) for i in range(devices)])


def layer_norm(values, gains):
    average = jnp.mean(values, axis=-1, keepdims=True)
    centred = values - average
    variance = jnp.mean(centred * centred, axis=-1, keepdims=True)
    return centred * lax.rsqrt(variance + 1e-05) * gains


def key_norm(queries):
    return (
        queries
        * lax.rsqrt(jnp.mean(queries * queries, axis=-1, keepdims=True) + 1e-06)
        * queries.shape[-1] ** (-0.5)
    )


def row_norm(queries):
    return jnp.sqrt(jnp.sum(queries * queries, axis=-1) + 1e-06)


def group_ids(stretch_ids, heads_count, cycle_count, local_rows, cycle_index):
    shaped = stretch_ids.reshape(stretch_ids.shape[0], heads_count, cycle_count, local_rows)
    picked = lax.dynamic_slice_in_dim(shaped, cycle_index, 1, 2)
    places = (
        jnp.arange(heads_count, dtype=jnp.int32)[:, None] * cycle_count + cycle_index
    ) * local_rows
    places = places + jnp.arange(local_rows, dtype=jnp.int32)[None, :]
    return (picked.reshape(stretch_ids.shape[0], heads_count * local_rows), places.reshape(-1))


def pair_counts(query_ids, query_places, key_ids, key_places, nchunk):
    previous = (query_ids + nchunk - 1) % nchunk
    same_stretch = key_ids[:, None, :] == query_ids[:, :, None]
    before = key_ids[:, None, :] == previous[:, :, None]
    counts = jnp.sum((same_stretch | before).astype(jnp.float32), axis=0)
    return counts * (query_places[:, None] != key_places[None, :]).astype(jnp.float32)


def forward_block(queries, query_norms, counts, key_block, value_block):
    scores = jnp.einsum("qhd,khd->hqk", queries, key_block, preferred_element_type=jnp.float32)
    weights = counts[None] * jnp.exp(scores - query_norms.T[:, :, None])
    summed = jnp.einsum(
        "hqk,khd->qhd",
        weights.astype(jnp.bfloat16),
        value_block,
        preferred_element_type=jnp.float32,
    )
    return (jnp.sum(weights, axis=-1), summed)


def backward_block(queries, query_norms, counts, key_block, value_block, grad_summed, grad_totals):
    scores = jnp.einsum("qhd,khd->hqk", queries, key_block, preferred_element_type=jnp.float32)
    weights = counts[None] * jnp.exp(scores - query_norms.T[:, :, None])
    grad_weights = jnp.einsum(
        "qhd,khd->hqk", grad_summed, value_block, preferred_element_type=jnp.float32
    )
    grad_scores_f = weights * (grad_weights + grad_totals[:, :, None])
    grad_scores = grad_scores_f.astype(jnp.bfloat16)
    grad_norms = -jnp.sum(grad_scores_f, axis=-1)
    grad_values = jnp.einsum(
        "hqk,qhd->khd",
        weights.astype(jnp.bfloat16),
        grad_summed,
        preferred_element_type=jnp.float32,
    )
    grad_direct = jnp.einsum(
        "hqk,khd->qhd", grad_scores, key_block, preferred_element_type=jnp.float32
    )
    grad_keys = jnp.einsum("hqk,qhd->khd", grad_scores, queries, preferred_element_type=jnp.float32)
    return (grad_norms, grad_direct, grad_keys, grad_values)


def feed_forward(normed_ffn, grad_output, up_part, down_part):
    pre_act = jnp.dot(normed_ffn, up_part, preferred_element_type=jnp.float32)
    hidden_f, gelu_back = jax.vjp(jax.nn.gelu, pre_act)
    hidden = hidden_f.astype(jnp.bfloat16)
    ffn_result = jnp.dot(hidden, down_part, preferred_element_type=jnp.float32)
    grad_hidden = jnp.dot(grad_output, down_part.T, preferred_element_type=jnp.float32)
    grad_pre = gelu_back(grad_hidden)[0].astype(jnp.bfloat16)
    grad_normed = jnp.dot(grad_pre, up_part.T, preferred_element_type=jnp.float32)
    grad_up = jnp.dot(normed_ffn.T, grad_pre, preferred_element_type=jnp.float32)
    grad_down = jnp.dot(hidden.T, grad_output, preferred_element_type=jnp.float32)
    return (ffn_result, grad_normed, grad_up, grad_down)


def ring_plan(
    first_half,
    second_half,
    grad_first,
    grad_second,
    qk_weight,
    value_weight,
    out_weight,
    attn_gain,
    ffn_gain,
    up_weight,
    down_weight,
    stretch_ids,
):
    heads_count = lax.axis_size("head")
    cycle_count = lax.axis_size("blk")
    cycle_index = lax.axis_index("blk")
    local_rows = first_half.shape[0]
    model_width = first_half.shape[1]
    group_rows = local_rows * heads_count
    local_heads = NH // heads_count
    nchunk = stretch_ids.shape[1] // STRETCH
    full_qk, full_value, full_out, full_attn_gain, full_ffn_gain, up_part, down_part = (
        lax.all_gather(qk_weight, ("head", "blk"), axis=0, tiled=True),
        lax.all_gather(value_weight, ("head", "blk"), axis=0, tiled=True),
        lax.all_gather(out_weight, ("head", "blk"), axis=0, tiled=True),
        lax.all_gather(attn_gain, ("head", "blk"), axis=0, tiled=True),
        lax.all_gather(ffn_gain, ("head", "blk"), axis=0, tiled=True),
        lax.all_gather(up_weight, ("head", "blk"), axis=1, tiled=True),
        lax.all_gather(down_weight, ("head", "blk"), axis=0, tiled=True),
    )
    second_f = second_half.astype(jnp.float32)
    normed_f, attn_norm_back = jax.vjp(layer_norm, second_f, full_attn_gain.astype(jnp.float32))
    normed = normed_f.astype(jnp.bfloat16)
    query_tok = jnp.dot(normed, full_qk, preferred_element_type=jnp.float32).astype(jnp.bfloat16)
    value_tok = jnp.dot(normed, full_value, preferred_element_type=jnp.float32).astype(jnp.bfloat16)
    query_heads = query_tok.reshape(local_rows, NH, DH)
    value_heads = value_tok.reshape(local_rows, NH, DH)
    queries, values = (
        lax.all_to_all(query_heads, "head", split_axis=1, concat_axis=0, tiled=True),
        lax.all_to_all(value_heads, "head", split_axis=1, concat_axis=0, tiled=True),
    )
    query_f = queries.astype(jnp.float32)
    key_f, key_back = jax.vjp(key_norm, query_f)
    keys = key_f.astype(jnp.bfloat16)
    query_norms, norm_back = jax.vjp(row_norm, query_f)
    query_ids, query_places = group_ids(
        stretch_ids, heads_count, cycle_count, local_rows, cycle_index
    )

    def counts_for(cycle_step):
        source_index = (cycle_index - cycle_step + cycle_count) % cycle_count
        key_ids, key_places = group_ids(
            stretch_ids, heads_count, cycle_count, local_rows, source_index
        )
        return pair_counts(query_ids, query_places, key_ids, key_places, nchunk)

    def rotate(key_block, value_block):
        return shifted((key_block, value_block), "blk", 1)

    def forward_step(cycle_step, carried):
        key_block, value_block, totals, summed = carried
        part_totals, part_summed = forward_block(
            queries, query_norms, counts_for(cycle_step), key_block, value_block
        )
        key_next, value_next = rotate(key_block, value_block)
        return (key_next, value_next, totals + part_totals, summed + part_summed)

    initial = (
        keys,
        values,
        jnp.zeros((local_heads, group_rows), jnp.float32),
        jnp.zeros((group_rows, local_heads, DH), jnp.float32),
    )
    key_block, value_block, totals, summed = lax.fori_loop(
        0, cycle_count - 1, forward_step, initial
    )
    part_totals, part_summed = forward_block(
        queries, query_norms, counts_for(cycle_count - 1), key_block, value_block
    )
    totals = totals + part_totals
    summed = summed + part_summed
    attended = summed / totals.T[:, :, None]
    attn_tok = lax.all_to_all(
        attended.astype(jnp.bfloat16), "head", split_axis=0, concat_axis=1, tiled=True
    ).reshape(local_rows, model_width)
    first_out = first_half.astype(jnp.float32) + jnp.dot(
        attn_tok, full_out, preferred_element_type=jnp.float32
    )
    normed_ffn_f, ffn_norm_back = jax.vjp(layer_norm, first_out, full_ffn_gain.astype(jnp.float32))
    normed_ffn = normed_ffn_f.astype(jnp.bfloat16)
    ffn_result, grad_normed_ffn, grad_up, grad_down = feed_forward(
        normed_ffn, grad_second, up_part, down_part
    )
    second_out = second_f + ffn_result
    grad_mid_ffn, grad_ffn_gain = ffn_norm_back(grad_normed_ffn)
    grad_mid = grad_first.astype(jnp.float32) + grad_mid_ffn
    grad_mid_low = grad_mid.astype(jnp.bfloat16)
    grad_out = jnp.dot(attn_tok.T, grad_mid_low, preferred_element_type=jnp.float32)
    grad_attn_tok = jnp.dot(grad_mid_low, full_out.T, preferred_element_type=jnp.float32).astype(
        jnp.bfloat16
    )
    grad_attn = lax.all_to_all(
        grad_attn_tok.reshape(local_rows, NH, DH), "head", split_axis=1, concat_axis=0, tiled=True
    )
    grad_attn_f = grad_attn.astype(jnp.float32)
    grad_summed = (grad_attn_f / totals.T[:, :, None]).astype(jnp.bfloat16)
    grad_totals = (-jnp.sum(grad_attn_f * attended, axis=-1) / totals.T).T

    def pass_grads(grad_keys, grad_values):
        return (
            shifted(grad_keys.astype(jnp.bfloat16), "blk", 1).astype(grad_keys.dtype),
            shifted(grad_values.astype(jnp.bfloat16), "blk", 1).astype(grad_values.dtype),
        )

    def backward_step(cycle_step, carried):
        key_block, value_block, grad_keys, grad_values, grad_norms, grad_direct = carried
        pieces = backward_block(
            queries,
            query_norms,
            counts_for(cycle_step),
            key_block,
            value_block,
            grad_summed,
            grad_totals,
        )
        key_next, value_next = rotate(key_block, value_block)
        grad_keys, grad_values = pass_grads(grad_keys + pieces[2], grad_values + pieces[3])
        return (
            key_next,
            value_next,
            grad_keys,
            grad_values,
            grad_norms + pieces[0],
            grad_direct + pieces[1],
        )

    zero_rows = jnp.zeros((group_rows, local_heads, DH), jnp.float32)
    initial = (
        keys,
        values,
        zero_rows,
        zero_rows,
        jnp.zeros((local_heads, group_rows), jnp.float32),
        zero_rows,
    )
    carried = lax.fori_loop(0, cycle_count - 1, backward_step, initial)
    pieces = backward_block(
        queries,
        query_norms,
        counts_for(cycle_count - 1),
        carried[0],
        carried[1],
        grad_summed,
        grad_totals,
    )
    grad_keys, grad_values = pass_grads(carried[2] + pieces[2], carried[3] + pieces[3])
    grad_norms = carried[4] + pieces[0]
    grad_direct = carried[5] + pieces[1]
    grad_queries = grad_direct + norm_back(grad_norms.T)[0] + key_back(grad_keys)[0]
    grad_q_tok, grad_v_tok = (
        lax.all_to_all(
            grad_queries.astype(jnp.bfloat16), "head", split_axis=0, concat_axis=1, tiled=True
        ),
        lax.all_to_all(
            grad_values.astype(jnp.bfloat16), "head", split_axis=0, concat_axis=1, tiled=True
        ),
    )
    grad_q_tok = grad_q_tok.reshape(local_rows, model_width)
    grad_v_tok = grad_v_tok.reshape(local_rows, model_width)
    grad_normed = jnp.dot(grad_q_tok, full_qk.T, preferred_element_type=jnp.float32) + jnp.dot(
        grad_v_tok, full_value.T, preferred_element_type=jnp.float32
    )
    grad_qk = jnp.dot(normed.T, grad_q_tok, preferred_element_type=jnp.float32)
    grad_value = jnp.dot(normed.T, grad_v_tok, preferred_element_type=jnp.float32)
    grad_second_attn, grad_attn_gain = attn_norm_back(grad_normed)
    grad_second_total = grad_second.astype(jnp.float32) + grad_second_attn
    sum_qk, sum_value, sum_out, sum_attn_gain, sum_ffn_gain, sum_up, sum_down = (
        lax.psum_scatter(grad_qk, ("head", "blk"), scatter_dimension=0, tiled=True),
        lax.psum_scatter(grad_value, ("head", "blk"), scatter_dimension=0, tiled=True),
        lax.psum_scatter(grad_out, ("head", "blk"), scatter_dimension=0, tiled=True),
        lax.psum_scatter(grad_attn_gain, ("head", "blk"), scatter_dimension=0, tiled=True),
        lax.psum_scatter(grad_ffn_gain, ("head", "blk"), scatter_dimension=0, tiled=True),
        lax.psum_scatter(grad_up, ("head", "blk"), scatter_dimension=1, tiled=True),
        lax.psum_scatter(grad_down, ("head", "blk"), scatter_dimension=0, tiled=True),
    )
    return (
        first_out.astype(jnp.bfloat16),
        second_out.astype(jnp.bfloat16),
        grad_mid.astype(jnp.bfloat16),
        grad_second_total.astype(jnp.bfloat16),
        sum_qk,
        sum_value,
        sum_out,
        sum_attn_gain,
        sum_ffn_gain,
        sum_up,
        sum_down,
    )


BITS = ("y", "core", "z_hi", "z_lo", "x")
Y, CORE, Z_HI, Z_LO, X = 16, 8, 4, 2, 1
HEAD_AXES = ("core", "z_hi", "x")
LOG2E = 1.4426950408889634
HIGH_BITS = -2139062144
NT = (((1,), (1,)), ((), ()))
NN = (((1,), (0,)), ((), ()))
TN = (((0,), (0,)), ((), ()))
F32, BF16, I32 = jnp.float32, jnp.bfloat16, jnp.int32
VMEM = pl.BlockSpec(memory_space=pltpu.VMEM)
SMEM = pl.BlockSpec(memory_space=pltpu.SMEM)


def dot(left, right, dims=NN):
    return lax.dot_general(left, right, dims, preferred_element_type=F32)


def swap(value, mask):
    return lax.ppermute(value, BITS, [(i, i ^ mask) for i in range(32)])


def after(value, *others):
    return lax.optimization_barrier((value, *others))[0]


def shaped(*shape, dtype=BF16):
    return jax.ShapeDtypeStruct(shape, dtype)


def call(kernel, inputs, out_shape, name, flops, mib=40, specs=None):
    flat = jax.tree.leaves(out_shape)
    moved = sum(a.size * a.dtype.itemsize for a in [*inputs, *flat])
    return pl.pallas_call(
        kernel,
        in_specs=specs or [VMEM] * len(inputs),
        out_specs=jax.tree.map(lambda _: VMEM, out_shape),
        out_shape=out_shape,
        compiler_params=pltpu.CompilerParams(vmem_limit_bytes=mib * 2**20),
        cost_estimate=pl.CostEstimate(flops=flops, bytes_accessed=moved, transcendentals=0),
        name=name,
    )(*inputs)


def with_cores(near):
    return near + [swap(part, CORE) for part in near]


def gather_xy(value):
    return with_cores([value, swap(value, X), swap(value, Y), swap(value, X | Y)])


def gather_xz(value):
    over_z = swap(value, Z_HI)
    return with_cores([value, swap(value, X), over_z, swap(over_z, X)])


def scatter_xy(blocks):
    arrived = [swap(block, CORE) for block in blocks[4:]]
    sums = [
        (near.astype(F32) + far.astype(F32)).astype(BF16)
        for near, far in zip(blocks[1:4], arrived[1:], strict=True)
    ]
    sent = [swap(part, mask) for part, mask in zip(sums, (X, Y, X | Y), strict=True)]
    return [blocks[0], arrived[0], *sent]


def normalised(values):
    centred = values - jnp.mean(values, axis=-1, keepdims=True)
    rstd = lax.rsqrt(jnp.mean(centred * centred, axis=-1, keepdims=True) + 1e-05)
    return centred * rstd, rstd


def norm_back(scaled_grads, xhat, rstd):
    return rstd * (
        scaled_grads
        - jnp.mean(scaled_grads, axis=-1, keepdims=True)
        - xhat * jnp.mean(scaled_grads * xhat, axis=-1, keepdims=True)
    )


def to_row(column_ref, row_ref):
    for i in range(row_ref.shape[1] // 128):
        chunk = slice(i * 128, (i + 1) * 128)
        square = jnp.broadcast_to(column_ref[chunk, :], (128, 128))
        row_ref[:, chunk] = square.T[0:8, :]


def project_kernel(*refs):
    blocks, (gain_ref, weight_ref), outs = refs[:8], refs[8:10], refs[10:]
    normed_ref, q_ref, k_ref, v_ref, norm_ref, row_ref = outs
    weight = weight_ref[...]
    gain = gain_ref[0:1, :]
    for i, block in enumerate(blocks):
        rows = pl.ds(i * block.shape[0], block.shape[0])
        normed = (normalised(block[...].astype(F32))[0] * gain).astype(BF16)
        normed_ref[rows, :] = normed
        both = dot(normed, weight)
        queries = both[:, :DH].astype(BF16)
        q_ref[rows, :] = queries
        v_ref[rows, :] = both[:, DH:].astype(BF16)
        query_f = queries.astype(F32)
        squares = jnp.sum(query_f * query_f, axis=-1, keepdims=True)
        k_ref[rows, :] = (query_f * lax.rsqrt(squares / DH + 1e-06) * DH ** (-0.5)).astype(BF16)
        norm_ref[rows, :] = jnp.sqrt(squares + 1e-06) * LOG2E
    to_row(norm_ref, row_ref)


def pair_count(one, other, neighbour, diagonal):
    high = jnp.int32(HIGH_BITS)
    match = ((high - (one ^ other)) | (high - (one ^ neighbour))) & high
    counts = lax.population_count(match)
    if diagonal is not None:
        across = lax.broadcasted_iota(I32, counts.shape, 0) - lax.broadcasted_iota(
            I32, counts.shape, 1
        )
        counts = jnp.where(across == diagonal, 0, counts)
    return counts.astype(F32)


def forward_kernel(*refs, tile, own, first, last):
    q_ref, n_ref, qid_ref, k_ref, v_ref, kid_ref = refs[:6]
    acc_in = None if first else refs[6]
    head_ref = refs[6 + (not first)] if last else None
    acc_ref = refs[-2] if last else refs[-1]
    step = pl.program_id(0)

    @pl.when(step == 0)
    def _():
        acc_ref[...] = jnp.zeros_like(acc_ref) if first else acc_in[...]

    keys = k_ref[...]
    count = keys.shape[0]
    values = jnp.concatenate([v_ref[...], jnp.ones((count, DH), BF16)], axis=1)
    for i in range(q_ref.shape[0] // tile):
        rows = slice(i * tile, (i + 1) * tile)
        scores = dot(q_ref[rows, :], keys, NT)
        powers = jnp.exp2(scores * LOG2E - n_ref[rows, :])
        diagonal = step * count - i * tile if own else None
        counts = pair_count(qid_ref[rows, :], kid_ref[0:1, :], kid_ref[2:3, :], diagonal)
        acc_ref[rows, :] += dot((powers * counts).astype(BF16), values)

    if last:
        send_ref = refs[-1]
        rows = send_ref.shape[1]

        @pl.when(step == pl.num_programs(0) - 1)
        def _():
            for j in range(NH):
                block = acc_ref[j * rows : (j + 1) * rows, :]
                send_ref[head_ref[0] ^ j] = (block[:, :DH] / block[:, DH:]).astype(BF16)


def forward_call(queries, norms, ids, keys, values, part, acc, head=None, tk=768, tile=256):
    nq, nk = queries.shape[0], keys.shape[0]
    steps = nk // tk
    column = pl.BlockSpec((nq, 1), lambda j: (0, 0))
    full = pl.BlockSpec((nq, DH), lambda j: (0, 0))
    keyed = pl.BlockSpec((tk, DH), lambda j: (j, 0))
    wide = pl.BlockSpec((nq, 2 * DH), lambda j: (0, 0))
    listed = pl.BlockSpec((8, tk), lambda j: (0, part * steps + j))
    inputs = [queries, norms, ids[0], keys, values, ids[1]]
    specs = [full, column, column, keyed, keyed, listed]
    out_shape, out_specs = [shaped(nq, 2 * DH, dtype=F32)], [wide]
    if acc is not None:
        inputs.append(acc)
        specs.append(wide)
    if head is not None:
        inputs.append(head)
        specs.append(SMEM)
        out_shape.append(shaped(NH, nq // NH, DH))
        out_specs.append(pl.BlockSpec((NH, nq // NH, DH), lambda j: (0, 0, 0)))
    return pl.pallas_call(
        functools.partial(
            forward_kernel,
            tile=tile,
            own=part == 0,
            first=acc is None,
            last=head is not None,
        ),
        grid=(steps,),
        in_specs=specs,
        out_specs=out_specs,
        out_shape=out_shape,
        input_output_aliases={} if acc is None else {6: 0},
        compiler_params=pltpu.CompilerParams(vmem_limit_bytes=40 * 2**20),
        cost_estimate=pl.CostEstimate(
            flops=32 * nq * nk * DH, bytes_accessed=2 * nq * nk, transcendentals=nq * nk
        ),
        name="attention_forward",
    )(*inputs)


def backward_kernel(*refs, tile, own, first):
    q_ref, g_ref, n_ref, t_ref, qid_ref, k_ref, v_ref, kid_ref = refs[:8]
    dq_ref, dk_ref, dv_ref = refs[-3:]
    step = pl.program_id(0)

    @pl.when(step == 0)
    def _():
        dq_ref[...] = jnp.zeros_like(dq_ref) if first else refs[8][...]

    keys, values, key_ids = k_ref[...], v_ref[...], kid_ref[...]
    count = keys.shape[0]
    wide_keys = jnp.concatenate([keys, jnp.ones(keys.shape, BF16)], axis=1)
    grad_keys = jnp.zeros(keys.shape, F32)
    grad_values = jnp.zeros(keys.shape, F32)
    for i in range(q_ref.shape[0] // tile):
        rows = slice(i * tile, (i + 1) * tile)
        queries, grads = q_ref[rows, :], g_ref[rows, :]
        scores = dot(keys, queries, NT)
        powers = jnp.exp2(scores * LOG2E - n_ref[0:1, rows])
        diagonal = i * tile - step * count if own else None
        weights = powers * pair_count(key_ids, qid_ref[0:1, rows], qid_ref[1:2, rows], diagonal)
        grad_weights = dot(values, grads, NT)
        grad_scores = (weights * (grad_weights + t_ref[0:1, rows])).astype(BF16)
        grad_values = grad_values + dot(weights.astype(BF16), grads)
        grad_keys = grad_keys + dot(grad_scores, queries)
        dq_ref[rows, :] += dot(grad_scores, wide_keys, TN)
    dk_ref[...] = grad_keys.astype(BF16)
    dv_ref[...] = grad_values.astype(BF16)


def backward_call(queries, grads, norms, terms, ids, keys, values, part, acc, tk=768, tile=256):
    nq, nk = queries.shape[0], keys.shape[0]
    steps = nk // tk
    full = pl.BlockSpec((nq, DH), lambda j: (0, 0))
    row = pl.BlockSpec((8, nq), lambda j: (0, 0))
    keyed = pl.BlockSpec((tk, DH), lambda j: (j, 0))
    wide = pl.BlockSpec((nq, 2 * DH), lambda j: (0, 0))
    listed = pl.BlockSpec((tk, 1), lambda j: (part * steps + j, 0))
    more = [] if acc is None else [acc]
    return pl.pallas_call(
        functools.partial(backward_kernel, tile=tile, own=part == 0, first=acc is None),
        grid=(steps,),
        in_specs=[full, full, row, row, row, keyed, keyed, listed] + [wide] * len(more),
        out_specs=[wide, keyed, keyed],
        out_shape=[shaped(nq, 2 * DH, dtype=F32), shaped(nk, DH), shaped(nk, DH)],
        input_output_aliases={8: 0} if more else {},
        compiler_params=pltpu.CompilerParams(vmem_limit_bytes=40 * 2**20),
        cost_estimate=pl.CostEstimate(
            flops=40 * nq * nk * DH, bytes_accessed=2 * nq * nk, transcendentals=nq * nk
        ),
        name="attention_backward",
    )(queries, grads, norms, terms, ids[1], keys, values, ids[0], *more)


def out_kernel(attn_ref, half_ref, weight_ref, gain_ref, low_ref, out_ref, normed_ref):
    attn = jnp.concatenate([attn_ref[h] for h in range(NH)], axis=1)
    first_out = half_ref[...].astype(F32) + dot(attn, weight_ref[...])
    out_ref[...] = first_out
    low_ref[...] = first_out.astype(BF16)
    normed_ref[...] = (normalised(first_out)[0] * gain_ref[0:1, :]).astype(BF16)


def hidden_back_kernel(*refs):
    blocks, weight_ref, out_ref = refs[:8], refs[8], refs[9]
    down = weight_ref[:, weight_ref.shape[1] // 2 :]
    for i, block in enumerate(blocks):
        rows = pl.ds(i * block.shape[0], block.shape[0])
        out_ref[rows, :] = dot(block[...], down, NT)


def ffn_kernel(*refs):
    blocks, (back_ref, weight_ref), outs = refs[:8], refs[8:10], refs[10:]
    hidden_ref, grad_ref = outs[8:]
    up = weight_ref[:, : weight_ref.shape[1] // 2]
    slope = 0.7978845608028654
    for i, block in enumerate(blocks):
        rows = pl.ds(i * block.shape[0], block.shape[0])
        v = dot(block[...], up, NT)
        square = v * v
        t = jnp.tanh(slope * v * (1.0 + 0.044715 * square))
        half = 0.5 * (1.0 + t)
        hidden_ref[rows, :] = (v * half).astype(BF16)
        back = half + 0.5 * v * (1.0 - t * t) * slope * (1.0 + 3 * 0.044715 * square)
        grad = (back_ref[rows, :] * back).astype(BF16)
        grad_ref[rows, :] = grad
        outs[i][...] = dot(grad, up).astype(BF16)


def ffn_rest_kernel(*refs):
    blocks, grads = refs[:8], refs[8:16]
    hidden_ref, grad_ref, weight_ref = refs[16:19]
    outs, sum_ref = refs[19:27], refs[27]
    width = weight_ref.shape[1] // 2
    down = weight_ref[:, width:]
    for i in range(8):
        rows = pl.ds(i * blocks[i].shape[0], blocks[i].shape[0])
        outs[i][...] = dot(hidden_ref[rows, :], down).astype(BF16)
    inputs = jnp.concatenate([block[...] for block in blocks], axis=0)
    sum_ref[:, :width] = dot(grad_ref[...], inputs, TN).astype(BF16)
    cotangents = jnp.concatenate([block[...] for block in grads], axis=0)
    sum_ref[:, width:] = dot(hidden_ref[...], cotangents, TN).astype(BF16)


def mid_kernel(*refs):
    parts, rest, outs = refs[:5], refs[5:9], refs[9:]
    out_ref, first_ref, gain_ref, weight_ref = rest
    mid_ref, send_ref, gain_sum_ref = outs
    xhat, rstd = normalised(out_ref[...])
    grads = sum(part[...].astype(F32) for part in parts)
    gain_sum_ref[...] = jnp.broadcast_to(
        jnp.sum(grads * xhat, axis=0, keepdims=True), gain_sum_ref.shape
    )
    mid = first_ref[...].astype(F32) + norm_back(grads * gain_ref[0:1, :], xhat, rstd)
    mid = mid.astype(BF16)
    mid_ref[...] = mid
    grad_attn = dot(mid, weight_ref[...], NT).astype(BF16)
    for h in range(NH):
        send_ref[h] = grad_attn[:, h * DH : (h + 1) * DH]


def turn_kernel(arrived_ref, acc_ref, head_ref, grads_ref, row_ref, attn_ref, column_ref):
    rows = arrived_ref.shape[1]
    for j in range(NH):
        place = slice(j * rows, (j + 1) * rows)
        block = acc_ref[place, :]
        totals = block[:, DH:]
        attended = block[:, :DH] / totals
        attn_ref[place, :] = attended.astype(BF16)
        grad_attn = arrived_ref[head_ref[0] ^ j].astype(F32)
        grads_ref[place, :] = (grad_attn / totals).astype(BF16)
        column_ref[place, :] = (
            -jnp.sum(grad_attn * attended, axis=-1, keepdims=True) / totals[:, :1]
        )
    to_row(column_ref, row_ref)


def gather_grads_kernel(*refs):
    direct_ref, q_ref, n_ref, head_ref = refs[:4]
    key_refs, value_refs = refs[4:7], refs[7:10]
    send_ref, both_ref = refs[10:]
    rows = send_ref.shape[1]
    for j in range(NH):
        place = slice(j * rows, (j + 1) * rows)
        grad_keys = sum(ref[place, :].astype(F32) for ref in key_refs)
        grad_values = sum(ref[place, :].astype(F32) for ref in value_refs)
        queries = q_ref[place, :].astype(F32)
        inverse = lax.rsqrt(jnp.mean(queries * queries, axis=-1, keepdims=True) + 1e-06)
        mean_part = jnp.mean(grad_keys * queries, axis=-1, keepdims=True)
        grad_norms = -direct_ref[place, DH:]
        grad_queries = (
            direct_ref[place, :DH]
            + grad_norms * queries * (LOG2E / n_ref[place, :])
            + (inverse * DH ** (-0.5)) * (grad_keys - queries * (inverse * inverse * mean_part))
        )
        both = jnp.concatenate([grad_queries.astype(BF16), grad_values.astype(BF16)], axis=1)
        both_ref[place, :] = both
        send_ref[head_ref[0] ^ j] = both


def last_kernel(arrived_ref, half_ref, grad_ref, gain_ref, weight_ref, out_ref):
    width = half_ref.shape[1]
    grad_q = jnp.concatenate([arrived_ref[h][:, :DH] for h in range(NH)], axis=1)
    grad_v = jnp.concatenate([arrived_ref[h][:, DH:] for h in range(NH)], axis=1)
    grads = dot(grad_q, weight_ref[:, :width], NT) + dot(grad_v, weight_ref[:, width:], NT)
    xhat, rstd = normalised(half_ref[...].astype(F32))
    out_ref[...] = (
        grad_ref[...].astype(F32) + norm_back(grads * gain_ref[0:1, :], xhat, rstd)
    ).astype(BF16)


def cube_plan(
    first_half,
    second_half,
    grad_first,
    grad_second,
    qk_weight,
    value_weight,
    out_weight,
    attn_gain,
    ffn_gain,
    up_weight,
    down_weight,
    stretch_ids,
):
    y, core, z_hi, z_lo, x = (lax.axis_index(name) for name in BITS)
    head = (core * 4 + z_hi * 2 + x).astype(I32).reshape(1)
    rows, width = first_half.shape
    wide_rows = rows * 8
    own_rows = qk_weight.shape[0]
    rounds, tokens = stretch_ids.shape
    nchunk = tokens // STRETCH
    row_block = shaped(rows, width)

    gains = jnp.concatenate([attn_gain, ffn_gain, jnp.zeros((128 - 2 * own_rows,), BF16)])
    gains = jnp.broadcast_to(gains.astype(F32), (32, 1, 128))
    gains = lax.all_to_all(gains, BITS, 0, 0, tiled=True).reshape(32, 128)
    attn_gain_row = jnp.broadcast_to(gains[:, :own_rows].reshape(1, width), (8, width))
    ffn_gain_row = jnp.broadcast_to(
        gains[:, own_rows : 2 * own_rows].reshape(1, width), (8, width)
    )
    columns = jnp.stack([qk_weight, value_weight]).reshape(2, own_rows, NH, DH)
    columns = columns.transpose(2, 1, 0, 3).reshape(NH, own_rows, 2 * DH)
    heads_of = [((d >> 3) & 1) * 4 + ((d >> 2) & 1) * 2 + (d & 1) for d in range(32)]
    columns = jnp.stack([columns[h] for h in heads_of])
    columns = lax.all_to_all(columns, BITS, 0, 0, tiled=True).reshape(width, 2 * DH)
    blocks = gather_xz(second_half)

    out_full = lax.all_gather(out_weight, BITS, axis=0, tiled=True)
    ffn_weights = lax.all_gather(
        jnp.concatenate([up_weight.T, down_weight], axis=1), ("z_hi", "z_lo"), axis=0, tiled=True
    )
    qv_full = lax.all_gather(
        jnp.concatenate([qk_weight, value_weight], axis=1), BITS, axis=0, tiled=True
    )

    ids = stretch_ids.reshape(rounds, 2, 2, 2, 2, 2, rows)
    for axis, bit in enumerate((y, core, z_hi, z_lo, x), 1):
        ids = jnp.where(bit == 1, jnp.flip(ids, axis), ids)
    ids = ids.transpose(0, 4, 1, 2, 3, 5, 6).reshape(rounds, tokens)

    def packed(numbers):
        return sum(numbers[r] << (8 * r) for r in range(rounds))

    ids_row = packed(ids)
    ids_rows = jnp.concatenate(
        [
            ids_row[None],
            packed((ids + nchunk - 1) % nchunk)[None],
            packed((ids + 1) % nchunk)[None],
            jnp.zeros((5, tokens), I32),
        ]
    )
    ids_both = (ids_row[:, None], ids_rows)

    normed, queries, keys, values, norms, norm_row = call(
        project_kernel,
        [*blocks, attn_gain_row, columns],
        [
            shaped(wide_rows, width),
            *[shaped(wide_rows, DH)] * 3,
            shaped(wide_rows, 1, dtype=F32),
            shaped(8, wide_rows, dtype=F32),
        ],
        "project",
        8 * wide_rows * width * DH,
    )
    key_y, value_z = swap(keys, Y), swap(values, Z_LO)
    key_z, value_y = swap(keys, Z_LO), swap(values, Y)
    key_yz, value_yz = swap(key_y, Z_LO), swap(value_z, Y)
    key_parts = [keys, key_y, key_z, key_yz]
    value_parts = [values, value_y, value_z, value_yz]
    acc = None
    for part in range(4):
        acc, *attn_send = forward_call(
            queries,
            norms,
            ids_both,
            key_parts[part],
            value_parts[part],
            part,
            acc,
            head if part == 3 else None,
        )
    attn_tok = lax.all_to_all(attn_send[0], HEAD_AXES, 0, 0, tiled=True)

    y_first, first_out, normed_ffn = call(
        out_kernel,
        [attn_tok, first_half, out_full, ffn_gain_row],
        [row_block, shaped(rows, width, dtype=F32), row_block],
        "project_out",
        2 * rows * width * width,
    )
    units = ffn_weights.shape[0]
    ffn_flops = 2 * wide_rows * width * units
    cotangents = gather_xy(grad_second)
    hidden_back = call(
        hidden_back_kernel,
        [*cotangents, ffn_weights],
        shaped(wide_rows, units, dtype=F32),
        "hidden_back",
        ffn_flops,
    )
    ffn_in = gather_xy(normed_ffn)
    *grad_blocks, hidden, grad_pre = call(
        ffn_kernel,
        [*ffn_in, hidden_back, ffn_weights],
        [row_block] * 8 + [shaped(wide_rows, units)] * 2,
        "feed_forward",
        3 * ffn_flops,
    )
    grad_parts = scatter_xy(grad_blocks)
    *ffn_blocks, grad_ffn = call(
        ffn_rest_kernel,
        [*ffn_in, *cotangents, hidden, grad_pre, ffn_weights],
        [row_block] * 8 + [shaped(units, 2 * width)],
        "feed_forward_rest",
        4 * ffn_flops,
    )
    grad_mid, grad_attn, gain_sum = call(
        mid_kernel,
        [*grad_parts, first_out, grad_first, ffn_gain_row, out_full],
        [row_block, shaped(NH, rows, DH), shaped(8, width, dtype=F32)],
        "mid",
        2 * rows * width * width,
    )

    grad_attn = lax.all_to_all(grad_attn, HEAD_AXES, 0, 0, tiled=True)
    grads, term_row, attn, _ = call(
        turn_kernel,
        [grad_attn, acc, head],
        [
            shaped(wide_rows, DH),
            shaped(8, wide_rows, dtype=F32),
            shaped(wide_rows, DH),
            shaped(wide_rows, 1, dtype=F32),
        ],
        "turn",
        wide_rows * DH,
        specs=[VMEM, VMEM, SMEM],
    )

    def backward(part, acc):
        return backward_call(
            queries,
            grads,
            norm_row,
            term_row,
            ids_both,
            key_parts[part],
            value_parts[part],
            part,
            acc,
        )

    direct, far_key, far_value = backward(3, None)
    far_key, far_value = swap(far_key, Y), swap(far_value, Z_LO)
    direct, z_key, z_value = backward(2, direct)
    z_value = swap(z_value, Z_LO)
    direct = after(direct, far_key, far_value)
    direct, y_key, y_value = backward(1, direct)
    y_key = swap(y_key, Y)
    z_key = swap((z_key.astype(F32) + far_key.astype(F32)).astype(BF16), Z_LO)
    y_value = swap((y_value.astype(F32) + far_value.astype(F32)).astype(BF16), Y)
    direct, grad_keys, grad_values = backward(0, direct)

    ffn_blocks = [after(block, grad_attn) for block in ffn_blocks]
    second_out = second_half.astype(F32) + sum(
        part.astype(F32) for part in scatter_xy(ffn_blocks)
    )
    grad_ffn = lax.psum_scatter(
        grad_ffn, ("z_hi", "z_lo"), scatter_dimension=0, tiled=True
    ).astype(F32)
    gain_sum = after(gain_sum, grad_attn)[0].reshape(32, 1, own_rows)
    gain_sum = jnp.pad(gain_sum, ((0, 0), (0, 0), (0, 128 - own_rows)))
    gain_sum = lax.all_to_all(gain_sum, BITS, 0, 0, tiled=True)
    grad_ffn_gain = jnp.sum(gain_sum, axis=(0, 1))[:own_rows]

    def halve(value, axis, bit, mask):
        keep = lax.dynamic_index_in_dim(value, bit, axis, keepdims=False)
        send = lax.dynamic_index_in_dim(value, 1 - bit, axis, keepdims=False)
        return keep + swap(send.astype(BF16), mask).astype(F32)

    grad_mid_all = jnp.concatenate(gather_xz(after(grad_mid, grad_attn)), axis=0)
    grad_out = dot(attn, grad_mid_all, TN).reshape(2, 2, DH // 4, width)
    grad_out = halve(halve(grad_out, 1, y, Y), 0, z_lo, Z_LO)
    owners = []
    for d in range(32):
        dy, dc, dh, dl, dx = ((d >> s) & 1 for s in (4, 3, 2, 1, 0))
        owners.append((d, dc * 16 + dh * 8 + dx * 4 + dl * 2 + dy))
    grad_out = lax.ppermute(grad_out.astype(BF16), BITS, owners).astype(F32)

    send, grad_both = call(
        gather_grads_kernel,
        [direct, queries, norms, head, grad_keys, y_key, z_key, grad_values, y_value, z_value],
        [shaped(NH, rows, 2 * DH), shaped(wide_rows, 2 * DH)],
        "gather_grads",
        wide_rows * DH,
        specs=[VMEM] * 3 + [SMEM] + [VMEM] * 6,
    )
    arrived = lax.all_to_all(send, HEAD_AXES, 0, 0, tiled=True)
    grad_second_half = call(
        last_kernel,
        [arrived, second_half, grad_second, attn_gain_row, qv_full],
        row_block,
        "last",
        4 * rows * width * width,
    )

    grad_rows = dot(normed, grad_both, TN).reshape(2, 2, 2, 2, 2, own_rows, 2 * DH)
    grad_rows = halve(halve(grad_rows, 0, y, Y), 2, z_lo, Z_LO)
    grad_rows = grad_rows.reshape(8, own_rows, 2 * DH).astype(BF16)
    grad_rows = lax.all_to_all(grad_rows, HEAD_AXES, 0, 0, tiled=True).astype(F32)
    grad_qk = grad_rows[:, :, :DH].transpose(1, 0, 2).reshape(own_rows, width)
    grad_value = grad_rows[:, :, DH:].transpose(1, 0, 2).reshape(own_rows, width)
    grad_attn_gain = jnp.sum(
        qk_weight.astype(F32) * grad_qk + value_weight.astype(F32) * grad_value, axis=-1
    ) / attn_gain.astype(F32)

    return (
        y_first,
        second_out.astype(BF16),
        grad_mid,
        grad_second_half,
        grad_qk,
        grad_value,
        grad_out,
        grad_attn_gain,
        grad_ffn_gain,
        grad_ffn[:, :width].T,
        grad_ffn[:, width:],
    )


def solution(mesh):
    if dict(mesh.shape) == {"head": 4, "blk": 8}:
        plan, axes = cube_plan, BITS
        mesh = jax.sharding.Mesh(mesh.devices.reshape((2,) * 5), BITS)
    else:
        plan, axes = ring_plan, ("head", "blk")
    by_row, by_column, vector = P(axes, None), P(None, axes), P(axes)
    return jax.shard_map(
        plan,
        mesh=mesh,
        in_specs=(by_row,) * 7 + (vector, vector, by_column, by_row, P()),
        out_specs=(by_row,) * 7 + (vector, vector, by_column, by_row),
        check_vma=False,
    )
```

```python
import functools

import jax
import jax.numpy as jnp
from jax import lax
from jax.experimental import pallas as pl
from jax.experimental.pallas import tpu as pltpu
from jax.sharding import PartitionSpec as P

NH = 8
DH = 128
STRETCH = 64


def shifted(value, axis, by):
    devices = lax.axis_size(axis)
    return lax.ppermute(value, axis, [(i, (i + by) % devices) for i in range(devices)])


def layer_norm(values, gains):
    average = jnp.mean(values, axis=-1, keepdims=True)
    centred = values - average
    variance = jnp.mean(centred * centred, axis=-1, keepdims=True)
    return centred * lax.rsqrt(variance + 1e-05) * gains


def key_norm(queries):
    return (
        queries
        * lax.rsqrt(jnp.mean(queries * queries, axis=-1, keepdims=True) + 1e-06)
        * queries.shape[-1] ** (-0.5)
    )


def row_norm(queries):
    return jnp.sqrt(jnp.sum(queries * queries, axis=-1) + 1e-06)


def group_ids(stretch_ids, heads_count, cycle_count, local_rows, cycle_index):
    shaped = stretch_ids.reshape(stretch_ids.shape[0], heads_count, cycle_count, local_rows)
    picked = lax.dynamic_slice_in_dim(shaped, cycle_index, 1, 2)
    places = (
        jnp.arange(heads_count, dtype=jnp.int32)[:, None] * cycle_count + cycle_index
    ) * local_rows
    places = places + jnp.arange(local_rows, dtype=jnp.int32)[None, :]
    return (picked.reshape(stretch_ids.shape[0], heads_count * local_rows), places.reshape(-1))


def pair_counts(query_ids, query_places, key_ids, key_places, nchunk):
    previous = (query_ids + nchunk - 1) % nchunk
    same_stretch = key_ids[:, None, :] == query_ids[:, :, None]
    before = key_ids[:, None, :] == previous[:, :, None]
    counts = jnp.sum((same_stretch | before).astype(jnp.float32), axis=0)
    return counts * (query_places[:, None] != key_places[None, :]).astype(jnp.float32)


def forward_block(queries, query_norms, counts, key_block, value_block):
    scores = jnp.einsum("qhd,khd->hqk", queries, key_block, preferred_element_type=jnp.float32)
    weights = counts[None] * jnp.exp(scores - query_norms.T[:, :, None])
    summed = jnp.einsum(
        "hqk,khd->qhd",
        weights.astype(jnp.bfloat16),
        value_block,
        preferred_element_type=jnp.float32,
    )
    return (jnp.sum(weights, axis=-1), summed)


def backward_block(queries, query_norms, counts, key_block, value_block, grad_summed, grad_totals):
    scores = jnp.einsum("qhd,khd->hqk", queries, key_block, preferred_element_type=jnp.float32)
    weights = counts[None] * jnp.exp(scores - query_norms.T[:, :, None])
    grad_weights = jnp.einsum(
        "qhd,khd->hqk", grad_summed, value_block, preferred_element_type=jnp.float32
    )
    grad_scores_f = weights * (grad_weights + grad_totals[:, :, None])
    grad_scores = grad_scores_f.astype(jnp.bfloat16)
    grad_norms = -jnp.sum(grad_scores_f, axis=-1)
    grad_values = jnp.einsum(
        "hqk,qhd->khd",
        weights.astype(jnp.bfloat16),
        grad_summed,
        preferred_element_type=jnp.float32,
    )
    grad_direct = jnp.einsum(
        "hqk,khd->qhd", grad_scores, key_block, preferred_element_type=jnp.float32
    )
    grad_keys = jnp.einsum("hqk,qhd->khd", grad_scores, queries, preferred_element_type=jnp.float32)
    return (grad_norms, grad_direct, grad_keys, grad_values)


def feed_forward(normed_ffn, grad_output, up_part, down_part):
    pre_act = jnp.dot(normed_ffn, up_part, preferred_element_type=jnp.float32)
    hidden_f, gelu_back = jax.vjp(jax.nn.gelu, pre_act)
    hidden = hidden_f.astype(jnp.bfloat16)
    ffn_result = jnp.dot(hidden, down_part, preferred_element_type=jnp.float32)
    grad_hidden = jnp.dot(grad_output, down_part.T, preferred_element_type=jnp.float32)
    grad_pre = gelu_back(grad_hidden)[0].astype(jnp.bfloat16)
    grad_normed = jnp.dot(grad_pre, up_part.T, preferred_element_type=jnp.float32)
    grad_up = jnp.dot(normed_ffn.T, grad_pre, preferred_element_type=jnp.float32)
    grad_down = jnp.dot(hidden.T, grad_output, preferred_element_type=jnp.float32)
    return (ffn_result, grad_normed, grad_up, grad_down)


def ring_plan(
    first_half,
    second_half,
    grad_first,
    grad_second,
    qk_weight,
    value_weight,
    out_weight,
    attn_gain,
    ffn_gain,
    up_weight,
    down_weight,
    stretch_ids,
):
    heads_count = lax.axis_size("head")
    cycle_count = lax.axis_size("blk")
    cycle_index = lax.axis_index("blk")
    local_rows = first_half.shape[0]
    model_width = first_half.shape[1]
    group_rows = local_rows * heads_count
    local_heads = NH // heads_count
    nchunk = stretch_ids.shape[1] // STRETCH
    full_qk, full_value, full_out, full_attn_gain, full_ffn_gain, up_part, down_part = (
        lax.all_gather(qk_weight, ("head", "blk"), axis=0, tiled=True),
        lax.all_gather(value_weight, ("head", "blk"), axis=0, tiled=True),
        lax.all_gather(out_weight, ("head", "blk"), axis=0, tiled=True),
        lax.all_gather(attn_gain, ("head", "blk"), axis=0, tiled=True),
        lax.all_gather(ffn_gain, ("head", "blk"), axis=0, tiled=True),
        lax.all_gather(up_weight, ("head", "blk"), axis=1, tiled=True),
        lax.all_gather(down_weight, ("head", "blk"), axis=0, tiled=True),
    )
    second_f = second_half.astype(jnp.float32)
    normed_f, attn_norm_back = jax.vjp(layer_norm, second_f, full_attn_gain.astype(jnp.float32))
    normed = normed_f.astype(jnp.bfloat16)
    query_tok = jnp.dot(normed, full_qk, preferred_element_type=jnp.float32).astype(jnp.bfloat16)
    value_tok = jnp.dot(normed, full_value, preferred_element_type=jnp.float32).astype(jnp.bfloat16)
    query_heads = query_tok.reshape(local_rows, NH, DH)
    value_heads = value_tok.reshape(local_rows, NH, DH)
    queries, values = (
        lax.all_to_all(query_heads, "head", split_axis=1, concat_axis=0, tiled=True),
        lax.all_to_all(value_heads, "head", split_axis=1, concat_axis=0, tiled=True),
    )
    query_f = queries.astype(jnp.float32)
    key_f, key_back = jax.vjp(key_norm, query_f)
    keys = key_f.astype(jnp.bfloat16)
    query_norms, norm_back = jax.vjp(row_norm, query_f)
    query_ids, query_places = group_ids(
        stretch_ids, heads_count, cycle_count, local_rows, cycle_index
    )

    def counts_for(cycle_step):
        source_index = (cycle_index - cycle_step + cycle_count) % cycle_count
        key_ids, key_places = group_ids(
            stretch_ids, heads_count, cycle_count, local_rows, source_index
        )
        return pair_counts(query_ids, query_places, key_ids, key_places, nchunk)

    def rotate(key_block, value_block):
        return shifted((key_block, value_block), "blk", 1)

    def forward_step(cycle_step, carried):
        key_block, value_block, totals, summed = carried
        part_totals, part_summed = forward_block(
            queries, query_norms, counts_for(cycle_step), key_block, value_block
        )
        key_next, value_next = rotate(key_block, value_block)
        return (key_next, value_next, totals + part_totals, summed + part_summed)

    initial = (
        keys,
        values,
        jnp.zeros((local_heads, group_rows), jnp.float32),
        jnp.zeros((group_rows, local_heads, DH), jnp.float32),
    )
    key_block, value_block, totals, summed = lax.fori_loop(
        0, cycle_count - 1, forward_step, initial
    )
    part_totals, part_summed = forward_block(
        queries, query_norms, counts_for(cycle_count - 1), key_block, value_block
    )
    totals = totals + part_totals
    summed = summed + part_summed
    attended = summed / totals.T[:, :, None]
    attn_tok = lax.all_to_all(
        attended.astype(jnp.bfloat16), "head", split_axis=0, concat_axis=1, tiled=True
    ).reshape(local_rows, model_width)
    first_out = first_half.astype(jnp.float32) + jnp.dot(
        attn_tok, full_out, preferred_element_type=jnp.float32
    )
    normed_ffn_f, ffn_norm_back = jax.vjp(layer_norm, first_out, full_ffn_gain.astype(jnp.float32))
    normed_ffn = normed_ffn_f.astype(jnp.bfloat16)
    ffn_result, grad_normed_ffn, grad_up, grad_down = feed_forward(
        normed_ffn, grad_second, up_part, down_part
    )
    second_out = second_f + ffn_result
    grad_mid_ffn, grad_ffn_gain = ffn_norm_back(grad_normed_ffn)
    grad_mid = grad_first.astype(jnp.float32) + grad_mid_ffn
    grad_mid_low = grad_mid.astype(jnp.bfloat16)
    grad_out = jnp.dot(attn_tok.T, grad_mid_low, preferred_element_type=jnp.float32)
    grad_attn_tok = jnp.dot(grad_mid_low, full_out.T, preferred_element_type=jnp.float32).astype(
        jnp.bfloat16
    )
    grad_attn = lax.all_to_all(
        grad_attn_tok.reshape(local_rows, NH, DH), "head", split_axis=1, concat_axis=0, tiled=True
    )
    grad_attn_f = grad_attn.astype(jnp.float32)
    grad_summed = (grad_attn_f / totals.T[:, :, None]).astype(jnp.bfloat16)
    grad_totals = (-jnp.sum(grad_attn_f * attended, axis=-1) / totals.T).T

    def pass_grads(grad_keys, grad_values):
        return (
            shifted(grad_keys.astype(jnp.bfloat16), "blk", 1).astype(grad_keys.dtype),
            shifted(grad_values.astype(jnp.bfloat16), "blk", 1).astype(grad_values.dtype),
        )

    def backward_step(cycle_step, carried):
        key_block, value_block, grad_keys, grad_values, grad_norms, grad_direct = carried
        pieces = backward_block(
            queries,
            query_norms,
            counts_for(cycle_step),
            key_block,
            value_block,
            grad_summed,
            grad_totals,
        )
        key_next, value_next = rotate(key_block, value_block)
        grad_keys, grad_values = pass_grads(grad_keys + pieces[2], grad_values + pieces[3])
        return (
            key_next,
            value_next,
            grad_keys,
            grad_values,
            grad_norms + pieces[0],
            grad_direct + pieces[1],
        )

    zero_rows = jnp.zeros((group_rows, local_heads, DH), jnp.float32)
    initial = (
        keys,
        values,
        zero_rows,
        zero_rows,
        jnp.zeros((local_heads, group_rows), jnp.float32),
        zero_rows,
    )
    carried = lax.fori_loop(0, cycle_count - 1, backward_step, initial)
    pieces = backward_block(
        queries,
        query_norms,
        counts_for(cycle_count - 1),
        carried[0],
        carried[1],
        grad_summed,
        grad_totals,
    )
    grad_keys, grad_values = pass_grads(carried[2] + pieces[2], carried[3] + pieces[3])
    grad_norms = carried[4] + pieces[0]
    grad_direct = carried[5] + pieces[1]
    grad_queries = grad_direct + norm_back(grad_norms.T)[0] + key_back(grad_keys)[0]
    grad_q_tok, grad_v_tok = (
        lax.all_to_all(
            grad_queries.astype(jnp.bfloat16), "head", split_axis=0, concat_axis=1, tiled=True
        ),
        lax.all_to_all(
            grad_values.astype(jnp.bfloat16), "head", split_axis=0, concat_axis=1, tiled=True
        ),
    )
    grad_q_tok = grad_q_tok.reshape(local_rows, model_width)
    grad_v_tok = grad_v_tok.reshape(local_rows, model_width)
    grad_normed = jnp.dot(grad_q_tok, full_qk.T, preferred_element_type=jnp.float32) + jnp.dot(
        grad_v_tok, full_value.T, preferred_element_type=jnp.float32
    )
    grad_qk = jnp.dot(normed.T, grad_q_tok, preferred_element_type=jnp.float32)
    grad_value = jnp.dot(normed.T, grad_v_tok, preferred_element_type=jnp.float32)
    grad_second_attn, grad_attn_gain = attn_norm_back(grad_normed)
    grad_second_total = grad_second.astype(jnp.float32) + grad_second_attn
    sum_qk, sum_value, sum_out, sum_attn_gain, sum_ffn_gain, sum_up, sum_down = (
        lax.psum_scatter(grad_qk, ("head", "blk"), scatter_dimension=0, tiled=True),
        lax.psum_scatter(grad_value, ("head", "blk"), scatter_dimension=0, tiled=True),
        lax.psum_scatter(grad_out, ("head", "blk"), scatter_dimension=0, tiled=True),
        lax.psum_scatter(grad_attn_gain, ("head", "blk"), scatter_dimension=0, tiled=True),
        lax.psum_scatter(grad_ffn_gain, ("head", "blk"), scatter_dimension=0, tiled=True),
        lax.psum_scatter(grad_up, ("head", "blk"), scatter_dimension=1, tiled=True),
        lax.psum_scatter(grad_down, ("head", "blk"), scatter_dimension=0, tiled=True),
    )
    return (
        first_out.astype(jnp.bfloat16),
        second_out.astype(jnp.bfloat16),
        grad_mid.astype(jnp.bfloat16),
        grad_second_total.astype(jnp.bfloat16),
        sum_qk,
        sum_value,
        sum_out,
        sum_attn_gain,
        sum_ffn_gain,
        sum_up,
        sum_down,
    )


BITS = ("y", "core", "z_hi", "z_lo", "x")
Y, CORE, Z_HI, Z_LO, X = 16, 8, 4, 2, 1
HEAD_AXES = ("z_hi", "z_lo", "x")
PARTS = (0, CORE, Y, Y | CORE)
LOG2E = 1.4426950408889634
HIGH_BITS = -2139062144
NT = (((1,), (1,)), ((), ()))
NN = (((1,), (0,)), ((), ()))
TN = (((0,), (0,)), ((), ()))
F32, BF16, I32 = jnp.float32, jnp.bfloat16, jnp.int32
LONG = pl.CostEstimate(flops=10**11, bytes_accessed=1, transcendentals=0)
SMEM = pl.BlockSpec(memory_space=pltpu.SMEM)


def dot(left, right, dims=NN):
    return lax.dot_general(left, right, dims, preferred_element_type=F32)


def swap(value, mask):
    return lax.ppermute(value, BITS, [(i, i ^ mask) for i in range(32)])


def after(value, *others):
    return lax.optimization_barrier((value, *others))[0]


def shaped(*shape, dtype=BF16):
    return jax.ShapeDtypeStruct(shape, dtype)


class Far:
    def __init__(self, value):
        self.value = value


def call(kernel, inputs, out_shape, name, far_out=(), mib=56, scalars=(), scratch=(), cost=LONG):
    far_in = [i for i, a in enumerate(inputs) if isinstance(a, Far)]
    arrays = [a.value if isinstance(a, Far) else a for a in inputs]
    first_in, first_out = len(scalars), len(scalars) + len(arrays)
    first_scratch = first_out + len(out_shape)
    staged = [arrays[i] for i in far_in] + [out_shape[i] for i in far_out]

    def body(*refs):
        refs, sems = list(refs[:-1]), refs[-1]
        own = refs[first_scratch : first_scratch + len(scratch)]
        stages = refs[first_scratch + len(scratch) :]
        copies = []
        for k, i in enumerate(far_in):
            copies.append(pltpu.make_async_copy(refs[first_in + i], stages[k], sems.at[k]))
            refs[first_in + i] = stages[k]
        for copy in copies:
            copy.start()
        for copy in copies:
            copy.wait()
        copies = []
        for k, i in enumerate(far_out, len(far_in)):
            copies.append(pltpu.make_async_copy(stages[k], refs[first_out + i], sems.at[k]))
            refs[first_out + i] = stages[k]
        kernel(*refs[:first_scratch], *own)
        for copy in copies:
            copy.start()
        for copy in copies:
            copy.wait()

    near, far = pl.BlockSpec(memory_space=pltpu.VMEM), pl.BlockSpec(memory_space=pl.ANY)
    return pl.pallas_call(
        body,
        in_specs=[SMEM] * len(scalars) + [far if i in far_in else near for i in range(len(arrays))],
        out_specs=[far if i in far_out else near for i in range(len(out_shape))],
        out_shape=out_shape,
        scratch_shapes=[
            *scratch,
            *(pltpu.VMEM(a.shape, a.dtype) for a in staged),
            pltpu.SemaphoreType.DMA((max(len(staged), 1),)),
        ],
        compiler_params=pltpu.CompilerParams(vmem_limit_bytes=mib * 2**20),
        cost_estimate=cost,
        name=name,
    )(*scalars, *arrays)


def with_cores(near):
    return near + [swap(part, CORE) for part in near]


def near_xy(value):
    return [value, swap(value, X), swap(value, Y), swap(value, X | Y)]


def gather_xy(value):
    return with_cores(near_xy(value))


def gather_zx(value):
    low, high = swap(value, Z_LO), swap(value, Z_HI)
    line = [value, low, high, swap(high, Z_LO)]
    return [block for part in line for block in (part, swap(part, X))]


def scatter_xy(blocks):
    arrived = [swap(block, CORE) for block in blocks[4:]]
    sums = [
        (near.astype(F32) + far.astype(F32)).astype(BF16)
        for near, far in zip(blocks[1:4], arrived[1:], strict=True)
    ]
    sent = [swap(part, mask) for part, mask in zip(sums, (X, Y, X | Y), strict=True)]
    return [blocks[0], arrived[0], *sent]


def scatter_by_x(blocks):
    arrived = [swap(block, CORE) for block in blocks[4:]]
    own, one, two, both = (
        near.astype(F32) + far.astype(F32) for near, far in zip(blocks[:4], arrived, strict=True)
    )
    own = own + swap(one.astype(BF16), X).astype(F32)
    two = two + swap(both.astype(BF16), X).astype(F32)
    return own + swap(two.astype(BF16), Y).astype(F32)


def shares(value):
    over_y = swap(value, Y)
    return [value, swap(value, CORE), over_y, swap(over_y, CORE)]


def sum_shares(blocks):
    return [blocks[0]] + [swap(b, mask) for b, mask in zip(blocks[1:], PARTS[1:], strict=True)]


def normalised(values):
    centred = values - jnp.mean(values, axis=-1, keepdims=True)
    rstd = lax.rsqrt(jnp.mean(centred * centred, axis=-1, keepdims=True) + 1e-05)
    return centred * rstd, rstd


def norm_back(scaled_grads, xhat, rstd):
    return rstd * (
        scaled_grads
        - jnp.mean(scaled_grads, axis=-1, keepdims=True)
        - xhat * jnp.mean(scaled_grads * xhat, axis=-1, keepdims=True)
    )


def to_row(column_ref, row_ref):
    for i in range(row_ref.shape[1] // 128):
        chunk = slice(i * 128, (i + 1) * 128)
        square = jnp.broadcast_to(column_ref[chunk, :], (128, 128))
        row_ref[:, chunk] = square.T[0:8, :]


def pack_kernel(*refs):
    qk_ref, value_ref, out_ref, up_ref, down_ref, gain_ref, columns_ref, z_ref, qv_ref = refs
    rows, width = qk_ref.shape
    units = down_ref.shape[0]
    for h in range(NH):
        lanes = slice(h * DH, (h + 1) * DH)
        columns_ref[h, :, :DH] = qk_ref[:, lanes]
        columns_ref[h, :, DH : 2 * DH] = value_ref[:, lanes]
        columns_ref[h, :, 2 * DH :] = gain_ref[...]
    z_ref[:units, :width] = up_ref[...].astype(F32).T.astype(BF16)
    z_ref[:units, width:] = down_ref[...]
    z_ref[units:, :width] = out_ref[: rows // 2, :]
    z_ref[units:, width:] = out_ref[rows // 2 :, :]
    qv_ref[:, :width] = qk_ref[...]
    qv_ref[:, width:] = value_ref[...]


def column_kernel(row_ref, column_ref):
    for i in range(row_ref.shape[1] // 128):
        chunk = slice(i * 128, (i + 1) * 128)
        square = jnp.broadcast_to(row_ref[0:1, chunk], (128, 128))
        column_ref[chunk, :] = square.T[:, 0:1]


def project_kernel(place_ref, *refs):
    blocks, parts, outs = refs[:8], refs[8:12], refs[12:18]
    weight_ref = refs[18]
    normed_ref, q_ref, kv_ref, norm_ref, row_ref, gain_ref = outs
    me = place_ref[0]
    rows = parts[0].shape[1]
    for part, mask in zip(parts, PARTS, strict=True):
        for s in range(NH):
            owner = ((me ^ mask) & (Y | CORE)) | s
            weight_ref[pl.ds(pl.multiple_of(owner * rows, rows), rows), :] = part[s]
    for i in range(weight_ref.shape[0] // 128):
        chunk = slice(i * 128, (i + 1) * 128)
        gain_ref[:, chunk] = weight_ref[chunk, 2 * DH :].astype(F32).T[0:8, :]
    weight = weight_ref[:, : 2 * DH]
    gain = gain_ref[0:1, :]
    for i, block in enumerate(blocks):
        rows = pl.ds(i * block.shape[0], block.shape[0])
        normed = (normalised(block[...].astype(F32))[0] * gain).astype(BF16)
        normed_ref[rows, :] = normed
        both = dot(normed, weight)
        queries = both[:, :DH].astype(BF16)
        q_ref[rows, :] = queries
        query_f = queries.astype(F32)
        squares = jnp.sum(query_f * query_f, axis=-1, keepdims=True)
        keys = (query_f * lax.rsqrt(squares / DH + 1e-06) * DH ** (-0.5)).astype(BF16)
        kv_ref[rows, :] = jnp.concatenate([keys, both[:, DH:].astype(BF16)], axis=1)
        norm_ref[rows, :] = jnp.sqrt(squares + 1e-06) * LOG2E
    to_row(norm_ref, row_ref)


def pair_count(one, other, neighbour, diagonal):
    high = jnp.int32(HIGH_BITS)
    match = ((high - (one ^ other)) | (high - (one ^ neighbour))) & high
    counts = lax.population_count(match)
    if diagonal is not None:
        across = lax.broadcasted_iota(I32, counts.shape, 0) - lax.broadcasted_iota(
            I32, counts.shape, 1
        )
        counts = jnp.where(across == diagonal, 0, counts)
    return counts.astype(F32)


def forward_kernel(*refs, tile, own, last):
    q_ref, n_ref, qid_ref, kid_ref = refs[:4]
    kv_refs = refs[4:6]
    acc_in = None if own else refs[6]
    place_ref = refs[6 + (not own)] if last else None
    acc_ref = refs[-2] if last else refs[-1]
    step = pl.program_id(0)
    steps = pl.num_programs(0) // 2

    @pl.when(step == 0)
    def _():
        acc_ref[...] = jnp.zeros_like(acc_ref) if own else acc_in[...]

    def part(kv_ref, diagonal_at):
        count = kv_ref.shape[0]
        keys = kv_ref[:, :DH]
        values = jnp.concatenate([kv_ref[:, DH:], jnp.ones((count, DH), BF16)], axis=1)
        for i in range(q_ref.shape[0] // tile):
            rows = slice(i * tile, (i + 1) * tile)
            scores = dot(q_ref[rows, :], keys, NT)
            powers = jnp.exp2(scores * LOG2E - n_ref[rows, :])
            diagonal = None if diagonal_at is None else diagonal_at * count - i * tile
            counts = pair_count(qid_ref[rows, :], kid_ref[0:1, :], kid_ref[2:3, :], diagonal)
            acc_ref[rows, :] += dot((powers * counts).astype(BF16), values)

    @pl.when(step < steps)
    def _():
        part(kv_refs[0], step if own else None)

    @pl.when(step >= steps)
    def _():
        part(kv_refs[1], None)

    if last:
        send_ref = refs[-1]
        rows = send_ref.shape[1]

        @pl.when(step == 2 * steps - 1)
        def _():
            for j in range(NH):
                block = acc_ref[j * rows : (j + 1) * rows, :]
                send_ref[place_ref[1] ^ j] = (block[:, :DH] / block[:, DH:]).astype(BF16)


def forward_call(queries, norms, ids, kv_pair, part, acc, place=None, tk=768, tile=256):
    nq, nk = queries.shape[0], kv_pair[0].shape[0]
    steps = nk // tk
    column = pl.BlockSpec((nq, 1), lambda j: (0, 0))
    full = pl.BlockSpec((nq, DH), lambda j: (0, 0))
    first = pl.BlockSpec((tk, 2 * DH), lambda j: (jnp.minimum(j, steps - 1), 0))
    second = pl.BlockSpec((tk, 2 * DH), lambda j: (jnp.maximum(j - steps, 0), 0))
    wide = pl.BlockSpec((nq, 2 * DH), lambda j: (0, 0))
    listed = pl.BlockSpec((8, tk), lambda j: (0, part * steps + j))
    inputs = [queries, norms, ids[0], ids[1], *kv_pair]
    specs = [full, column, column, listed, first, second]
    out_shape, out_specs = [shaped(nq, 2 * DH, dtype=F32)], [wide]
    if acc is not None:
        inputs.append(acc)
        specs.append(wide)
    if place is not None:
        inputs.append(place)
        specs.append(SMEM)
        out_shape.append(shaped(NH, nq // NH, DH))
        out_specs.append(pl.BlockSpec((NH, nq // NH, DH), lambda j: (0, 0, 0)))
    return pl.pallas_call(
        functools.partial(forward_kernel, tile=tile, own=acc is None, last=place is not None),
        grid=(2 * steps,),
        in_specs=specs,
        out_specs=out_specs,
        out_shape=out_shape,
        input_output_aliases={} if acc is None else {6: 0},
        compiler_params=pltpu.CompilerParams(vmem_limit_bytes=56 * 2**20),
        name="attention_forward",
    )(*inputs)


def backward_kernel(*refs, tile, own):
    q_ref, g_ref, n_ref, t_ref, qid_ref, kid_ref = refs[:6]
    kv_refs = refs[6:8]
    dq_ref, *dkv_refs = refs[-3:]
    step = pl.program_id(0)
    steps = pl.num_programs(0) // 2

    @pl.when(step == 0)
    def _():
        dq_ref[...] = refs[8][...] if own else jnp.zeros_like(dq_ref)

    def part(kv_ref, dkv_ref, diagonal_at):
        keys, values, key_ids = kv_ref[:, :DH], kv_ref[:, DH:], kid_ref[...]
        count = keys.shape[0]
        wide_keys = jnp.concatenate([keys, jnp.ones(keys.shape, BF16)], axis=1)
        grad_keys = jnp.zeros(keys.shape, F32)
        grad_values = jnp.zeros(keys.shape, F32)
        for i in range(q_ref.shape[0] // tile):
            rows = slice(i * tile, (i + 1) * tile)
            queries, grads = q_ref[rows, :], g_ref[rows, :]
            scores = dot(keys, queries, NT)
            powers = jnp.exp2(scores * LOG2E - n_ref[0:1, rows])
            diagonal = None if diagonal_at is None else i * tile - diagonal_at * count
            counts = pair_count(key_ids, qid_ref[0:1, rows], qid_ref[1:2, rows], diagonal)
            weights = powers * counts
            grad_weights = dot(values, grads, NT)
            grad_scores = (weights * (grad_weights + t_ref[0:1, rows])).astype(BF16)
            grad_values = grad_values + dot(weights.astype(BF16), grads)
            grad_keys = grad_keys + dot(grad_scores, queries)
            dq_ref[rows, :] += dot(grad_scores, wide_keys, TN)
        dkv_ref[...] = jnp.concatenate([grad_keys, grad_values], axis=1).astype(BF16)

    @pl.when(step < steps)
    def _():
        part(kv_refs[0], dkv_refs[0], step if own else None)

    @pl.when(step >= steps)
    def _():
        part(kv_refs[1], dkv_refs[1], None)


def backward_call(queries, grads, norms, terms, ids, kv_pair, part, acc, tk=768, tile=256):
    nq, nk = queries.shape[0], kv_pair[0].shape[0]
    steps = nk // tk
    full = pl.BlockSpec((nq, DH), lambda j: (0, 0))
    row = pl.BlockSpec((8, nq), lambda j: (0, 0))
    first = pl.BlockSpec((tk, 2 * DH), lambda j: (jnp.minimum(j, steps - 1), 0))
    second = pl.BlockSpec((tk, 2 * DH), lambda j: (jnp.maximum(j - steps, 0), 0))
    wide = pl.BlockSpec((nq, 2 * DH), lambda j: (0, 0))
    listed = pl.BlockSpec((tk, 1), lambda j: (part * steps + j, 0))
    more = [] if acc is None else [acc]
    return pl.pallas_call(
        functools.partial(backward_kernel, tile=tile, own=acc is not None),
        grid=(2 * steps,),
        in_specs=[full, full, row, row, row, listed, first, second] + [wide] * len(more),
        out_specs=[wide, first, second],
        out_shape=[shaped(nq, 2 * DH, dtype=F32), *[shaped(nk, 2 * DH)] * 2],
        input_output_aliases={8: 0} if more else {},
        compiler_params=pltpu.CompilerParams(vmem_limit_bytes=56 * 2**20),
        cost_estimate=LONG,
        name="attention_backward",
    )(queries, grads, norms, terms, ids[1], ids[0], *kv_pair, *more)


def out_kernel(place_ref, attn_ref, half_ref, gain_ref, *refs):
    parts, (low_ref, out_ref, normed_ref, weight_ref) = refs[:8], refs[8:]
    rows, width = weight_ref.shape[0] // 32, weight_ref.shape[1]
    masks = [core | near for core in (0, CORE) for near in (0, X, Y, X | Y)]
    for part, mask in zip(parts, masks, strict=True):
        for p in range(4):
            start = pl.multiple_of((((place_ref[0] ^ mask) & (Y | CORE | X)) | (p * Z_LO)) * rows, rows)
            weight_ref[pl.ds(start, rows // 2), :] = part[p, :, :width]
            middle = pl.multiple_of(start + rows // 2, rows // 2)
            weight_ref[pl.ds(middle, rows // 2), :] = part[p, :, width:]
    attn = jnp.concatenate([attn_ref[h] for h in range(NH)], axis=1)
    first_out = half_ref[...].astype(F32) + dot(attn, weight_ref[...])
    out_ref[...] = first_out
    low_ref[...] = first_out.astype(BF16)
    normed_ref[...] = (normalised(first_out)[0] * gain_ref[1:2, :]).astype(BF16)


def ffn_part(z_ref, units, down):
    width = z_ref.shape[2] // 2
    lanes = slice(width, None) if down else slice(width)
    return jnp.concatenate([z_ref[p, :units, lanes] for p in range(4)], axis=0)


def hidden_back_kernel(*refs):
    blocks, z_ref, out_ref = refs[:8], refs[8], refs[9]
    down = ffn_part(z_ref, out_ref.shape[1] // 4, True)
    for i, block in enumerate(blocks):
        rows = pl.ds(i * block.shape[0], block.shape[0])
        out_ref[rows, :] = dot(block[...], down, NT)


def ffn_kernel(*refs):
    blocks, back_ref, z_ref, outs = refs[:8], refs[8], refs[9], refs[10:]
    hidden_ref, grad_ref = outs[8:]
    up = ffn_part(z_ref, hidden_ref.shape[1] // 4, False)
    slope = 0.7978845608028654
    for i in (4, 5, 6, 7, 0, 1, 2, 3):
        block = blocks[i]
        rows = pl.ds(i * block.shape[0], block.shape[0])
        v = dot(block[...], up, NT)
        square = v * v
        t = jnp.tanh(slope * v * (1.0 + 0.044715 * square))
        half = 0.5 * (1.0 + t)
        hidden_ref[rows, :] = (v * half).astype(BF16)
        back = half + 0.5 * v * (1.0 - t * t) * slope * (1.0 + 3 * 0.044715 * square)
        grad = (back_ref[rows, :] * back).astype(BF16)
        grad_ref[rows, :] = grad
        outs[i][...] = dot(grad, up).astype(BF16)


def ffn_rest_kernel(*refs):
    blocks, grads, z_ref = refs[:8], refs[8:16], refs[18]
    hidden_ref, grad_ref = refs[16:18]
    near_ref, far_ref, sum_ref = refs[19:]
    width = sum_ref.shape[1] // 2
    units = sum_ref.shape[0] // 4
    down = ffn_part(z_ref, units, True)
    for i in range(8):
        rows = pl.ds(i * blocks[i].shape[0], blocks[i].shape[0])
        out = (near_ref, far_ref)[i // 4]
        out[i % 4] = dot(hidden_ref[rows, :], down).astype(BF16)
    inputs = jnp.concatenate([block[...] for block in blocks], axis=0)
    sum_ref[:, :width] = dot(grad_ref[...], inputs, TN).astype(BF16)
    cotangents = jnp.concatenate([block[...] for block in grads], axis=0)
    sum_ref[:, width:] = dot(hidden_ref[...], cotangents, TN).astype(BF16)


def mid_kernel(*refs):
    parts, rest, outs = refs[:5], refs[5:9], refs[9:]
    out_ref, first_ref, gain_ref, weight_ref = rest
    mid_ref, send_ref, gain_sum_ref = outs
    xhat, rstd = normalised(out_ref[...])
    grads = sum(part[...].astype(F32) for part in parts)
    gain_sum_ref[...] = jnp.broadcast_to(
        jnp.sum(grads * xhat, axis=0, keepdims=True), gain_sum_ref.shape
    )
    mid = first_ref[...].astype(F32) + norm_back(grads * gain_ref[1:2, :], xhat, rstd)
    mid = mid.astype(BF16)
    mid_ref[...] = mid
    grad_attn = dot(mid, weight_ref[...], NT).astype(BF16)
    for h in range(NH):
        send_ref[h] = grad_attn[:, h * DH : (h + 1) * DH]


def turn_kernel(place_ref, arrived_ref, acc_ref, grads_ref, row_ref, column_ref):
    rows = arrived_ref.shape[1]
    for j in range(NH):
        place = slice(j * rows, (j + 1) * rows)
        block = acc_ref[place, :]
        totals = block[:, DH:]
        attended = block[:, :DH] / totals
        grad_attn = arrived_ref[place_ref[1] ^ j].astype(F32)
        grads_ref[place, :] = (grad_attn / totals).astype(BF16)
        column_ref[place, :] = (
            -jnp.sum(grad_attn * attended, axis=-1, keepdims=True) / totals[:, :1]
        )
    to_row(column_ref, row_ref)


def grad_out_kernel(place_ref, attn_ref, mid_ref, gain_ref, keep_ref, send_ref):
    width = mid_ref.shape[1]
    heads = NH // 4
    core = (place_ref[0] >> 3) & 1
    gains = [
        jnp.broadcast_to(gain_ref[0:1, h * DH : (h + 1) * DH], (DH, DH)).T for h in range(NH)
    ]
    for ref, bit in ((keep_ref, core), (send_ref, 1 - core)):
        for i in range(NH // 2):
            first, k = divmod(i, heads)
            rows = slice(i * DH, (i + 1) * DH)
            attn = attn_ref[(2 * first + bit) * heads + k]
            ref[rows, :width] = dot(attn, mid_ref[...], TN).astype(BF16)
            low, high = (gains[(2 * first + b) * heads + k] for b in range(2))
            ref[rows, width:] = jnp.where(bit == 0, low, high).astype(BF16)


def halve_kernel(place_ref, kept_ref, came_ref, keep_ref, send_ref, *, shift, blocks):
    rows = kept_ref.shape[0] // (2 * blocks)
    bit = (place_ref[0] >> shift) & 1
    for i in range(blocks):
        out = slice(i * rows, (i + 1) * rows)
        for ref, half in ((keep_ref, bit), (send_ref, 1 - bit)):
            start = pl.ds(pl.multiple_of((2 * i + half) * rows, rows), rows)
            total = kept_ref[start, :].astype(F32) + came_ref[start, :].astype(F32)
            ref[out, :] = total.astype(BF16)


def gather_grads_kernel(place_ref, direct_ref, q_ref, n_ref, *refs):
    kv_refs, (send_ref, both_ref) = refs[:3], refs[3:]
    rows = send_ref.shape[1]
    for j in range(NH):
        place = slice(j * rows, (j + 1) * rows)
        grad_kv = sum(ref[place, :].astype(F32) for ref in kv_refs)
        grad_keys, grad_values = grad_kv[:, :DH], grad_kv[:, DH:]
        queries = q_ref[place, :].astype(F32)
        inverse = lax.rsqrt(jnp.mean(queries * queries, axis=-1, keepdims=True) + 1e-06)
        mean_part = jnp.mean(grad_keys * queries, axis=-1, keepdims=True)
        grad_norms = -direct_ref[place, DH:]
        grad_queries = (
            direct_ref[place, :DH]
            + grad_norms * queries * (LOG2E / n_ref[place, :])
            + (inverse * DH ** (-0.5)) * (grad_keys - queries * (inverse * inverse * mean_part))
        )
        both = jnp.concatenate([grad_queries.astype(BF16), grad_values.astype(BF16)], axis=1)
        both_ref[place, :] = both
        send_ref[place_ref[1] ^ j] = both


def project_back_kernel(place_ref, normed_ref, both_ref, *refs):
    outs, sum_ref = refs[:4], refs[4]
    sum_ref[...] = dot(normed_ref[...], both_ref[...], TN)
    rows = outs[0].shape[1]
    for out, mask in zip(outs, PARTS, strict=True):
        for j in range(NH):
            start = pl.multiple_of((place_ref[0] ^ mask ^ j) * rows, rows)
            out[j] = sum_ref[pl.ds(start, rows), :].astype(BF16)


def sum_kernel(place_ref, *refs):
    parts, out = refs[:4], refs[4]
    for j in range(NH):
        out[place_ref[1] ^ j] = sum(part[j].astype(F32) for part in parts).astype(BF16)


def own_rows_kernel(rows_ref, qk_ref, value_ref, gain_ref, *outs):
    grad_qk_ref, grad_value_ref, grad_gain_ref = outs
    for h in range(NH):
        lanes = slice(h * DH, (h + 1) * DH)
        grad_qk_ref[:, lanes] = rows_ref[h, :, :DH].astype(F32)
        grad_value_ref[:, lanes] = rows_ref[h, :, DH:].astype(F32)
    total = jnp.sum(
        qk_ref[...].astype(F32) * grad_qk_ref[...]
        + value_ref[...].astype(F32) * grad_value_ref[...],
        axis=-1,
        keepdims=True,
    )
    grad_gain_ref[...] = jnp.broadcast_to(
        total / gain_ref[:, :1].astype(F32), grad_gain_ref.shape
    )


def unpack_kernel(sum_ref, up_ref, down_ref):
    width = sum_ref.shape[1] // 2
    up_ref[...] = sum_ref[:, :width].astype(F32).T
    down_ref[...] = sum_ref[:, width:].astype(F32)


def last_kernel(arrived_ref, half_ref, grad_ref, gain_ref, weight_ref, out_ref):
    width = half_ref.shape[1]
    grad_q = jnp.concatenate([arrived_ref[h][:, :DH] for h in range(NH)], axis=1)
    grad_v = jnp.concatenate([arrived_ref[h][:, DH:] for h in range(NH)], axis=1)
    grads = dot(grad_q, weight_ref[:, :width], NT) + dot(grad_v, weight_ref[:, width:], NT)
    xhat, rstd = normalised(half_ref[...].astype(F32))
    out_ref[...] = (
        grad_ref[...].astype(F32) + norm_back(grads * gain_ref[0:1, :], xhat, rstd)
    ).astype(BF16)


def cube_plan(
    first_half,
    second_half,
    grad_first,
    grad_second,
    qk_weight,
    value_weight,
    out_weight,
    attn_gain,
    ffn_gain,
    up_weight,
    down_weight,
    stretch_ids,
):
    y, core, z_hi, z_lo, x = (lax.axis_index(name) for name in BITS)
    me = y * 16 + core * 8 + z_hi * 4 + z_lo * 2 + x
    place = jnp.stack([me, me & 7]).astype(I32)
    rows, width = first_half.shape
    wide_rows = rows * 8
    own_rows = qk_weight.shape[0]
    own_units = down_weight.shape[0]
    units = own_units * 4
    rounds, tokens = stretch_ids.shape
    nchunk = tokens // STRETCH
    row_block = shaped(rows, width)
    acc_shape = shaped(rows, width, dtype=F32)

    blocks = gather_zx(second_half)
    gains = jnp.pad(jnp.stack([attn_gain, ffn_gain], axis=1), ((0, 0), (0, DH - 2)))
    columns, z_rows, qv_rows = call(
        pack_kernel,
        [Far(a) for a in (qk_weight, value_weight, out_weight, up_weight, down_weight, gains)],
        [
            shaped(NH, own_rows, 3 * DH),
            shaped(own_units + own_rows // 2, 2 * width),
            shaped(own_rows, 2 * width),
        ],
        "pack",
        cost=None,
        far_out=(1, 2),
    )
    columns = shares(lax.all_to_all(columns, HEAD_AXES, 0, 0, tiled=True))
    weights = lax.all_gather(after(z_rows, blocks[4]), ("z_hi", "z_lo"), axis=0)
    cotangent_y = swap(grad_second, Y)

    ids = stretch_ids.reshape(rounds, 2, 2, 2, 2, 2, rows)
    for axis, bit in enumerate((y, core, z_hi, z_lo, x), 1):
        ids = jnp.where(bit == 1, jnp.flip(ids, axis), ids)
    ids = ids.reshape(rounds, tokens)

    def packed(numbers):
        return sum(numbers[r] << (8 * r) for r in range(rounds))

    ids_row = packed(ids)
    ids_rows = jnp.concatenate(
        [
            ids_row[None],
            packed((ids + nchunk - 1) % nchunk)[None],
            packed((ids + 1) % nchunk)[None],
            jnp.zeros((5, tokens), I32),
        ]
    )
    ids_column = call(
        column_kernel, [Far(ids_rows)], [shaped(tokens, 1, dtype=I32)], "ids", far_out=(0,), cost=None
    )[0]
    ids_both = (ids_column, ids_rows)

    columns[0] = after(columns[0], *ids_both)
    normed, queries, kv, norms, norm_row, gain_rows = call(
        project_kernel,
        [Far(blocks[0]), *blocks[1:], *columns],
        [
            shaped(wide_rows, width),
            shaped(wide_rows, DH),
            shaped(wide_rows, 2 * DH),
            shaped(wide_rows, 1, dtype=F32),
            shaped(8, wide_rows, dtype=F32),
            shaped(8, width, dtype=F32),
        ],
        "project",
        cost=None,
        far_out=range(6),
        scalars=[place],
        scratch=[pltpu.VMEM((width, 3 * DH), BF16)],
    )
    kv_parts = shares(kv)
    acc, = forward_call(queries, norms, ids_both, kv_parts[:2], 0, None)
    kv_parts[3] = swap(after(kv_parts[2], acc), CORE)
    near, near_y = after(grad_second, kv_parts[3]), after(cotangent_y, kv_parts[3])
    cotangents = [near, swap(near, X), near_y, swap(near_y, X)]
    acc, attn_send = forward_call(queries, norms, ids_both, kv_parts[2:], 2, acc, place)
    attn_send = after(attn_send, *cotangents)
    out_parts = gather_xy(after(weights, attn_send)[:, own_units:])
    cotangents = with_cores([after(a, attn_send) for a in cotangents])
    qv_full = lax.all_gather(after(qv_rows, attn_send), BITS, axis=0, tiled=True)
    attn_tok = lax.all_to_all(attn_send, HEAD_AXES, 0, 0, tiled=True)
    units = own_units * 4
    hidden_back = call(
        hidden_back_kernel,
        [*map(Far, cotangents), Far(weights)],
        [shaped(wide_rows, units, dtype=F32)],
        "hidden_back",
        cost=None,
        far_out=(0,),
    )[0]
    attn_tok = after(attn_tok, hidden_back)
    y_first, first_out, normed_ffn, out_full = call(
        out_kernel,
        [attn_tok, Far(first_half), Far(gain_rows), *out_parts],
        [row_block, acc_shape, row_block, shaped(width, width)],
        "project_out",
        cost=None,
        far_out=(0, 1, 3),
        scalars=[place],
    )
    ffn_in = gather_xy(normed_ffn)
    *grad_blocks, hidden, grad_pre = call(
        ffn_kernel,
        [*ffn_in, Far(hidden_back), Far(weights)],
        [row_block] * 8 + [shaped(wide_rows, units)] * 2,
        "feed_forward",
        cost=None,
        mib=44,
    )
    grad_parts = scatter_xy(grad_blocks)
    ffn_near, ffn_far, grad_ffn = call(
        ffn_rest_kernel,
        [*ffn_in, *map(Far, cotangents), hidden, grad_pre, Far(weights)],
        [shaped(4, rows, width)] * 2 + [shaped(units, 2 * width)],
        "feed_forward_rest",
        cost=None,
        far_out=range(3),
        mib=48,
    )
    grad_mid, grad_attn, gain_sum = call(
        mid_kernel,
        [
            *grad_parts,
            *map(Far, (after(first_out, grad_ffn, qv_full), grad_first, gain_rows, out_full)),
        ],
        [row_block, shaped(NH, rows, DH), shaped(8, width, dtype=F32)],
        "mid",
        cost=None,
        far_out=(0,),
    )

    grad_attn = lax.all_to_all(grad_attn, HEAD_AXES, 0, 0, tiled=True)

    out_width = width + DH
    half = shaped(width // 2, out_width)
    keep, move = call(
        grad_out_kernel,
        [Far(attn_tok), Far(grad_mid), Far(gain_sum)],
        [half, half],
        "grad_out",
        far_out=(0,),
        scalars=[place],
    )

    def halve(keep, came, shift, blocks):
        half = shaped(keep.shape[0] // 2, out_width)
        return call(
            functools.partial(halve_kernel, shift=shift, blocks=blocks),
            [Far(keep), came],
            [half, half],
            "halve",
            far_out=(0,),
            scalars=[place],
        )

    keep, move = halve(keep, swap(move, CORE), 4, 1)
    came = swap(move, Y)
    grads, term_row = call(
        turn_kernel,
        [after(grad_attn, move), Far(acc)],
        [shaped(wide_rows, DH), shaped(8, wide_rows, dtype=F32)],
        "turn",
        far_out=(0, 1),
        scalars=[place],
        scratch=[pltpu.VMEM((wide_rows, 1), F32)],
    )

    def backward(part, acc):
        return backward_call(
            queries, grads, norm_row, term_row, ids_both, kv_parts[part : part + 2], part, acc
        )

    ffn_far = swap(after(ffn_far, grads), CORE)
    grad_ffn = lax.psum_scatter(
        grad_ffn, ("z_hi", "z_lo"), scatter_dimension=0, tiled=True
    )
    direct, over_y, far = backward(2, None)
    far = swap(far, CORE)
    keep, move = halve(keep, after(came, direct), 0, 4)
    over_y = (over_y.astype(F32) + after(far, move).astype(F32)).astype(BF16)
    direct = after(direct, over_y)
    over_y = swap(over_y, Y)
    came = swap(move, X)
    direct, grad_kv, over_core = backward(0, direct)
    direct = after(direct, grad_ffn)
    over_core = swap(after(over_core, over_y), CORE)

    send, grad_both = call(
        gather_grads_kernel,
        [*map(Far, (direct, queries, norms, grad_kv)), over_core, over_y],
        [shaped(NH, rows, 2 * DH), shaped(wide_rows, 2 * DH)],
        "gather_grads",
        far_out=(1,),
        scalars=[place],
    )
    arrived = lax.all_to_all(send, HEAD_AXES, 0, 0, tiled=True)

    grad_rows = call(
        project_back_kernel,
        [Far(normed), Far(grad_both)],
        [shaped(NH, own_rows, 2 * DH)] * 4,
        "project_back",
        scalars=[place],
        scratch=[pltpu.VMEM((width, 2 * DH), F32)],
    )
    rows_parts = grad_rows
    grad_rows = call(
        sum_kernel,
        [after(part, arrived) for part in sum_shares(grad_rows)],
        [shaped(NH, own_rows, 2 * DH)],
        "sum_rows",
        scalars=[place],
    )
    rows_send = grad_rows[0]
    grad_rows = lax.all_to_all(rows_send, HEAD_AXES, 0, 0, tiled=True)
    grad_second_half = call(
        last_kernel,
        [arrived, *map(Far, (second_half, grad_second, gain_rows, qv_full))],
        [row_block],
        "last",
        far_out=(0,),
    )[0]

    keep, move = halve(keep, after(came, rows_parts[0]), 1, 2)
    keep, move = halve(keep, after(swap(move, Z_LO), rows_send), 2, 1)
    grad_out = keep.astype(F32) + swap(move, Z_HI).astype(F32)
    ffn_sum = after(ffn_near, rows_parts[0]).astype(F32) + ffn_far.astype(F32)
    ffn_move = swap(ffn_sum[1::2].astype(BF16), X)
    ffn_sum = ffn_sum[0::2] + after(ffn_move, rows_send).astype(F32)
    ffn_sum = ffn_sum[0] + swap(ffn_sum[1].astype(BF16), Y).astype(F32)
    second_out = second_half.astype(F32) + ffn_sum
    grad_up, grad_down = call(
        unpack_kernel,
        [Far(after(grad_ffn, arrived))],
        [shaped(width, own_units, dtype=F32), shaped(own_units, width, dtype=F32)],
        "unpack",
        far_out=(0, 1),
    )
    grad_qk, grad_value, grad_attn_gain = call(
        own_rows_kernel,
        [after(grad_rows, grad_second_half, grad_up), Far(qk_weight), Far(value_weight), Far(gains)],
        [shaped(own_rows, width, dtype=F32)] * 2 + [shaped(own_rows, 128, dtype=F32)],
        "own_rows",
        far_out=(0, 1),
    )

    return (
        y_first,
        second_out.astype(BF16),
        grad_mid,
        grad_second_half,
        grad_qk,
        grad_value,
        grad_out[:, :width],
        grad_attn_gain[:, 0],
        grad_out[:, width],
        grad_up,
        grad_down,
    )


def solution(mesh):
    if dict(mesh.shape) == {"head": 4, "blk": 8}:
        plan, axes = cube_plan, BITS
        mesh = jax.sharding.Mesh(mesh.devices.reshape((2,) * 5), BITS)
    else:
        plan, axes = ring_plan, ("head", "blk")
    by_row, by_column, vector = P(axes, None), P(None, axes), P(axes)
    return jax.shard_map(
        plan,
        mesh=mesh,
        in_specs=(by_row,) * 7 + (vector, vector, by_column, by_row, P()),
        out_specs=(by_row,) * 7 + (vector, vector, by_column, by_row),
        check_vma=False,
    )
```

```python
import functools

import jax
import jax.numpy as jnp
from jax import lax
from jax.experimental import pallas as pl
from jax.experimental.pallas import tpu as pltpu
from jax.sharding import PartitionSpec as P

NH = 8
DH = 128
STRETCH = 64


def shifted(value, axis, by):
    devices = lax.axis_size(axis)
    return lax.ppermute(value, axis, [(i, (i + by) % devices) for i in range(devices)])


def layer_norm(values, gains):
    average = jnp.mean(values, axis=-1, keepdims=True)
    centred = values - average
    variance = jnp.mean(centred * centred, axis=-1, keepdims=True)
    return centred * lax.rsqrt(variance + 1e-05) * gains


def key_norm(queries):
    return (
        queries
        * lax.rsqrt(jnp.mean(queries * queries, axis=-1, keepdims=True) + 1e-06)
        * queries.shape[-1] ** (-0.5)
    )


def row_norm(queries):
    return jnp.sqrt(jnp.sum(queries * queries, axis=-1) + 1e-06)


def group_ids(stretch_ids, heads_count, cycle_count, local_rows, cycle_index):
    shaped = stretch_ids.reshape(stretch_ids.shape[0], heads_count, cycle_count, local_rows)
    picked = lax.dynamic_slice_in_dim(shaped, cycle_index, 1, 2)
    places = (
        jnp.arange(heads_count, dtype=jnp.int32)[:, None] * cycle_count + cycle_index
    ) * local_rows
    places = places + jnp.arange(local_rows, dtype=jnp.int32)[None, :]
    return (picked.reshape(stretch_ids.shape[0], heads_count * local_rows), places.reshape(-1))


def pair_counts(query_ids, query_places, key_ids, key_places, nchunk):
    previous = (query_ids + nchunk - 1) % nchunk
    same_stretch = key_ids[:, None, :] == query_ids[:, :, None]
    before = key_ids[:, None, :] == previous[:, :, None]
    counts = jnp.sum((same_stretch | before).astype(jnp.float32), axis=0)
    return counts * (query_places[:, None] != key_places[None, :]).astype(jnp.float32)


def forward_block(queries, query_norms, counts, key_block, value_block):
    scores = jnp.einsum("qhd,khd->hqk", queries, key_block, preferred_element_type=jnp.float32)
    weights = counts[None] * jnp.exp(scores - query_norms.T[:, :, None])
    summed = jnp.einsum(
        "hqk,khd->qhd",
        weights.astype(jnp.bfloat16),
        value_block,
        preferred_element_type=jnp.float32,
    )
    return (jnp.sum(weights, axis=-1), summed)


def backward_block(queries, query_norms, counts, key_block, value_block, grad_summed, grad_totals):
    scores = jnp.einsum("qhd,khd->hqk", queries, key_block, preferred_element_type=jnp.float32)
    weights = counts[None] * jnp.exp(scores - query_norms.T[:, :, None])
    grad_weights = jnp.einsum(
        "qhd,khd->hqk", grad_summed, value_block, preferred_element_type=jnp.float32
    )
    grad_scores_f = weights * (grad_weights + grad_totals[:, :, None])
    grad_scores = grad_scores_f.astype(jnp.bfloat16)
    grad_norms = -jnp.sum(grad_scores_f, axis=-1)
    grad_values = jnp.einsum(
        "hqk,qhd->khd",
        weights.astype(jnp.bfloat16),
        grad_summed,
        preferred_element_type=jnp.float32,
    )
    grad_direct = jnp.einsum(
        "hqk,khd->qhd", grad_scores, key_block, preferred_element_type=jnp.float32
    )
    grad_keys = jnp.einsum("hqk,qhd->khd", grad_scores, queries, preferred_element_type=jnp.float32)
    return (grad_norms, grad_direct, grad_keys, grad_values)


def feed_forward(normed_ffn, grad_output, up_part, down_part):
    pre_act = jnp.dot(normed_ffn, up_part, preferred_element_type=jnp.float32)
    hidden_f, gelu_back = jax.vjp(jax.nn.gelu, pre_act)
    hidden = hidden_f.astype(jnp.bfloat16)
    ffn_result = jnp.dot(hidden, down_part, preferred_element_type=jnp.float32)
    grad_hidden = jnp.dot(grad_output, down_part.T, preferred_element_type=jnp.float32)
    grad_pre = gelu_back(grad_hidden)[0].astype(jnp.bfloat16)
    grad_normed = jnp.dot(grad_pre, up_part.T, preferred_element_type=jnp.float32)
    grad_up = jnp.dot(normed_ffn.T, grad_pre, preferred_element_type=jnp.float32)
    grad_down = jnp.dot(hidden.T, grad_output, preferred_element_type=jnp.float32)
    return (ffn_result, grad_normed, grad_up, grad_down)


def ring_plan(
    first_half,
    second_half,
    grad_first,
    grad_second,
    qk_weight,
    value_weight,
    out_weight,
    attn_gain,
    ffn_gain,
    up_weight,
    down_weight,
    stretch_ids,
):
    heads_count = lax.axis_size("head")
    cycle_count = lax.axis_size("blk")
    cycle_index = lax.axis_index("blk")
    local_rows = first_half.shape[0]
    model_width = first_half.shape[1]
    group_rows = local_rows * heads_count
    local_heads = NH // heads_count
    nchunk = stretch_ids.shape[1] // STRETCH
    full_qk, full_value, full_out, full_attn_gain, full_ffn_gain, up_part, down_part = (
        lax.all_gather(qk_weight, ("head", "blk"), axis=0, tiled=True),
        lax.all_gather(value_weight, ("head", "blk"), axis=0, tiled=True),
        lax.all_gather(out_weight, ("head", "blk"), axis=0, tiled=True),
        lax.all_gather(attn_gain, ("head", "blk"), axis=0, tiled=True),
        lax.all_gather(ffn_gain, ("head", "blk"), axis=0, tiled=True),
        lax.all_gather(up_weight, ("head", "blk"), axis=1, tiled=True),
        lax.all_gather(down_weight, ("head", "blk"), axis=0, tiled=True),
    )
    second_f = second_half.astype(jnp.float32)
    normed_f, attn_norm_back = jax.vjp(layer_norm, second_f, full_attn_gain.astype(jnp.float32))
    normed = normed_f.astype(jnp.bfloat16)
    query_tok = jnp.dot(normed, full_qk, preferred_element_type=jnp.float32).astype(jnp.bfloat16)
    value_tok = jnp.dot(normed, full_value, preferred_element_type=jnp.float32).astype(jnp.bfloat16)
    query_heads = query_tok.reshape(local_rows, NH, DH)
    value_heads = value_tok.reshape(local_rows, NH, DH)
    queries, values = (
        lax.all_to_all(query_heads, "head", split_axis=1, concat_axis=0, tiled=True),
        lax.all_to_all(value_heads, "head", split_axis=1, concat_axis=0, tiled=True),
    )
    query_f = queries.astype(jnp.float32)
    key_f, key_back = jax.vjp(key_norm, query_f)
    keys = key_f.astype(jnp.bfloat16)
    query_norms, norm_back = jax.vjp(row_norm, query_f)
    query_ids, query_places = group_ids(
        stretch_ids, heads_count, cycle_count, local_rows, cycle_index
    )

    def counts_for(cycle_step):
        source_index = (cycle_index - cycle_step + cycle_count) % cycle_count
        key_ids, key_places = group_ids(
            stretch_ids, heads_count, cycle_count, local_rows, source_index
        )
        return pair_counts(query_ids, query_places, key_ids, key_places, nchunk)

    def rotate(key_block, value_block):
        return shifted((key_block, value_block), "blk", 1)

    def forward_step(cycle_step, carried):
        key_block, value_block, totals, summed = carried
        part_totals, part_summed = forward_block(
            queries, query_norms, counts_for(cycle_step), key_block, value_block
        )
        key_next, value_next = rotate(key_block, value_block)
        return (key_next, value_next, totals + part_totals, summed + part_summed)

    initial = (
        keys,
        values,
        jnp.zeros((local_heads, group_rows), jnp.float32),
        jnp.zeros((group_rows, local_heads, DH), jnp.float32),
    )
    key_block, value_block, totals, summed = lax.fori_loop(
        0, cycle_count - 1, forward_step, initial
    )
    part_totals, part_summed = forward_block(
        queries, query_norms, counts_for(cycle_count - 1), key_block, value_block
    )
    totals = totals + part_totals
    summed = summed + part_summed
    attended = summed / totals.T[:, :, None]
    attn_tok = lax.all_to_all(
        attended.astype(jnp.bfloat16), "head", split_axis=0, concat_axis=1, tiled=True
    ).reshape(local_rows, model_width)
    first_out = first_half.astype(jnp.float32) + jnp.dot(
        attn_tok, full_out, preferred_element_type=jnp.float32
    )
    normed_ffn_f, ffn_norm_back = jax.vjp(layer_norm, first_out, full_ffn_gain.astype(jnp.float32))
    normed_ffn = normed_ffn_f.astype(jnp.bfloat16)
    ffn_result, grad_normed_ffn, grad_up, grad_down = feed_forward(
        normed_ffn, grad_second, up_part, down_part
    )
    second_out = second_f + ffn_result
    grad_mid_ffn, grad_ffn_gain = ffn_norm_back(grad_normed_ffn)
    grad_mid = grad_first.astype(jnp.float32) + grad_mid_ffn
    grad_mid_low = grad_mid.astype(jnp.bfloat16)
    grad_out = jnp.dot(attn_tok.T, grad_mid_low, preferred_element_type=jnp.float32)
    grad_attn_tok = jnp.dot(grad_mid_low, full_out.T, preferred_element_type=jnp.float32).astype(
        jnp.bfloat16
    )
    grad_attn = lax.all_to_all(
        grad_attn_tok.reshape(local_rows, NH, DH), "head", split_axis=1, concat_axis=0, tiled=True
    )
    grad_attn_f = grad_attn.astype(jnp.float32)
    grad_summed = (grad_attn_f / totals.T[:, :, None]).astype(jnp.bfloat16)
    grad_totals = (-jnp.sum(grad_attn_f * attended, axis=-1) / totals.T).T

    def pass_grads(grad_keys, grad_values):
        return (
            shifted(grad_keys.astype(jnp.bfloat16), "blk", 1).astype(grad_keys.dtype),
            shifted(grad_values.astype(jnp.bfloat16), "blk", 1).astype(grad_values.dtype),
        )

    def backward_step(cycle_step, carried):
        key_block, value_block, grad_keys, grad_values, grad_norms, grad_direct = carried
        pieces = backward_block(
            queries,
            query_norms,
            counts_for(cycle_step),
            key_block,
            value_block,
            grad_summed,
            grad_totals,
        )
        key_next, value_next = rotate(key_block, value_block)
        grad_keys, grad_values = pass_grads(grad_keys + pieces[2], grad_values + pieces[3])
        return (
            key_next,
            value_next,
            grad_keys,
            grad_values,
            grad_norms + pieces[0],
            grad_direct + pieces[1],
        )

    zero_rows = jnp.zeros((group_rows, local_heads, DH), jnp.float32)
    initial = (
        keys,
        values,
        zero_rows,
        zero_rows,
        jnp.zeros((local_heads, group_rows), jnp.float32),
        zero_rows,
    )
    carried = lax.fori_loop(0, cycle_count - 1, backward_step, initial)
    pieces = backward_block(
        queries,
        query_norms,
        counts_for(cycle_count - 1),
        carried[0],
        carried[1],
        grad_summed,
        grad_totals,
    )
    grad_keys, grad_values = pass_grads(carried[2] + pieces[2], carried[3] + pieces[3])
    grad_norms = carried[4] + pieces[0]
    grad_direct = carried[5] + pieces[1]
    grad_queries = grad_direct + norm_back(grad_norms.T)[0] + key_back(grad_keys)[0]
    grad_q_tok, grad_v_tok = (
        lax.all_to_all(
            grad_queries.astype(jnp.bfloat16), "head", split_axis=0, concat_axis=1, tiled=True
        ),
        lax.all_to_all(
            grad_values.astype(jnp.bfloat16), "head", split_axis=0, concat_axis=1, tiled=True
        ),
    )
    grad_q_tok = grad_q_tok.reshape(local_rows, model_width)
    grad_v_tok = grad_v_tok.reshape(local_rows, model_width)
    grad_normed = jnp.dot(grad_q_tok, full_qk.T, preferred_element_type=jnp.float32) + jnp.dot(
        grad_v_tok, full_value.T, preferred_element_type=jnp.float32
    )
    grad_qk = jnp.dot(normed.T, grad_q_tok, preferred_element_type=jnp.float32)
    grad_value = jnp.dot(normed.T, grad_v_tok, preferred_element_type=jnp.float32)
    grad_second_attn, grad_attn_gain = attn_norm_back(grad_normed)
    grad_second_total = grad_second.astype(jnp.float32) + grad_second_attn
    sum_qk, sum_value, sum_out, sum_attn_gain, sum_ffn_gain, sum_up, sum_down = (
        lax.psum_scatter(grad_qk, ("head", "blk"), scatter_dimension=0, tiled=True),
        lax.psum_scatter(grad_value, ("head", "blk"), scatter_dimension=0, tiled=True),
        lax.psum_scatter(grad_out, ("head", "blk"), scatter_dimension=0, tiled=True),
        lax.psum_scatter(grad_attn_gain, ("head", "blk"), scatter_dimension=0, tiled=True),
        lax.psum_scatter(grad_ffn_gain, ("head", "blk"), scatter_dimension=0, tiled=True),
        lax.psum_scatter(grad_up, ("head", "blk"), scatter_dimension=1, tiled=True),
        lax.psum_scatter(grad_down, ("head", "blk"), scatter_dimension=0, tiled=True),
    )
    return (
        first_out.astype(jnp.bfloat16),
        second_out.astype(jnp.bfloat16),
        grad_mid.astype(jnp.bfloat16),
        grad_second_total.astype(jnp.bfloat16),
        sum_qk,
        sum_value,
        sum_out,
        sum_attn_gain,
        sum_ffn_gain,
        sum_up,
        sum_down,
    )


BITS = ("y", "core", "z_hi", "z_lo", "x")
Y, CORE, Z_HI, Z_LO, X = 16, 8, 4, 2, 1
HEAD_AXES = ("z_hi", "z_lo", "x")
PARTS = (0, CORE, Y, Y | CORE)
LOG2E = 1.4426950408889634
HIGH_BITS = -2139062144
NT = (((1,), (1,)), ((), ()))
NN = (((1,), (0,)), ((), ()))
TN = (((0,), (0,)), ((), ()))
F32, BF16, I32 = jnp.float32, jnp.bfloat16, jnp.int32
LONG = pl.CostEstimate(flops=10**11, bytes_accessed=1, transcendentals=0)
SMEM = pl.BlockSpec(memory_space=pltpu.SMEM)


def dot(left, right, dims=NN):
    return lax.dot_general(left, right, dims, preferred_element_type=F32)


def swap(value, mask):
    return lax.ppermute(value, BITS, [(i, i ^ mask) for i in range(32)])


def after(value, *others):
    return lax.optimization_barrier((value, *others))[0]


def shaped(*shape, dtype=BF16):
    return jax.ShapeDtypeStruct(shape, dtype)


class Far:
    def __init__(self, value):
        self.value = value


def call(kernel, inputs, out_shape, name, far_out=(), mib=56, scalars=(), scratch=(), cost=LONG):
    far_in = [i for i, a in enumerate(inputs) if isinstance(a, Far)]
    arrays = [a.value if isinstance(a, Far) else a for a in inputs]
    first_in, first_out = len(scalars), len(scalars) + len(arrays)
    first_scratch = first_out + len(out_shape)
    staged = [arrays[i] for i in far_in] + [out_shape[i] for i in far_out]

    def body(*refs):
        refs, sems = list(refs[:-1]), refs[-1]
        own = refs[first_scratch : first_scratch + len(scratch)]
        stages = refs[first_scratch + len(scratch) :]
        copies = []
        for k, i in enumerate(far_in):
            copies.append(pltpu.make_async_copy(refs[first_in + i], stages[k], sems.at[k]))
            refs[first_in + i] = stages[k]
        for copy in copies:
            copy.start()
        for copy in copies:
            copy.wait()
        copies = []
        for k, i in enumerate(far_out, len(far_in)):
            copies.append(pltpu.make_async_copy(stages[k], refs[first_out + i], sems.at[k]))
            refs[first_out + i] = stages[k]
        kernel(*refs[:first_scratch], *own)
        for copy in copies:
            copy.start()
        for copy in copies:
            copy.wait()

    near, far = pl.BlockSpec(memory_space=pltpu.VMEM), pl.BlockSpec(memory_space=pl.ANY)
    return pl.pallas_call(
        body,
        in_specs=[SMEM] * len(scalars) + [far if i in far_in else near for i in range(len(arrays))],
        out_specs=[far if i in far_out else near for i in range(len(out_shape))],
        out_shape=out_shape,
        scratch_shapes=[
            *scratch,
            *(pltpu.VMEM(a.shape, a.dtype) for a in staged),
            pltpu.SemaphoreType.DMA((max(len(staged), 1),)),
        ],
        compiler_params=pltpu.CompilerParams(vmem_limit_bytes=mib * 2**20),
        cost_estimate=cost,
        name=name,
    )(*scalars, *arrays)


def with_cores(near):
    return near + [swap(part, CORE) for part in near]


def near_xy(value):
    return [value, swap(value, X), swap(value, Y), swap(value, X | Y)]


def gather_xy(value):
    return with_cores(near_xy(value))


def gather_zx(value):
    low, high = swap(value, Z_LO), swap(value, Z_HI)
    line = [value, low, high, swap(high, Z_LO)]
    return [block for part in line for block in (part, swap(part, X))]


def scatter_xy(blocks):
    arrived = [swap(block, CORE) for block in blocks[4:]]
    sums = [
        (near.astype(F32) + far.astype(F32)).astype(BF16)
        for near, far in zip(blocks[1:4], arrived[1:], strict=True)
    ]
    sent = [swap(part, mask) for part, mask in zip(sums, (X, Y, X | Y), strict=True)]
    return [blocks[0], arrived[0], *sent]


def scatter_by_x(blocks):
    arrived = [swap(block, CORE) for block in blocks[4:]]
    own, one, two, both = (
        near.astype(F32) + far.astype(F32) for near, far in zip(blocks[:4], arrived, strict=True)
    )
    own = own + swap(one.astype(BF16), X).astype(F32)
    two = two + swap(both.astype(BF16), X).astype(F32)
    return own + swap(two.astype(BF16), Y).astype(F32)


def shares(value):
    over_y = swap(value, Y)
    return [value, swap(value, CORE), over_y, swap(over_y, CORE)]


def sum_shares(blocks):
    return [blocks[0]] + [swap(b, mask) for b, mask in zip(blocks[1:], PARTS[1:], strict=True)]


def normalised(values):
    centred = values - jnp.mean(values, axis=-1, keepdims=True)
    rstd = lax.rsqrt(jnp.mean(centred * centred, axis=-1, keepdims=True) + 1e-05)
    return centred * rstd, rstd


def norm_back(scaled_grads, xhat, rstd):
    return rstd * (
        scaled_grads
        - jnp.mean(scaled_grads, axis=-1, keepdims=True)
        - xhat * jnp.mean(scaled_grads * xhat, axis=-1, keepdims=True)
    )


def to_row(column_ref, row_ref):
    for i in range(row_ref.shape[1] // 128):
        chunk = slice(i * 128, (i + 1) * 128)
        square = jnp.broadcast_to(column_ref[chunk, :], (128, 128))
        row_ref[:, chunk] = square.T[0:8, :]


def pack_kernel(*refs):
    qk_ref, value_ref, out_ref, up_ref, down_ref, gain_ref, columns_ref, z_ref, qv_ref = refs
    rows, width = qk_ref.shape
    units = down_ref.shape[0]
    for h in range(NH):
        lanes = slice(h * DH, (h + 1) * DH)
        columns_ref[h, :, :DH] = qk_ref[:, lanes]
        columns_ref[h, :, DH : 2 * DH] = value_ref[:, lanes]
        columns_ref[h, :, 2 * DH :] = gain_ref[...]
    z_ref[:units, :width] = up_ref[...].astype(F32).T.astype(BF16)
    z_ref[:units, width:] = down_ref[...]
    z_ref[units:, :width] = out_ref[: rows // 2, :]
    z_ref[units:, width:] = out_ref[rows // 2 :, :]
    qv_ref[:, :width] = qk_ref[...]
    qv_ref[:, width:] = value_ref[...]


def column_kernel(row_ref, column_ref):
    for i in range(row_ref.shape[1] // 128):
        chunk = slice(i * 128, (i + 1) * 128)
        square = jnp.broadcast_to(row_ref[0:1, chunk], (128, 128))
        column_ref[chunk, :] = square.T[:, 0:1]


def project_kernel(place_ref, *refs):
    blocks, parts, outs = refs[:8], refs[8:12], refs[12:18]
    weight_ref = refs[18]
    normed_ref, q_ref, kv_ref, norm_ref, row_ref, gain_ref = outs
    me = place_ref[0]
    rows = parts[0].shape[1]
    for part, mask in zip(parts, PARTS, strict=True):
        for s in range(NH):
            owner = ((me ^ mask) & (Y | CORE)) | s
            weight_ref[pl.ds(pl.multiple_of(owner * rows, rows), rows), :] = part[s]
    for i in range(weight_ref.shape[0] // 128):
        chunk = slice(i * 128, (i + 1) * 128)
        gain_ref[:, chunk] = weight_ref[chunk, 2 * DH :].astype(F32).T[0:8, :]
    weight = weight_ref[:, : 2 * DH]
    gain = gain_ref[0:1, :]
    for i, block in enumerate(blocks):
        rows = pl.ds(i * block.shape[0], block.shape[0])
        normed = (normalised(block[...].astype(F32))[0] * gain).astype(BF16)
        normed_ref[rows, :] = normed
        both = dot(normed, weight)
        queries = both[:, :DH].astype(BF16)
        q_ref[rows, :] = queries
        query_f = queries.astype(F32)
        squares = jnp.sum(query_f * query_f, axis=-1, keepdims=True)
        keys = (query_f * lax.rsqrt(squares / DH + 1e-06) * DH ** (-0.5)).astype(BF16)
        kv_ref[rows, :] = jnp.concatenate([keys, both[:, DH:].astype(BF16)], axis=1)
        norm_ref[rows, :] = jnp.sqrt(squares + 1e-06) * LOG2E
    to_row(norm_ref, row_ref)


def pair_count(one, other, neighbour, diagonal):
    high = jnp.int32(HIGH_BITS)
    match = ((high - (one ^ other)) | (high - (one ^ neighbour))) & high
    counts = lax.population_count(match)
    if diagonal is not None:
        across = lax.broadcasted_iota(I32, counts.shape, 0) - lax.broadcasted_iota(
            I32, counts.shape, 1
        )
        counts = jnp.where(across == diagonal, 0, counts)
    return counts.astype(F32)


def forward_kernel(*refs, tile, parts, own, last):
    q_ref, n_ref, qid_ref, kid_ref = refs[:4]
    kv_refs = refs[4 : 4 + parts]
    acc_in = None if own else refs[4 + parts]
    place_ref = refs[5 + parts] if last else None
    acc_ref = refs[-2] if last else refs[-1]
    step = pl.program_id(0)
    steps = pl.num_programs(0) // parts

    @pl.when(step == 0)
    def _():
        acc_ref[...] = jnp.zeros_like(acc_ref) if own else acc_in[...]

    def part(kv_ref, diagonal_at):
        count = kv_ref.shape[0]
        keys = kv_ref[:, :DH]
        values = jnp.concatenate([kv_ref[:, DH:], jnp.ones((count, DH), BF16)], axis=1)
        for i in range(q_ref.shape[0] // tile):
            rows = slice(i * tile, (i + 1) * tile)
            scores = dot(q_ref[rows, :], keys, NT)
            powers = jnp.exp2(scores * LOG2E - n_ref[rows, :])
            diagonal = None if diagonal_at is None else diagonal_at * count - i * tile
            counts = pair_count(qid_ref[rows, :], kid_ref[0:1, :], kid_ref[2:3, :], diagonal)
            acc_ref[rows, :] += dot((powers * counts).astype(BF16), values)

    for number, kv_ref in enumerate(kv_refs):

        @pl.when(step // steps == number)
        def _(kv_ref=kv_ref, diagonal_at=step if own and number == 0 else None):
            part(kv_ref, diagonal_at)

    if last:
        send_ref = refs[-1]
        rows = send_ref.shape[1]

        @pl.when(step == parts * steps - 1)
        def _():
            for j in range(NH):
                block = acc_ref[j * rows : (j + 1) * rows, :]
                send_ref[place_ref[1] ^ j] = (block[:, :DH] / block[:, DH:]).astype(BF16)


def forward_call(queries, norms, ids, kvs, part, acc, place=None, tk=768, tile=256):
    nq, nk = queries.shape[0], kvs[0].shape[0]
    steps = nk // tk
    column = pl.BlockSpec((nq, 1), lambda j: (0, 0))
    full = pl.BlockSpec((nq, DH), lambda j: (0, 0))
    keyed = [
        pl.BlockSpec((tk, 2 * DH), lambda j, n=n: (jnp.clip(j - n * steps, 0, steps - 1), 0))
        for n in range(len(kvs))
    ]
    wide = pl.BlockSpec((nq, 2 * DH), lambda j: (0, 0))
    listed = pl.BlockSpec((8, tk), lambda j: (0, part * steps + j))
    inputs = [queries, norms, ids[0], ids[1], *kvs]
    specs = [full, column, column, listed, *keyed]
    out_shape, out_specs = [shaped(nq, 2 * DH, dtype=F32)], [wide]
    if acc is not None:
        inputs.append(acc)
        specs.append(wide)
    if place is not None:
        inputs.append(place)
        specs.append(SMEM)
        out_shape.append(shaped(NH, nq // NH, DH))
        out_specs.append(pl.BlockSpec((NH, nq // NH, DH), lambda j: (0, 0, 0)))
    return pl.pallas_call(
        functools.partial(
            forward_kernel, tile=tile, parts=len(kvs), own=acc is None, last=place is not None
        ),
        grid=(len(kvs) * steps,),
        in_specs=specs,
        out_specs=out_specs,
        out_shape=out_shape,
        input_output_aliases={} if acc is None else {4 + len(kvs): 0},
        compiler_params=pltpu.CompilerParams(vmem_limit_bytes=56 * 2**20),
        name="attention_forward",
    )(*inputs)


def backward_kernel(*refs, tile, own):
    q_ref, g_ref, n_ref, t_ref, qid_ref, kid_ref = refs[:6]
    kv_refs = refs[6:8]
    dq_ref, *dkv_refs = refs[-3:]
    step = pl.program_id(0)
    steps = pl.num_programs(0) // 2

    @pl.when(step == 0)
    def _():
        dq_ref[...] = refs[8][...] if own else jnp.zeros_like(dq_ref)

    def part(kv_ref, dkv_ref, diagonal_at):
        keys, values, key_ids = kv_ref[:, :DH], kv_ref[:, DH:], kid_ref[...]
        count = keys.shape[0]
        wide_keys = jnp.concatenate([keys, jnp.ones(keys.shape, BF16)], axis=1)
        grad_keys = jnp.zeros(keys.shape, F32)
        grad_values = jnp.zeros(keys.shape, F32)
        for i in range(q_ref.shape[0] // tile):
            rows = slice(i * tile, (i + 1) * tile)
            queries, grads = q_ref[rows, :], g_ref[rows, :]
            scores = dot(keys, queries, NT)
            powers = jnp.exp2(scores * LOG2E - n_ref[0:1, rows])
            diagonal = None if diagonal_at is None else i * tile - diagonal_at * count
            counts = pair_count(key_ids, qid_ref[0:1, rows], qid_ref[1:2, rows], diagonal)
            weights = powers * counts
            grad_weights = dot(values, grads, NT)
            grad_scores = (weights * (grad_weights + t_ref[0:1, rows])).astype(BF16)
            grad_values = grad_values + dot(weights.astype(BF16), grads)
            grad_keys = grad_keys + dot(grad_scores, queries)
            dq_ref[rows, :] += dot(grad_scores, wide_keys, TN)
        dkv_ref[...] = jnp.concatenate([grad_keys, grad_values], axis=1).astype(BF16)

    @pl.when(step < steps)
    def _():
        part(kv_refs[0], dkv_refs[0], step if own else None)

    @pl.when(step >= steps)
    def _():
        part(kv_refs[1], dkv_refs[1], None)


def backward_call(queries, grads, norms, terms, ids, kv_pair, part, acc, tk=768, tile=256):
    nq, nk = queries.shape[0], kv_pair[0].shape[0]
    steps = nk // tk
    full = pl.BlockSpec((nq, DH), lambda j: (0, 0))
    row = pl.BlockSpec((8, nq), lambda j: (0, 0))
    first = pl.BlockSpec((tk, 2 * DH), lambda j: (jnp.minimum(j, steps - 1), 0))
    second = pl.BlockSpec((tk, 2 * DH), lambda j: (jnp.maximum(j - steps, 0), 0))
    wide = pl.BlockSpec((nq, 2 * DH), lambda j: (0, 0))
    listed = pl.BlockSpec((tk, 1), lambda j: (part * steps + j, 0))
    more = [] if acc is None else [acc]
    return pl.pallas_call(
        functools.partial(backward_kernel, tile=tile, own=acc is not None),
        grid=(2 * steps,),
        in_specs=[full, full, row, row, row, listed, first, second] + [wide] * len(more),
        out_specs=[wide, first, second],
        out_shape=[shaped(nq, 2 * DH, dtype=F32), *[shaped(nk, 2 * DH)] * 2],
        input_output_aliases={8: 0} if more else {},
        compiler_params=pltpu.CompilerParams(vmem_limit_bytes=56 * 2**20),
        cost_estimate=LONG,
        name="attention_backward",
    )(queries, grads, norms, terms, ids[1], ids[0], *kv_pair, *more)


def out_kernel(place_ref, attn_ref, half_ref, gain_ref, *refs):
    parts, (low_ref, out_ref, normed_ref, weight_ref) = refs[:8], refs[8:]
    rows, width = weight_ref.shape[0] // 32, weight_ref.shape[1]
    masks = [core | near for core in (0, CORE) for near in (0, X, Y, X | Y)]
    for part, mask in zip(parts, masks, strict=True):
        for p in range(4):
            start = pl.multiple_of((((place_ref[0] ^ mask) & (Y | CORE | X)) | (p * Z_LO)) * rows, rows)
            weight_ref[pl.ds(start, rows // 2), :] = part[p, :, :width]
            middle = pl.multiple_of(start + rows // 2, rows // 2)
            weight_ref[pl.ds(middle, rows // 2), :] = part[p, :, width:]
    attn = jnp.concatenate([attn_ref[h] for h in range(NH)], axis=1)
    first_out = half_ref[...].astype(F32) + dot(attn, weight_ref[...])
    out_ref[...] = first_out
    low_ref[...] = first_out.astype(BF16)
    normed_ref[...] = (normalised(first_out)[0] * gain_ref[1:2, :]).astype(BF16)


def ffn_part(z_ref, units, down):
    width = z_ref.shape[2] // 2
    lanes = slice(width, None) if down else slice(width)
    return jnp.concatenate([z_ref[p, :units, lanes] for p in range(4)], axis=0)


def hidden_back_kernel(*refs):
    blocks, z_ref, out_ref = refs[:8], refs[8], refs[9]
    down = ffn_part(z_ref, out_ref.shape[1] // 4, True)
    for i, block in enumerate(blocks):
        rows = pl.ds(i * block.shape[0], block.shape[0])
        out_ref[rows, :] = dot(block[...], down, NT)


def ffn_kernel(*refs):
    blocks, back_ref, z_ref, outs = refs[:8], refs[8], refs[9], refs[10:]
    hidden_ref, grad_ref = outs[8:]
    up = ffn_part(z_ref, hidden_ref.shape[1] // 4, False)
    slope = 0.7978845608028654
    for i in (4, 5, 6, 7, 0, 1, 2, 3):
        block = blocks[i]
        rows = pl.ds(i * block.shape[0], block.shape[0])
        v = dot(block[...], up, NT)
        square = v * v
        t = jnp.tanh(slope * v * (1.0 + 0.044715 * square))
        half = 0.5 * (1.0 + t)
        hidden_ref[rows, :] = (v * half).astype(BF16)
        back = half + 0.5 * v * (1.0 - t * t) * slope * (1.0 + 3 * 0.044715 * square)
        grad = (back_ref[rows, :] * back).astype(BF16)
        grad_ref[rows, :] = grad
        outs[i][...] = dot(grad, up).astype(BF16)


def ffn_rest_kernel(*refs):
    blocks, grads, z_ref = refs[:8], refs[8:16], refs[18]
    hidden_ref, grad_ref = refs[16:18]
    near_ref, far_ref, sum_ref = refs[19:]
    width = sum_ref.shape[1] // 2
    units = sum_ref.shape[0] // 4
    down = ffn_part(z_ref, units, True)
    for i in range(8):
        rows = pl.ds(i * blocks[i].shape[0], blocks[i].shape[0])
        out = (near_ref, far_ref)[i // 4]
        out[i % 4] = dot(hidden_ref[rows, :], down).astype(BF16)
    inputs = jnp.concatenate([block[...] for block in blocks], axis=0)
    sum_ref[:, :width] = dot(grad_ref[...], inputs, TN).astype(BF16)
    cotangents = jnp.concatenate([block[...] for block in grads], axis=0)
    sum_ref[:, width:] = dot(hidden_ref[...], cotangents, TN).astype(BF16)


def mid_kernel(*refs):
    parts, rest, outs = refs[:5], refs[5:9], refs[9:]
    out_ref, first_ref, gain_ref, weight_ref = rest
    mid_ref, send_ref, gain_sum_ref = outs
    xhat, rstd = normalised(out_ref[...])
    grads = sum(part[...].astype(F32) for part in parts)
    gain_sum_ref[...] = jnp.broadcast_to(
        jnp.sum(grads * xhat, axis=0, keepdims=True), gain_sum_ref.shape
    )
    mid = first_ref[...].astype(F32) + norm_back(grads * gain_ref[1:2, :], xhat, rstd)
    mid = mid.astype(BF16)
    mid_ref[...] = mid
    grad_attn = dot(mid, weight_ref[...], NT).astype(BF16)
    for h in range(NH):
        send_ref[h] = grad_attn[:, h * DH : (h + 1) * DH]


def turn_kernel(place_ref, arrived_ref, acc_ref, grads_ref, row_ref, column_ref):
    rows = arrived_ref.shape[1]
    for j in range(NH):
        place = slice(j * rows, (j + 1) * rows)
        block = acc_ref[place, :]
        totals = block[:, DH:]
        attended = block[:, :DH] / totals
        grad_attn = arrived_ref[place_ref[1] ^ j].astype(F32)
        grads_ref[place, :] = (grad_attn / totals).astype(BF16)
        column_ref[place, :] = (
            -jnp.sum(grad_attn * attended, axis=-1, keepdims=True) / totals[:, :1]
        )
    to_row(column_ref, row_ref)


def grad_out_kernel(place_ref, attn_ref, mid_ref, gain_ref, keep_ref, send_ref):
    width = mid_ref.shape[1]
    heads = NH // 4
    core = (place_ref[0] >> 3) & 1
    gains = [
        jnp.broadcast_to(gain_ref[0:1, h * DH : (h + 1) * DH], (DH, DH)).T for h in range(NH)
    ]
    for ref, bit in ((keep_ref, core), (send_ref, 1 - core)):
        for i in range(NH // 2):
            first, k = divmod(i, heads)
            rows = slice(i * DH, (i + 1) * DH)
            attn = attn_ref[(2 * first + bit) * heads + k]
            ref[rows, :width] = dot(attn, mid_ref[...], TN).astype(BF16)
            low, high = (gains[(2 * first + b) * heads + k] for b in range(2))
            ref[rows, width:] = jnp.where(bit == 0, low, high).astype(BF16)


def halve_kernel(place_ref, kept_ref, came_ref, keep_ref, send_ref, *, shift, blocks):
    rows = kept_ref.shape[0] // (2 * blocks)
    bit = (place_ref[0] >> shift) & 1
    for i in range(blocks):
        out = slice(i * rows, (i + 1) * rows)
        for ref, half in ((keep_ref, bit), (send_ref, 1 - bit)):
            start = pl.ds(pl.multiple_of((2 * i + half) * rows, rows), rows)
            total = kept_ref[start, :].astype(F32) + came_ref[start, :].astype(F32)
            ref[out, :] = total.astype(BF16)


def gather_grads_kernel(place_ref, direct_ref, q_ref, n_ref, *refs):
    kv_refs, (send_ref, both_ref) = refs[:3], refs[3:]
    rows = send_ref.shape[1]
    for j in range(NH):
        place = slice(j * rows, (j + 1) * rows)
        grad_kv = sum(ref[place, :].astype(F32) for ref in kv_refs)
        grad_keys, grad_values = grad_kv[:, :DH], grad_kv[:, DH:]
        queries = q_ref[place, :].astype(F32)
        inverse = lax.rsqrt(jnp.mean(queries * queries, axis=-1, keepdims=True) + 1e-06)
        mean_part = jnp.mean(grad_keys * queries, axis=-1, keepdims=True)
        grad_norms = -direct_ref[place, DH:]
        grad_queries = (
            direct_ref[place, :DH]
            + grad_norms * queries * (LOG2E / n_ref[place, :])
            + (inverse * DH ** (-0.5)) * (grad_keys - queries * (inverse * inverse * mean_part))
        )
        both = jnp.concatenate([grad_queries.astype(BF16), grad_values.astype(BF16)], axis=1)
        both_ref[place, :] = both
        send_ref[place_ref[1] ^ j] = both


def project_back_kernel(place_ref, normed_ref, both_ref, *refs):
    outs, sum_ref = refs[:4], refs[4]
    sum_ref[...] = dot(normed_ref[...], both_ref[...], TN)
    rows = outs[0].shape[1]
    for out, mask in zip(outs, PARTS, strict=True):
        for j in range(NH):
            start = pl.multiple_of((place_ref[0] ^ mask ^ j) * rows, rows)
            out[j] = sum_ref[pl.ds(start, rows), :].astype(BF16)


def sum_kernel(place_ref, *refs):
    parts, out = refs[:4], refs[4]
    for j in range(NH):
        out[place_ref[1] ^ j] = sum(part[j].astype(F32) for part in parts).astype(BF16)


def own_rows_kernel(rows_ref, qk_ref, value_ref, gain_ref, *outs):
    grad_qk_ref, grad_value_ref, grad_gain_ref = outs
    for h in range(NH):
        lanes = slice(h * DH, (h + 1) * DH)
        grad_qk_ref[:, lanes] = rows_ref[h, :, :DH].astype(F32)
        grad_value_ref[:, lanes] = rows_ref[h, :, DH:].astype(F32)
    total = jnp.sum(
        qk_ref[...].astype(F32) * grad_qk_ref[...]
        + value_ref[...].astype(F32) * grad_value_ref[...],
        axis=-1,
        keepdims=True,
    )
    grad_gain_ref[...] = jnp.broadcast_to(
        total / gain_ref[:, :1].astype(F32), grad_gain_ref.shape
    )


def unpack_kernel(sum_ref, up_ref, down_ref):
    width = sum_ref.shape[1] // 2
    up_ref[...] = sum_ref[:, :width].astype(F32).T
    down_ref[...] = sum_ref[:, width:].astype(F32)


def last_kernel(arrived_ref, half_ref, grad_ref, gain_ref, weight_ref, out_ref):
    width = half_ref.shape[1]
    grad_q = jnp.concatenate([arrived_ref[h][:, :DH] for h in range(NH)], axis=1)
    grad_v = jnp.concatenate([arrived_ref[h][:, DH:] for h in range(NH)], axis=1)
    grads = dot(grad_q, weight_ref[:, :width], NT) + dot(grad_v, weight_ref[:, width:], NT)
    xhat, rstd = normalised(half_ref[...].astype(F32))
    out_ref[...] = (
        grad_ref[...].astype(F32) + norm_back(grads * gain_ref[0:1, :], xhat, rstd)
    ).astype(BF16)


def cube_plan(
    first_half,
    second_half,
    grad_first,
    grad_second,
    qk_weight,
    value_weight,
    out_weight,
    attn_gain,
    ffn_gain,
    up_weight,
    down_weight,
    stretch_ids,
):
    y, core, z_hi, z_lo, x = (lax.axis_index(name) for name in BITS)
    me = y * 16 + core * 8 + z_hi * 4 + z_lo * 2 + x
    place = jnp.stack([me, me & 7]).astype(I32)
    rows, width = first_half.shape
    wide_rows = rows * 8
    own_rows = qk_weight.shape[0]
    own_units = down_weight.shape[0]
    units = own_units * 4
    rounds, tokens = stretch_ids.shape
    nchunk = tokens // STRETCH
    row_block = shaped(rows, width)
    acc_shape = shaped(rows, width, dtype=F32)

    blocks = gather_zx(second_half)
    gains = jnp.pad(jnp.stack([attn_gain, ffn_gain], axis=1), ((0, 0), (0, DH - 2)))
    columns, z_rows, qv_rows = call(
        pack_kernel,
        [Far(a) for a in (qk_weight, value_weight, out_weight, up_weight, down_weight, gains)],
        [
            shaped(NH, own_rows, 3 * DH),
            shaped(own_units + own_rows // 2, 2 * width),
            shaped(own_rows, 2 * width),
        ],
        "pack",
        cost=None,
        far_out=(1, 2),
    )
    columns = shares(lax.all_to_all(columns, HEAD_AXES, 0, 0, tiled=True))
    weights = lax.all_gather(after(z_rows, blocks[4]), ("z_hi", "z_lo"), axis=0)
    cotangent_y = swap(grad_second, Y)

    ids = stretch_ids.reshape(rounds, 2, 2, 2, 2, 2, rows)
    for axis, bit in enumerate((y, core, z_hi, z_lo, x), 1):
        ids = jnp.where(bit == 1, jnp.flip(ids, axis), ids)
    ids = ids.reshape(rounds, tokens)

    def packed(numbers):
        return sum(numbers[r] << (8 * r) for r in range(rounds))

    ids_row = packed(ids)
    ids_rows = jnp.concatenate(
        [
            ids_row[None],
            packed((ids + nchunk - 1) % nchunk)[None],
            packed((ids + 1) % nchunk)[None],
            jnp.zeros((5, tokens), I32),
        ]
    )
    ids_column = call(
        column_kernel, [Far(ids_rows)], [shaped(tokens, 1, dtype=I32)], "ids", far_out=(0,), cost=None
    )[0]
    ids_both = (ids_column, ids_rows)

    columns[0] = after(columns[0], *ids_both, cotangent_y)
    normed, queries, kv, norms, norm_row, gain_rows = call(
        project_kernel,
        [Far(blocks[0]), *blocks[1:], *columns],
        [
            shaped(wide_rows, width),
            shaped(wide_rows, DH),
            shaped(wide_rows, 2 * DH),
            shaped(wide_rows, 1, dtype=F32),
            shaped(8, wide_rows, dtype=F32),
            shaped(8, width, dtype=F32),
        ],
        "project",
        cost=None,
        far_out=range(6),
        scalars=[place],
        scratch=[pltpu.VMEM((width, 3 * DH), BF16)],
    )
    kv_parts = shares(kv)
    near, near_y = after(grad_second, kv), after(cotangent_y, kv)
    cotangents = [near, swap(near, X), near_y, swap(near_y, X)]
    acc, = forward_call(queries, norms, ids_both, kv_parts[:2], 0, None)
    kv_parts[2] = after(kv_parts[2], acc, *cotangents)
    kv_parts[3] = swap(kv_parts[2], CORE)
    qv_full = lax.all_gather(after(qv_rows, kv_parts[2]), BITS, axis=0, tiled=True)
    acc, = forward_call(queries, norms, ids_both, kv_parts[2:3], 2, acc)
    out_near = near_xy(after(weights, acc)[:, own_units:])
    acc, attn_send = forward_call(queries, norms, ids_both, kv_parts[3:], 3, acc, place)
    out_parts = with_cores([after(a, attn_send) for a in out_near])
    cotangents = with_cores([after(a, attn_send) for a in cotangents])
    attn_tok = lax.all_to_all(attn_send, HEAD_AXES, 0, 0, tiled=True)
    units = own_units * 4
    hidden_back = call(
        hidden_back_kernel,
        [*map(Far, cotangents), Far(weights)],
        [shaped(wide_rows, units, dtype=F32)],
        "hidden_back",
        cost=None,
        far_out=(0,),
    )[0]
    attn_tok = after(attn_tok, hidden_back)
    y_first, first_out, normed_ffn, out_full = call(
        out_kernel,
        [attn_tok, Far(first_half), Far(gain_rows), *out_parts],
        [row_block, acc_shape, row_block, shaped(width, width)],
        "project_out",
        cost=None,
        far_out=(0, 1, 3),
        scalars=[place],
    )
    ffn_in = gather_xy(normed_ffn)
    *grad_blocks, hidden, grad_pre = call(
        ffn_kernel,
        [*ffn_in, Far(hidden_back), Far(weights)],
        [row_block] * 8 + [shaped(wide_rows, units)] * 2,
        "feed_forward",
        cost=None,
        mib=44,
    )
    grad_parts = scatter_xy(grad_blocks)
    ffn_near, ffn_far, grad_ffn = call(
        ffn_rest_kernel,
        [*ffn_in, *map(Far, cotangents), hidden, grad_pre, Far(weights)],
        [shaped(4, rows, width)] * 2 + [shaped(units, 2 * width)],
        "feed_forward_rest",
        cost=None,
        far_out=range(3),
        mib=48,
    )
    grad_mid, grad_attn, gain_sum = call(
        mid_kernel,
        [
            *grad_parts,
            *map(Far, (after(first_out, grad_ffn, qv_full), grad_first, gain_rows, out_full)),
        ],
        [row_block, shaped(NH, rows, DH), shaped(8, width, dtype=F32)],
        "mid",
        cost=None,
        far_out=(0,),
    )

    grad_attn = lax.all_to_all(grad_attn, HEAD_AXES, 0, 0, tiled=True)

    out_width = width + DH
    half = shaped(width // 2, out_width)
    keep, move = call(
        grad_out_kernel,
        [Far(attn_tok), Far(grad_mid), Far(gain_sum)],
        [half, half],
        "grad_out",
        far_out=(0,),
        scalars=[place],
    )

    def halve(keep, came, shift, blocks):
        half = shaped(keep.shape[0] // 2, out_width)
        return call(
            functools.partial(halve_kernel, shift=shift, blocks=blocks),
            [Far(keep), came],
            [half, half],
            "halve",
            far_out=(0,),
            scalars=[place],
        )

    ffn_far = swap(after(ffn_far, grad_mid), CORE)
    keep, move = halve(keep, swap(move, CORE), 4, 1)
    came = swap(move, Y)
    ffn_sum = ffn_near.astype(F32) + ffn_far.astype(F32)
    ffn_move = ffn_sum[1::2].astype(BF16)
    grads, term_row = call(
        turn_kernel,
        [after(grad_attn, move, ffn_move), Far(acc)],
        [shaped(wide_rows, DH), shaped(8, wide_rows, dtype=F32)],
        "turn",
        far_out=(0, 1),
        scalars=[place],
        scratch=[pltpu.VMEM((wide_rows, 1), F32)],
    )

    def backward(part, acc):
        return backward_call(
            queries, grads, norm_row, term_row, ids_both, kv_parts[part : part + 2], part, acc
        )

    grad_ffn = lax.psum_scatter(
        grad_ffn, ("z_hi", "z_lo"), scatter_dimension=0, tiled=True
    )
    direct, over_y, far = backward(2, None)
    far = swap(far, CORE)
    keep, move = halve(keep, after(came, direct), 0, 4)
    over_y = (over_y.astype(F32) + after(far, move).astype(F32)).astype(BF16)
    ffn_move = swap(ffn_move, X)
    direct = after(direct, over_y, ffn_move)
    over_y = swap(over_y, Y)
    came = swap(move, X)
    direct, grad_kv, over_core = backward(0, direct)
    direct = after(direct, grad_ffn)
    over_core = swap(after(over_core, over_y), CORE)

    send, grad_both = call(
        gather_grads_kernel,
        [*map(Far, (direct, queries, norms, grad_kv)), over_core, over_y],
        [shaped(NH, rows, 2 * DH), shaped(wide_rows, 2 * DH)],
        "gather_grads",
        far_out=(1,),
        scalars=[place],
    )
    arrived = lax.all_to_all(send, HEAD_AXES, 0, 0, tiled=True)

    grad_rows = call(
        project_back_kernel,
        [Far(normed), Far(grad_both)],
        [shaped(NH, own_rows, 2 * DH)] * 4,
        "project_back",
        scalars=[place],
        scratch=[pltpu.VMEM((width, 2 * DH), F32)],
    )
    rows_parts = grad_rows
    grad_rows = call(
        sum_kernel,
        sum_shares(grad_rows),
        [shaped(NH, own_rows, 2 * DH)],
        "sum_rows",
        scalars=[place],
    )
    rows_send = grad_rows[0]
    grad_up, grad_down = call(
        unpack_kernel,
        [Far(after(grad_ffn, rows_send))],
        [shaped(width, own_units, dtype=F32), shaped(own_units, width, dtype=F32)],
        "unpack",
        far_out=(0, 1),
    )
    arrived = after(arrived, rows_send, grad_up)
    grad_rows = lax.all_to_all(after(rows_send, arrived), HEAD_AXES, 0, 0, tiled=True)
    grad_second_half = call(
        last_kernel,
        [arrived, *map(Far, (second_half, grad_second, gain_rows, qv_full))],
        [row_block],
        "last",
        far_out=(0,),
    )[0]

    keep, move = halve(keep, after(came, rows_send), 1, 2)
    keep, move = halve(keep, after(swap(move, Z_LO), arrived), 2, 1)
    grad_out = keep.astype(F32) + swap(move, Z_HI).astype(F32)
    ffn_sum = ffn_sum[0::2] + after(ffn_move, rows_send).astype(F32)
    ffn_sum = ffn_sum[0] + after(swap(ffn_sum[1].astype(BF16), Y), arrived).astype(F32)
    second_out = second_half.astype(F32) + ffn_sum
    grad_qk, grad_value, grad_attn_gain = call(
        own_rows_kernel,
        [after(grad_rows, grad_second_half, grad_up), Far(qk_weight), Far(value_weight), Far(gains)],
        [shaped(own_rows, width, dtype=F32)] * 2 + [shaped(own_rows, 128, dtype=F32)],
        "own_rows",
        far_out=(0, 1),
    )

    return (
        y_first,
        second_out.astype(BF16),
        grad_mid,
        grad_second_half,
        grad_qk,
        grad_value,
        grad_out[:, :width],
        grad_attn_gain[:, 0],
        grad_out[:, width],
        grad_up,
        grad_down,
    )


def solution(mesh):
    if dict(mesh.shape) == {"head": 4, "blk": 8}:
        plan, axes = cube_plan, BITS
        mesh = jax.sharding.Mesh(mesh.devices.reshape((2,) * 5), BITS)
    else:
        plan, axes = ring_plan, ("head", "blk")
    by_row, by_column, vector = P(axes, None), P(None, axes), P(axes)
    return jax.shard_map(
        plan,
        mesh=mesh,
        in_specs=(by_row,) * 7 + (vector, vector, by_column, by_row, P()),
        out_specs=(by_row,) * 7 + (vector, vector, by_column, by_row),
        check_vma=False,
    )
```

```python
import functools

import jax
import jax.numpy as jnp
from jax import lax
from jax.experimental import pallas as pl
from jax.experimental.pallas import tpu as pltpu
from jax.sharding import PartitionSpec as P

NH = 8
DH = 128
STRETCH = 64


def shifted(value, axis, by):
    devices = lax.axis_size(axis)
    return lax.ppermute(value, axis, [(i, (i + by) % devices) for i in range(devices)])


def layer_norm(values, gains):
    average = jnp.mean(values, axis=-1, keepdims=True)
    centred = values - average
    variance = jnp.mean(centred * centred, axis=-1, keepdims=True)
    return centred * lax.rsqrt(variance + 1e-05) * gains


def key_norm(queries):
    return (
        queries
        * lax.rsqrt(jnp.mean(queries * queries, axis=-1, keepdims=True) + 1e-06)
        * queries.shape[-1] ** (-0.5)
    )


def row_norm(queries):
    return jnp.sqrt(jnp.sum(queries * queries, axis=-1) + 1e-06)


def group_ids(stretch_ids, heads_count, cycle_count, local_rows, cycle_index):
    shaped = stretch_ids.reshape(stretch_ids.shape[0], heads_count, cycle_count, local_rows)
    picked = lax.dynamic_slice_in_dim(shaped, cycle_index, 1, 2)
    places = (
        jnp.arange(heads_count, dtype=jnp.int32)[:, None] * cycle_count + cycle_index
    ) * local_rows
    places = places + jnp.arange(local_rows, dtype=jnp.int32)[None, :]
    return (picked.reshape(stretch_ids.shape[0], heads_count * local_rows), places.reshape(-1))


def pair_counts(query_ids, query_places, key_ids, key_places, nchunk):
    previous = (query_ids + nchunk - 1) % nchunk
    same_stretch = key_ids[:, None, :] == query_ids[:, :, None]
    before = key_ids[:, None, :] == previous[:, :, None]
    counts = jnp.sum((same_stretch | before).astype(jnp.float32), axis=0)
    return counts * (query_places[:, None] != key_places[None, :]).astype(jnp.float32)


def forward_block(queries, query_norms, counts, key_block, value_block):
    scores = jnp.einsum("qhd,khd->hqk", queries, key_block, preferred_element_type=jnp.float32)
    weights = counts[None] * jnp.exp(scores - query_norms.T[:, :, None])
    summed = jnp.einsum(
        "hqk,khd->qhd",
        weights.astype(jnp.bfloat16),
        value_block,
        preferred_element_type=jnp.float32,
    )
    return (jnp.sum(weights, axis=-1), summed)


def backward_block(queries, query_norms, counts, key_block, value_block, grad_summed, grad_totals):
    scores = jnp.einsum("qhd,khd->hqk", queries, key_block, preferred_element_type=jnp.float32)
    weights = counts[None] * jnp.exp(scores - query_norms.T[:, :, None])
    grad_weights = jnp.einsum(
        "qhd,khd->hqk", grad_summed, value_block, preferred_element_type=jnp.float32
    )
    grad_scores_f = weights * (grad_weights + grad_totals[:, :, None])
    grad_scores = grad_scores_f.astype(jnp.bfloat16)
    grad_norms = -jnp.sum(grad_scores_f, axis=-1)
    grad_values = jnp.einsum(
        "hqk,qhd->khd",
        weights.astype(jnp.bfloat16),
        grad_summed,
        preferred_element_type=jnp.float32,
    )
    grad_direct = jnp.einsum(
        "hqk,khd->qhd", grad_scores, key_block, preferred_element_type=jnp.float32
    )
    grad_keys = jnp.einsum("hqk,qhd->khd", grad_scores, queries, preferred_element_type=jnp.float32)
    return (grad_norms, grad_direct, grad_keys, grad_values)


def feed_forward(normed_ffn, grad_output, up_part, down_part):
    pre_act = jnp.dot(normed_ffn, up_part, preferred_element_type=jnp.float32)
    hidden_f, gelu_back = jax.vjp(jax.nn.gelu, pre_act)
    hidden = hidden_f.astype(jnp.bfloat16)
    ffn_result = jnp.dot(hidden, down_part, preferred_element_type=jnp.float32)
    grad_hidden = jnp.dot(grad_output, down_part.T, preferred_element_type=jnp.float32)
    grad_pre = gelu_back(grad_hidden)[0].astype(jnp.bfloat16)
    grad_normed = jnp.dot(grad_pre, up_part.T, preferred_element_type=jnp.float32)
    grad_up = jnp.dot(normed_ffn.T, grad_pre, preferred_element_type=jnp.float32)
    grad_down = jnp.dot(hidden.T, grad_output, preferred_element_type=jnp.float32)
    return (ffn_result, grad_normed, grad_up, grad_down)


def ring_plan(
    first_half,
    second_half,
    grad_first,
    grad_second,
    qk_weight,
    value_weight,
    out_weight,
    attn_gain,
    ffn_gain,
    up_weight,
    down_weight,
    stretch_ids,
):
    heads_count = lax.axis_size("head")
    cycle_count = lax.axis_size("blk")
    cycle_index = lax.axis_index("blk")
    local_rows = first_half.shape[0]
    model_width = first_half.shape[1]
    group_rows = local_rows * heads_count
    local_heads = NH // heads_count
    nchunk = stretch_ids.shape[1] // STRETCH
    full_qk, full_value, full_out, full_attn_gain, full_ffn_gain, up_part, down_part = (
        lax.all_gather(qk_weight, ("head", "blk"), axis=0, tiled=True),
        lax.all_gather(value_weight, ("head", "blk"), axis=0, tiled=True),
        lax.all_gather(out_weight, ("head", "blk"), axis=0, tiled=True),
        lax.all_gather(attn_gain, ("head", "blk"), axis=0, tiled=True),
        lax.all_gather(ffn_gain, ("head", "blk"), axis=0, tiled=True),
        lax.all_gather(up_weight, ("head", "blk"), axis=1, tiled=True),
        lax.all_gather(down_weight, ("head", "blk"), axis=0, tiled=True),
    )
    second_f = second_half.astype(jnp.float32)
    normed_f, attn_norm_back = jax.vjp(layer_norm, second_f, full_attn_gain.astype(jnp.float32))
    normed = normed_f.astype(jnp.bfloat16)
    query_tok = jnp.dot(normed, full_qk, preferred_element_type=jnp.float32).astype(jnp.bfloat16)
    value_tok = jnp.dot(normed, full_value, preferred_element_type=jnp.float32).astype(jnp.bfloat16)
    query_heads = query_tok.reshape(local_rows, NH, DH)
    value_heads = value_tok.reshape(local_rows, NH, DH)
    queries, values = (
        lax.all_to_all(query_heads, "head", split_axis=1, concat_axis=0, tiled=True),
        lax.all_to_all(value_heads, "head", split_axis=1, concat_axis=0, tiled=True),
    )
    query_f = queries.astype(jnp.float32)
    key_f, key_back = jax.vjp(key_norm, query_f)
    keys = key_f.astype(jnp.bfloat16)
    query_norms, norm_back = jax.vjp(row_norm, query_f)
    query_ids, query_places = group_ids(
        stretch_ids, heads_count, cycle_count, local_rows, cycle_index
    )

    def counts_for(cycle_step):
        source_index = (cycle_index - cycle_step + cycle_count) % cycle_count
        key_ids, key_places = group_ids(
            stretch_ids, heads_count, cycle_count, local_rows, source_index
        )
        return pair_counts(query_ids, query_places, key_ids, key_places, nchunk)

    def rotate(key_block, value_block):
        return shifted((key_block, value_block), "blk", 1)

    def forward_step(cycle_step, carried):
        key_block, value_block, totals, summed = carried
        part_totals, part_summed = forward_block(
            queries, query_norms, counts_for(cycle_step), key_block, value_block
        )
        key_next, value_next = rotate(key_block, value_block)
        return (key_next, value_next, totals + part_totals, summed + part_summed)

    initial = (
        keys,
        values,
        jnp.zeros((local_heads, group_rows), jnp.float32),
        jnp.zeros((group_rows, local_heads, DH), jnp.float32),
    )
    key_block, value_block, totals, summed = lax.fori_loop(
        0, cycle_count - 1, forward_step, initial
    )
    part_totals, part_summed = forward_block(
        queries, query_norms, counts_for(cycle_count - 1), key_block, value_block
    )
    totals = totals + part_totals
    summed = summed + part_summed
    attended = summed / totals.T[:, :, None]
    attn_tok = lax.all_to_all(
        attended.astype(jnp.bfloat16), "head", split_axis=0, concat_axis=1, tiled=True
    ).reshape(local_rows, model_width)
    first_out = first_half.astype(jnp.float32) + jnp.dot(
        attn_tok, full_out, preferred_element_type=jnp.float32
    )
    normed_ffn_f, ffn_norm_back = jax.vjp(layer_norm, first_out, full_ffn_gain.astype(jnp.float32))
    normed_ffn = normed_ffn_f.astype(jnp.bfloat16)
    ffn_result, grad_normed_ffn, grad_up, grad_down = feed_forward(
        normed_ffn, grad_second, up_part, down_part
    )
    second_out = second_f + ffn_result
    grad_mid_ffn, grad_ffn_gain = ffn_norm_back(grad_normed_ffn)
    grad_mid = grad_first.astype(jnp.float32) + grad_mid_ffn
    grad_mid_low = grad_mid.astype(jnp.bfloat16)
    grad_out = jnp.dot(attn_tok.T, grad_mid_low, preferred_element_type=jnp.float32)
    grad_attn_tok = jnp.dot(grad_mid_low, full_out.T, preferred_element_type=jnp.float32).astype(
        jnp.bfloat16
    )
    grad_attn = lax.all_to_all(
        grad_attn_tok.reshape(local_rows, NH, DH), "head", split_axis=1, concat_axis=0, tiled=True
    )
    grad_attn_f = grad_attn.astype(jnp.float32)
    grad_summed = (grad_attn_f / totals.T[:, :, None]).astype(jnp.bfloat16)
    grad_totals = (-jnp.sum(grad_attn_f * attended, axis=-1) / totals.T).T

    def pass_grads(grad_keys, grad_values):
        return (
            shifted(grad_keys.astype(jnp.bfloat16), "blk", 1).astype(grad_keys.dtype),
            shifted(grad_values.astype(jnp.bfloat16), "blk", 1).astype(grad_values.dtype),
        )

    def backward_step(cycle_step, carried):
        key_block, value_block, grad_keys, grad_values, grad_norms, grad_direct = carried
        pieces = backward_block(
            queries,
            query_norms,
            counts_for(cycle_step),
            key_block,
            value_block,
            grad_summed,
            grad_totals,
        )
        key_next, value_next = rotate(key_block, value_block)
        grad_keys, grad_values = pass_grads(grad_keys + pieces[2], grad_values + pieces[3])
        return (
            key_next,
            value_next,
            grad_keys,
            grad_values,
            grad_norms + pieces[0],
            grad_direct + pieces[1],
        )

    zero_rows = jnp.zeros((group_rows, local_heads, DH), jnp.float32)
    initial = (
        keys,
        values,
        zero_rows,
        zero_rows,
        jnp.zeros((local_heads, group_rows), jnp.float32),
        zero_rows,
    )
    carried = lax.fori_loop(0, cycle_count - 1, backward_step, initial)
    pieces = backward_block(
        queries,
        query_norms,
        counts_for(cycle_count - 1),
        carried[0],
        carried[1],
        grad_summed,
        grad_totals,
    )
    grad_keys, grad_values = pass_grads(carried[2] + pieces[2], carried[3] + pieces[3])
    grad_norms = carried[4] + pieces[0]
    grad_direct = carried[5] + pieces[1]
    grad_queries = grad_direct + norm_back(grad_norms.T)[0] + key_back(grad_keys)[0]
    grad_q_tok, grad_v_tok = (
        lax.all_to_all(
            grad_queries.astype(jnp.bfloat16), "head", split_axis=0, concat_axis=1, tiled=True
        ),
        lax.all_to_all(
            grad_values.astype(jnp.bfloat16), "head", split_axis=0, concat_axis=1, tiled=True
        ),
    )
    grad_q_tok = grad_q_tok.reshape(local_rows, model_width)
    grad_v_tok = grad_v_tok.reshape(local_rows, model_width)
    grad_normed = jnp.dot(grad_q_tok, full_qk.T, preferred_element_type=jnp.float32) + jnp.dot(
        grad_v_tok, full_value.T, preferred_element_type=jnp.float32
    )
    grad_qk = jnp.dot(normed.T, grad_q_tok, preferred_element_type=jnp.float32)
    grad_value = jnp.dot(normed.T, grad_v_tok, preferred_element_type=jnp.float32)
    grad_second_attn, grad_attn_gain = attn_norm_back(grad_normed)
    grad_second_total = grad_second.astype(jnp.float32) + grad_second_attn
    sum_qk, sum_value, sum_out, sum_attn_gain, sum_ffn_gain, sum_up, sum_down = (
        lax.psum_scatter(grad_qk, ("head", "blk"), scatter_dimension=0, tiled=True),
        lax.psum_scatter(grad_value, ("head", "blk"), scatter_dimension=0, tiled=True),
        lax.psum_scatter(grad_out, ("head", "blk"), scatter_dimension=0, tiled=True),
        lax.psum_scatter(grad_attn_gain, ("head", "blk"), scatter_dimension=0, tiled=True),
        lax.psum_scatter(grad_ffn_gain, ("head", "blk"), scatter_dimension=0, tiled=True),
        lax.psum_scatter(grad_up, ("head", "blk"), scatter_dimension=1, tiled=True),
        lax.psum_scatter(grad_down, ("head", "blk"), scatter_dimension=0, tiled=True),
    )
    return (
        first_out.astype(jnp.bfloat16),
        second_out.astype(jnp.bfloat16),
        grad_mid.astype(jnp.bfloat16),
        grad_second_total.astype(jnp.bfloat16),
        sum_qk,
        sum_value,
        sum_out,
        sum_attn_gain,
        sum_ffn_gain,
        sum_up,
        sum_down,
    )


BITS = ("y", "core", "z_hi", "z_lo", "x")
Y, CORE, Z_HI, Z_LO, X = 16, 8, 4, 2, 1
HEAD_AXES = ("z_hi", "z_lo", "x")
PARTS = (0, CORE, Y, Y | CORE)
LOG2E = 1.4426950408889634
HIGH_BITS = -2139062144
NT = (((1,), (1,)), ((), ()))
NN = (((1,), (0,)), ((), ()))
TN = (((0,), (0,)), ((), ()))
F32, BF16, I32 = jnp.float32, jnp.bfloat16, jnp.int32
LONG = pl.CostEstimate(flops=10**11, bytes_accessed=1, transcendentals=0)
SMEM = pl.BlockSpec(memory_space=pltpu.SMEM)


def dot(left, right, dims=NN):
    return lax.dot_general(left, right, dims, preferred_element_type=F32)


def swap(value, mask):
    return lax.ppermute(value, BITS, [(i, i ^ mask) for i in range(32)])


def after(value, *others):
    return lax.optimization_barrier((value, *others))[0]


def shaped(*shape, dtype=BF16):
    return jax.ShapeDtypeStruct(shape, dtype)


class Far:
    def __init__(self, value):
        self.value = value


def call(kernel, inputs, out_shape, name, far_out=(), mib=62, scalars=(), scratch=(), cost=LONG):
    far_in = [i for i, a in enumerate(inputs) if isinstance(a, Far)]
    arrays = [a.value if isinstance(a, Far) else a for a in inputs]
    first_in, first_out = len(scalars), len(scalars) + len(arrays)
    first_scratch = first_out + len(out_shape)
    staged = [arrays[i] for i in far_in] + [out_shape[i] for i in far_out]

    def body(*refs):
        refs, sems = list(refs[:-1]), refs[-1]
        own = refs[first_scratch : first_scratch + len(scratch)]
        stages = refs[first_scratch + len(scratch) :]
        copies = []
        for k, i in enumerate(far_in):
            copies.append(pltpu.make_async_copy(refs[first_in + i], stages[k], sems.at[k]))
            refs[first_in + i] = stages[k]
        for copy in copies:
            copy.start()
        for copy in copies:
            copy.wait()
        copies = []
        for k, i in enumerate(far_out, len(far_in)):
            copies.append(pltpu.make_async_copy(stages[k], refs[first_out + i], sems.at[k]))
            refs[first_out + i] = stages[k]
        kernel(*refs[:first_scratch], *own)
        for copy in copies:
            copy.start()
        for copy in copies:
            copy.wait()

    near, far = pl.BlockSpec(memory_space=pltpu.VMEM), pl.BlockSpec(memory_space=pl.ANY)
    return pl.pallas_call(
        body,
        in_specs=[SMEM] * len(scalars) + [far if i in far_in else near for i in range(len(arrays))],
        out_specs=[far if i in far_out else near for i in range(len(out_shape))],
        out_shape=out_shape,
        scratch_shapes=[
            *scratch,
            *(pltpu.VMEM(a.shape, a.dtype) for a in staged),
            pltpu.SemaphoreType.DMA((max(len(staged), 1),)),
        ],
        compiler_params=pltpu.CompilerParams(vmem_limit_bytes=mib * 2**20),
        cost_estimate=cost,
        name=name,
    )(*scalars, *arrays)


def with_cores(near):
    return near + [swap(part, CORE) for part in near]


def near_xy(value):
    return [value, swap(value, X), swap(value, Y), swap(value, X | Y)]


def gather_xy(value):
    return with_cores(near_xy(value))


def gather_zx(value):
    low, high = swap(value, Z_LO), swap(value, Z_HI)
    both = swap(high, Z_LO)
    beside_low = swap(low, X)
    beside_high = swap(after(high, beside_low), X)
    beside_both = swap(after(both, beside_high), X)
    return [value, swap(value, X), low, beside_low, high, beside_high, both, beside_both]


def scatter_xy(blocks):
    arrived = [swap(block, CORE) for block in blocks[4:]]
    sums = [
        (near.astype(F32) + far.astype(F32)).astype(BF16)
        for near, far in zip(blocks[1:4], arrived[1:], strict=True)
    ]
    sent = [swap(part, mask) for part, mask in zip(sums, (X, Y, X | Y), strict=True)]
    return [blocks[0], arrived[0], *sent]


def scatter_by_x(blocks):
    arrived = [swap(block, CORE) for block in blocks[4:]]
    own, one, two, both = (
        near.astype(F32) + far.astype(F32) for near, far in zip(blocks[:4], arrived, strict=True)
    )
    own = own + swap(one.astype(BF16), X).astype(F32)
    two = two + swap(both.astype(BF16), X).astype(F32)
    return own + swap(two.astype(BF16), Y).astype(F32)


def shares(value):
    over_y = swap(value, Y)
    return [value, swap(value, CORE), over_y, swap(over_y, CORE)]


def sum_shares(blocks):
    return [blocks[0]] + [swap(b, mask) for b, mask in zip(blocks[1:], PARTS[1:], strict=True)]


def normalised(values):
    centred = values - jnp.mean(values, axis=-1, keepdims=True)
    rstd = lax.rsqrt(jnp.mean(centred * centred, axis=-1, keepdims=True) + 1e-05)
    return centred * rstd, rstd


def norm_back(scaled_grads, xhat, rstd):
    return rstd * (
        scaled_grads
        - jnp.mean(scaled_grads, axis=-1, keepdims=True)
        - xhat * jnp.mean(scaled_grads * xhat, axis=-1, keepdims=True)
    )


def to_row(column_ref, row_ref):
    for i in range(row_ref.shape[1] // 128):
        chunk = slice(i * 128, (i + 1) * 128)
        square = jnp.broadcast_to(column_ref[chunk, :], (128, 128))
        row_ref[:, chunk] = square.T[0:8, :]


def pack_kernel(*refs):
    qk_ref, value_ref, out_ref, up_ref, down_ref, gain_ref, columns_ref, z_ref, qv_ref = refs
    rows, width = qk_ref.shape
    units = down_ref.shape[0]
    for h in range(NH):
        lanes = slice(h * DH, (h + 1) * DH)
        columns_ref[h, :, :DH] = qk_ref[:, lanes]
        columns_ref[h, :, DH : 2 * DH] = value_ref[:, lanes]
        columns_ref[h, :, 2 * DH :] = gain_ref[...]
    z_ref[:units, :width] = up_ref[...].astype(F32).T.astype(BF16)
    z_ref[:units, width:] = down_ref[...]
    z_ref[units:, :width] = out_ref[: rows // 2, :]
    z_ref[units:, width:] = out_ref[rows // 2 :, :]
    qv_ref[:, :width] = qk_ref[...]
    qv_ref[:, width:] = value_ref[...]


def column_kernel(row_ref, column_ref):
    for i in range(row_ref.shape[1] // 128):
        chunk = slice(i * 128, (i + 1) * 128)
        square = jnp.broadcast_to(row_ref[0:1, chunk], (128, 128))
        column_ref[chunk, :] = square.T[:, 0:1]


def project_kernel(place_ref, *refs):
    blocks, parts, outs = refs[:8], refs[8:12], refs[12:18]
    weight_ref = refs[18]
    normed_ref, q_ref, kv_ref, norm_ref, row_ref, gain_ref = outs
    me = place_ref[0]
    rows = parts[0].shape[1]
    for part, mask in zip(parts, PARTS, strict=True):
        for s in range(NH):
            owner = ((me ^ mask) & (Y | CORE)) | s
            weight_ref[pl.ds(pl.multiple_of(owner * rows, rows), rows), :] = part[s]
    for i in range(weight_ref.shape[0] // 128):
        chunk = slice(i * 128, (i + 1) * 128)
        gain_ref[:, chunk] = weight_ref[chunk, 2 * DH :].astype(F32).T[0:8, :]
    weight = weight_ref[:, : 2 * DH]
    gain = gain_ref[0:1, :]
    for i, block in enumerate(blocks):
        rows = pl.ds(i * block.shape[0], block.shape[0])
        normed = (normalised(block[...].astype(F32))[0] * gain).astype(BF16)
        normed_ref[rows, :] = normed
        both = dot(normed, weight)
        queries = both[:, :DH].astype(BF16)
        q_ref[rows, :] = queries
        query_f = queries.astype(F32)
        squares = jnp.sum(query_f * query_f, axis=-1, keepdims=True)
        keys = (query_f * lax.rsqrt(squares / DH + 1e-06) * DH ** (-0.5)).astype(BF16)
        kv_ref[rows, :] = jnp.concatenate([keys, both[:, DH:].astype(BF16)], axis=1)
        norm_ref[rows, :] = jnp.sqrt(squares + 1e-06) * LOG2E
    to_row(norm_ref, row_ref)


def pair_count(one, other, neighbour, diagonal):
    high = jnp.int32(HIGH_BITS)
    match = ((high - (one ^ other)) | (high - (one ^ neighbour))) & high
    counts = lax.population_count(match)
    if diagonal is not None:
        across = lax.broadcasted_iota(I32, counts.shape, 0) - lax.broadcasted_iota(
            I32, counts.shape, 1
        )
        counts = jnp.where(across == diagonal, 0, counts)
    return counts.astype(F32)


def forward_kernel(*refs, tile, parts, own, last):
    q_ref, n_ref, qid_ref, kid_ref = refs[:4]
    kv_refs = refs[4 : 4 + parts]
    acc_in = None if own else refs[4 + parts]
    place_ref = refs[5 + parts] if last else None
    acc_ref = refs[-2] if last else refs[-1]
    step = pl.program_id(0)
    steps = pl.num_programs(0) // parts

    @pl.when(step == 0)
    def _():
        acc_ref[...] = jnp.zeros_like(acc_ref) if own else acc_in[...]

    def part(kv_ref, diagonal_at):
        count = kv_ref.shape[0]
        keys = kv_ref[:, :DH]
        values = jnp.concatenate([kv_ref[:, DH:], jnp.ones((count, DH), BF16)], axis=1)
        for i in range(q_ref.shape[0] // tile):
            rows = slice(i * tile, (i + 1) * tile)
            scores = dot(q_ref[rows, :], keys, NT)
            powers = jnp.exp2(scores * LOG2E - n_ref[rows, :])
            diagonal = None if diagonal_at is None else diagonal_at * count - i * tile
            counts = pair_count(qid_ref[rows, :], kid_ref[0:1, :], kid_ref[2:3, :], diagonal)
            acc_ref[rows, :] += dot((powers * counts).astype(BF16), values)

    for number, kv_ref in enumerate(kv_refs):

        @pl.when(step // steps == number)
        def _(kv_ref=kv_ref, diagonal_at=step if own and number == 0 else None):
            part(kv_ref, diagonal_at)

    if last:
        send_ref = refs[-1]
        rows = send_ref.shape[1]

        @pl.when(step == parts * steps - 1)
        def _():
            for j in range(NH):
                block = acc_ref[j * rows : (j + 1) * rows, :]
                send_ref[place_ref[1] ^ j] = (block[:, :DH] / block[:, DH:]).astype(BF16)


def forward_call(queries, norms, ids, kvs, part, acc, place=None, tk=768, tile=256):
    nq, nk = queries.shape[0], kvs[0].shape[0]
    steps = nk // tk
    column = pl.BlockSpec((nq, 1), lambda j: (0, 0))
    full = pl.BlockSpec((nq, DH), lambda j: (0, 0))
    keyed = [
        pl.BlockSpec((tk, 2 * DH), lambda j, n=n: (jnp.clip(j - n * steps, 0, steps - 1), 0))
        for n in range(len(kvs))
    ]
    wide = pl.BlockSpec((nq, 2 * DH), lambda j: (0, 0))
    listed = pl.BlockSpec((8, tk), lambda j: (0, part * steps + j))
    inputs = [queries, norms, ids[0], ids[1], *kvs]
    specs = [full, column, column, listed, *keyed]
    out_shape, out_specs = [shaped(nq, 2 * DH, dtype=F32)], [wide]
    if acc is not None:
        inputs.append(acc)
        specs.append(wide)
    if place is not None:
        inputs.append(place)
        specs.append(SMEM)
        out_shape.append(shaped(NH, nq // NH, DH))
        out_specs.append(pl.BlockSpec((NH, nq // NH, DH), lambda j: (0, 0, 0)))
    return pl.pallas_call(
        functools.partial(
            forward_kernel, tile=tile, parts=len(kvs), own=acc is None, last=place is not None
        ),
        grid=(len(kvs) * steps,),
        in_specs=specs,
        out_specs=out_specs,
        out_shape=out_shape,
        input_output_aliases={} if acc is None else {4 + len(kvs): 0},
        compiler_params=pltpu.CompilerParams(vmem_limit_bytes=62 * 2**20),
        name="attention_forward",
    )(*inputs)


def backward_kernel(*refs, tile, own):
    q_ref, g_ref, n_ref, t_ref, qid_ref, kid_ref = refs[:6]
    kv_refs = refs[6:8]
    dq_ref, *dkv_refs = refs[-3:]
    step = pl.program_id(0)
    steps = pl.num_programs(0) // 2

    @pl.when(step == 0)
    def _():
        dq_ref[...] = refs[8][...] if own else jnp.zeros_like(dq_ref)

    def part(kv_ref, dkv_ref, diagonal_at):
        keys, values, key_ids = kv_ref[:, :DH], kv_ref[:, DH:], kid_ref[...]
        count = keys.shape[0]
        wide_keys = jnp.concatenate([keys, jnp.ones(keys.shape, BF16)], axis=1)
        grad_keys = jnp.zeros(keys.shape, F32)
        grad_values = jnp.zeros(keys.shape, F32)
        for i in range(q_ref.shape[0] // tile):
            rows = slice(i * tile, (i + 1) * tile)
            queries, grads = q_ref[rows, :], g_ref[rows, :]
            scores = dot(keys, queries, NT)
            powers = jnp.exp2(scores * LOG2E - n_ref[0:1, rows])
            diagonal = None if diagonal_at is None else i * tile - diagonal_at * count
            counts = pair_count(key_ids, qid_ref[0:1, rows], qid_ref[1:2, rows], diagonal)
            weights = powers * counts
            grad_weights = dot(values, grads, NT)
            grad_scores = (weights * (grad_weights + t_ref[0:1, rows])).astype(BF16)
            grad_values = grad_values + dot(weights.astype(BF16), grads)
            grad_keys = grad_keys + dot(grad_scores, queries)
            dq_ref[rows, :] += dot(grad_scores, wide_keys, TN)
        dkv_ref[...] = jnp.concatenate([grad_keys, grad_values], axis=1).astype(BF16)

    @pl.when(step < steps)
    def _():
        part(kv_refs[0], dkv_refs[0], step if own else None)

    @pl.when(step >= steps)
    def _():
        part(kv_refs[1], dkv_refs[1], None)


def backward_call(queries, grads, norms, terms, ids, kv_pair, part, acc, tk=768, tile=256):
    nq, nk = queries.shape[0], kv_pair[0].shape[0]
    steps = nk // tk
    full = pl.BlockSpec((nq, DH), lambda j: (0, 0))
    row = pl.BlockSpec((8, nq), lambda j: (0, 0))
    first = pl.BlockSpec((tk, 2 * DH), lambda j: (jnp.minimum(j, steps - 1), 0))
    second = pl.BlockSpec((tk, 2 * DH), lambda j: (jnp.maximum(j - steps, 0), 0))
    wide = pl.BlockSpec((nq, 2 * DH), lambda j: (0, 0))
    listed = pl.BlockSpec((tk, 1), lambda j: (part * steps + j, 0))
    more = [] if acc is None else [acc]
    return pl.pallas_call(
        functools.partial(backward_kernel, tile=tile, own=acc is not None),
        grid=(2 * steps,),
        in_specs=[full, full, row, row, row, listed, first, second] + [wide] * len(more),
        out_specs=[wide, first, second],
        out_shape=[shaped(nq, 2 * DH, dtype=F32), *[shaped(nk, 2 * DH)] * 2],
        input_output_aliases={8: 0} if more else {},
        compiler_params=pltpu.CompilerParams(vmem_limit_bytes=62 * 2**20),
        cost_estimate=LONG,
        name="attention_backward",
    )(queries, grads, norms, terms, ids[1], ids[0], *kv_pair, *more)


def out_kernel(place_ref, attn_ref, half_ref, gain_ref, *refs):
    parts, (low_ref, out_ref, normed_ref, weight_ref) = refs[:8], refs[8:]
    rows, width = weight_ref.shape[0] // 32, weight_ref.shape[1]
    masks = [core | near for core in (0, CORE) for near in (0, X, Y, X | Y)]
    for part, mask in zip(parts, masks, strict=True):
        for p in range(4):
            start = pl.multiple_of((((place_ref[0] ^ mask) & (Y | CORE | X)) | (p * Z_LO)) * rows, rows)
            weight_ref[pl.ds(start, rows // 2), :] = part[p, :, :width]
            middle = pl.multiple_of(start + rows // 2, rows // 2)
            weight_ref[pl.ds(middle, rows // 2), :] = part[p, :, width:]
    attn = jnp.concatenate([attn_ref[h] for h in range(NH)], axis=1)
    first_out = half_ref[...].astype(F32) + dot(attn, weight_ref[...])
    out_ref[...] = first_out
    low_ref[...] = first_out.astype(BF16)
    normed_ref[...] = (normalised(first_out)[0] * gain_ref[1:2, :]).astype(BF16)


def ffn_part(z_ref, units, down):
    width = z_ref.shape[2] // 2
    lanes = slice(width, None) if down else slice(width)
    return jnp.concatenate([z_ref[p, :units, lanes] for p in range(4)], axis=0)


def hidden_back_kernel(*refs):
    blocks, z_ref, out_ref = refs[:8], refs[8], refs[9]
    down = ffn_part(z_ref, out_ref.shape[1] // 4, True)
    for i, block in enumerate(blocks):
        rows = pl.ds(i * block.shape[0], block.shape[0])
        out_ref[rows, :] = dot(block[...], down, NT)


def ffn_kernel(*refs):
    blocks, back_ref, z_ref, outs = refs[:8], refs[8], refs[9], refs[10:]
    hidden_ref, grad_ref = outs[8:]
    up = ffn_part(z_ref, hidden_ref.shape[1] // 4, False)
    slope = 0.7978845608028654
    for i in (4, 5, 6, 7, 0, 1, 2, 3):
        block = blocks[i]
        rows = pl.ds(i * block.shape[0], block.shape[0])
        v = dot(block[...], up, NT)
        square = v * v
        t = jnp.tanh(slope * v * (1.0 + 0.044715 * square))
        half = 0.5 * (1.0 + t)
        hidden_ref[rows, :] = (v * half).astype(BF16)
        back = half + 0.5 * v * (1.0 - t * t) * slope * (1.0 + 3 * 0.044715 * square)
        grad = (back_ref[rows, :] * back).astype(BF16)
        grad_ref[rows, :] = grad
        outs[i][...] = dot(grad, up).astype(BF16)


def ffn_rest_kernel(*refs):
    blocks, grads, z_ref = refs[:8], refs[8:16], refs[18]
    hidden_ref, grad_ref = refs[16:18]
    near_ref, far_ref, sum_ref = refs[19:]
    width = sum_ref.shape[1] // 2
    units = sum_ref.shape[0] // 4
    down = ffn_part(z_ref, units, True)
    for i in range(8):
        rows = pl.ds(i * blocks[i].shape[0], blocks[i].shape[0])
        out = (near_ref, far_ref)[i // 4]
        out[i % 4] = dot(hidden_ref[rows, :], down).astype(BF16)
    inputs = jnp.concatenate([block[...] for block in blocks], axis=0)
    sum_ref[:, :width] = dot(grad_ref[...], inputs, TN).astype(BF16)
    cotangents = jnp.concatenate([block[...] for block in grads], axis=0)
    sum_ref[:, width:] = dot(hidden_ref[...], cotangents, TN).astype(BF16)


def mid_kernel(place_ref, *refs):
    parts, rest, outs = refs[:5], refs[5:10], refs[10:]
    out_ref, first_ref, gain_ref, weight_ref, attn_ref = rest
    mid_ref, send_ref, keep_ref, move_ref = outs
    xhat, rstd = normalised(out_ref[...])
    grads = sum(part[...].astype(F32) for part in parts)
    gain_sum = jnp.sum(grads * xhat, axis=0, keepdims=True)
    mid = first_ref[...].astype(F32) + norm_back(grads * gain_ref[1:2, :], xhat, rstd)
    mid = mid.astype(BF16)
    mid_ref[...] = mid
    grad_attn = dot(mid, weight_ref[...], NT).astype(BF16)
    for h in range(NH):
        send_ref[h] = grad_attn[:, h * DH : (h + 1) * DH]
    width = mid_ref.shape[1]
    heads = NH // 4
    core = (place_ref[0] >> 3) & 1
    gains = [
        jnp.broadcast_to(gain_sum[:, h * DH : (h + 1) * DH], (DH, DH)).T for h in range(NH)
    ]
    for ref, bit in ((keep_ref, core), (move_ref, 1 - core)):
        for i in range(NH // 2):
            first, k = divmod(i, heads)
            rows = slice(i * DH, (i + 1) * DH)
            attn = attn_ref[(2 * first + bit) * heads + k]
            ref[rows, :width] = dot(attn, mid, TN).astype(BF16)
            low, high = (gains[(2 * first + b) * heads + k] for b in range(2))
            ref[rows, width:] = jnp.where(bit == 0, low, high).astype(BF16)


def turn_kernel(place_ref, arrived_ref, acc_ref, grads_ref, row_ref, column_ref):
    rows = arrived_ref.shape[1]
    for j in range(NH):
        place = slice(j * rows, (j + 1) * rows)
        block = acc_ref[place, :]
        totals = block[:, DH:]
        attended = block[:, :DH] / totals
        grad_attn = arrived_ref[place_ref[1] ^ j].astype(F32)
        grads_ref[place, :] = (grad_attn / totals).astype(BF16)
        column_ref[place, :] = (
            -jnp.sum(grad_attn * attended, axis=-1, keepdims=True) / totals[:, :1]
        )
    to_row(column_ref, row_ref)


def halve_kernel(place_ref, kept_ref, came_ref, keep_ref, send_ref, *, shift, blocks):
    rows = kept_ref.shape[0] // (2 * blocks)
    bit = (place_ref[0] >> shift) & 1
    for i in range(blocks):
        out = slice(i * rows, (i + 1) * rows)
        for ref, half in ((keep_ref, bit), (send_ref, 1 - bit)):
            start = pl.ds(pl.multiple_of((2 * i + half) * rows, rows), rows)
            total = kept_ref[start, :].astype(F32) + came_ref[start, :].astype(F32)
            ref[out, :] = total.astype(BF16)


def quarter_kernel(place_ref, kept_ref, came_ref, *outs):
    rows = outs[0].shape[0]
    for p, out in enumerate(outs):
        start = pl.ds(pl.multiple_of((((place_ref[0] >> 1) & 3) ^ p) * rows, rows), rows)
        total = kept_ref[start, :].astype(F32) + came_ref[start, :].astype(F32)
        out[...] = total.astype(BF16)


def gather_grads_kernel(place_ref, direct_ref, q_ref, n_ref, normed_ref, *refs):
    kv_refs, (send_ref, *outs), (both_ref, sum_ref) = refs[:3], refs[3:8], refs[8:]
    rows = send_ref.shape[1]
    for j in range(NH):
        place = slice(j * rows, (j + 1) * rows)
        grad_kv = sum(ref[place, :].astype(F32) for ref in kv_refs)
        grad_keys, grad_values = grad_kv[:, :DH], grad_kv[:, DH:]
        queries = q_ref[place, :].astype(F32)
        inverse = lax.rsqrt(jnp.mean(queries * queries, axis=-1, keepdims=True) + 1e-06)
        mean_part = jnp.mean(grad_keys * queries, axis=-1, keepdims=True)
        grad_norms = -direct_ref[place, DH:]
        grad_queries = (
            direct_ref[place, :DH]
            + grad_norms * queries * (LOG2E / n_ref[place, :])
            + (inverse * DH ** (-0.5)) * (grad_keys - queries * (inverse * inverse * mean_part))
        )
        both = jnp.concatenate([grad_queries.astype(BF16), grad_values.astype(BF16)], axis=1)
        both_ref[place, :] = both
        send_ref[place_ref[1] ^ j] = both
    sum_ref[...] = dot(normed_ref[...], both_ref[...], TN)
    rows = outs[0].shape[1]
    for out, mask in zip(outs, PARTS, strict=True):
        for j in range(NH):
            start = pl.multiple_of((place_ref[0] ^ mask ^ j) * rows, rows)
            out[j] = sum_ref[pl.ds(start, rows), :].astype(BF16)


def sum_kernel(place_ref, *refs):
    parts, out = refs[:4], refs[4]
    for j in range(NH):
        out[place_ref[1] ^ j] = sum(part[j].astype(F32) for part in parts).astype(BF16)


def own_rows_kernel(rows_ref, qk_ref, value_ref, gain_ref, *outs):
    grad_qk_ref, grad_value_ref, grad_gain_ref = outs
    for h in range(NH):
        lanes = slice(h * DH, (h + 1) * DH)
        grad_qk_ref[:, lanes] = rows_ref[h, :, :DH].astype(F32)
        grad_value_ref[:, lanes] = rows_ref[h, :, DH:].astype(F32)
    total = jnp.sum(
        qk_ref[...].astype(F32) * grad_qk_ref[...]
        + value_ref[...].astype(F32) * grad_value_ref[...],
        axis=-1,
        keepdims=True,
    )
    grad_gain_ref[...] = jnp.broadcast_to(
        total / gain_ref[:, :1].astype(F32), grad_gain_ref.shape
    )


def unpack_kernel(sum_ref, up_ref, down_ref):
    width = sum_ref.shape[1] // 2
    up_ref[...] = sum_ref[:, :width].astype(F32).T
    down_ref[...] = sum_ref[:, width:].astype(F32)


def last_kernel(arrived_ref, half_ref, grad_ref, gain_ref, weight_ref, out_ref):
    width = half_ref.shape[1]
    grad_q = jnp.concatenate([arrived_ref[h][:, :DH] for h in range(NH)], axis=1)
    grad_v = jnp.concatenate([arrived_ref[h][:, DH:] for h in range(NH)], axis=1)
    grads = dot(grad_q, weight_ref[:, :width], NT) + dot(grad_v, weight_ref[:, width:], NT)
    xhat, rstd = normalised(half_ref[...].astype(F32))
    out_ref[...] = (
        grad_ref[...].astype(F32) + norm_back(grads * gain_ref[0:1, :], xhat, rstd)
    ).astype(BF16)


def cube_plan(
    first_half,
    second_half,
    grad_first,
    grad_second,
    qk_weight,
    value_weight,
    out_weight,
    attn_gain,
    ffn_gain,
    up_weight,
    down_weight,
    stretch_ids,
):
    y, core, z_hi, z_lo, x = (lax.axis_index(name) for name in BITS)
    me = y * 16 + core * 8 + z_hi * 4 + z_lo * 2 + x
    place = jnp.stack([me, me & 7]).astype(I32)
    rows, width = first_half.shape
    wide_rows = rows * 8
    own_rows = qk_weight.shape[0]
    own_units = down_weight.shape[0]
    units = own_units * 4
    rounds, tokens = stretch_ids.shape
    nchunk = tokens // STRETCH
    row_block = shaped(rows, width)
    acc_shape = shaped(rows, width, dtype=F32)

    blocks = gather_zx(second_half)
    gains = jnp.pad(jnp.stack([attn_gain, ffn_gain], axis=1), ((0, 0), (0, DH - 2)))
    columns, z_rows, qv_rows = call(
        pack_kernel,
        [Far(a) for a in (qk_weight, value_weight, out_weight, up_weight, down_weight, gains)],
        [
            shaped(NH, own_rows, 3 * DH),
            shaped(own_units + own_rows // 2, 2 * width),
            shaped(own_rows, 2 * width),
        ],
        "pack",
        cost=None,
        far_out=(1, 2),
    )
    columns = shares(lax.all_to_all(columns, HEAD_AXES, 0, 0, tiled=True))
    weights = lax.all_gather(after(z_rows, blocks[4]), ("z_hi", "z_lo"), axis=0)
    cotangent_y = swap(grad_second, Y)

    ids = stretch_ids.reshape(rounds, 2, 2, 2, 2, 2, rows)
    for axis, bit in enumerate((y, core, z_hi, z_lo, x), 1):
        ids = jnp.where(bit == 1, jnp.flip(ids, axis), ids)
    ids = ids.reshape(rounds, tokens)

    def packed(numbers):
        return sum(numbers[r] << (8 * r) for r in range(rounds))

    ids_row = packed(ids)
    ids_rows = jnp.concatenate(
        [
            ids_row[None],
            packed((ids + nchunk - 1) % nchunk)[None],
            packed((ids + 1) % nchunk)[None],
            jnp.zeros((5, tokens), I32),
        ]
    )
    ids_column = call(
        column_kernel, [Far(ids_rows)], [shaped(tokens, 1, dtype=I32)], "ids", far_out=(0,), cost=None
    )[0]
    ids_both = (ids_column, ids_rows)

    columns[0] = after(columns[0], *ids_both, cotangent_y)
    normed, queries, kv, norms, norm_row, gain_rows = call(
        project_kernel,
        [Far(blocks[0]), *blocks[1:], *columns],
        [
            shaped(wide_rows, width),
            shaped(wide_rows, DH),
            shaped(wide_rows, 2 * DH),
            shaped(wide_rows, 1, dtype=F32),
            shaped(8, wide_rows, dtype=F32),
            shaped(8, width, dtype=F32),
        ],
        "project",
        cost=None,
        far_out=range(6),
        scalars=[place],
        scratch=[pltpu.VMEM((width, 3 * DH), BF16)],
    )
    kv_parts = shares(kv)
    near, near_y = after(grad_second, kv), after(cotangent_y, kv)
    cotangents = [near, swap(near, X), near_y, swap(near_y, X)]
    acc, = forward_call(queries, norms, ids_both, kv_parts[:2], 0, None)
    kv_parts[2] = after(kv_parts[2], acc, *cotangents)
    kv_parts[3] = swap(kv_parts[2], CORE)
    qv_full = lax.all_gather(after(qv_rows, kv_parts[2]), BITS, axis=0, tiled=True)
    acc, = forward_call(queries, norms, ids_both, kv_parts[2:3], 2, acc)
    out_near = near_xy(after(weights, acc)[:, own_units:])
    acc, attn_send = forward_call(queries, norms, ids_both, kv_parts[3:], 3, acc, place)
    cotangents = with_cores([after(a, attn_send) for a in cotangents])
    attn_tok = lax.all_to_all(attn_send, HEAD_AXES, 0, 0, tiled=True)
    units = own_units * 4
    hidden_back = call(
        hidden_back_kernel,
        [*map(Far, cotangents), Far(weights)],
        [shaped(wide_rows, units, dtype=F32)],
        "hidden_back",
        cost=None,
        far_out=(0,),
    )[0]
    out_parts = with_cores([after(a, hidden_back) for a in out_near])
    y_first, first_out, normed_ffn, out_full = call(
        out_kernel,
        [attn_tok, Far(first_half), Far(gain_rows), *out_parts],
        [row_block, acc_shape, row_block, shaped(width, width)],
        "project_out",
        cost=None,
        far_out=(0, 1, 3),
        scalars=[place],
    )
    ffn_in = gather_xy(normed_ffn)
    *grad_blocks, hidden, grad_pre = call(
        ffn_kernel,
        [Far(ffn_in[0]), *ffn_in[1:], Far(hidden_back), Far(weights)],
        [row_block] * 8 + [shaped(wide_rows, units)] * 2,
        "feed_forward",
        cost=None,
        mib=44,
        far_out=(8, 9),
    )
    grad_parts = scatter_xy(grad_blocks)
    ffn_near, ffn_far, grad_ffn = call(
        ffn_rest_kernel,
        [Far(ffn_in[0]), *ffn_in[1:], *map(Far, (*cotangents, hidden, grad_pre, weights))],
        [shaped(4, rows, width)] * 2 + [shaped(units, 2 * width)],
        "feed_forward_rest",
        cost=None,
        far_out=range(3),
        mib=48,
    )
    out_width = width + DH
    half = shaped(width // 2, out_width)
    grad_mid, grad_attn, keep, move = call(
        mid_kernel,
        [
            *grad_parts,
            *map(Far, (after(first_out, grad_ffn, qv_full), grad_first, gain_rows, out_full)),
            Far(attn_tok),
        ],
        [row_block, shaped(NH, rows, DH), half, half],
        "mid",
        cost=None,
        far_out=(0, 2),
        scalars=[place],
    )

    grad_attn = lax.all_to_all(grad_attn, HEAD_AXES, 0, 0, tiled=True)

    def halve(keep, came, shift, blocks):
        half = shaped(keep.shape[0] // 2, out_width)
        return call(
            functools.partial(halve_kernel, shift=shift, blocks=blocks),
            [Far(keep), came],
            [half, half],
            "halve",
            far_out=(0,),
            scalars=[place],
        )

    keep, move = halve(keep, swap(move, CORE), 4, 1)
    ffn_far = swap(after(ffn_far, move), CORE)
    came = swap(move, Y)
    ffn_sum = ffn_near.astype(F32) + ffn_far.astype(F32)
    ffn_move = ffn_sum[1::2].astype(BF16)
    grads, term_row = call(
        turn_kernel,
        [after(grad_attn, move, ffn_move), Far(acc)],
        [shaped(wide_rows, DH), shaped(8, wide_rows, dtype=F32)],
        "turn",
        far_out=(0, 1),
        scalars=[place],
        scratch=[pltpu.VMEM((wide_rows, 1), F32)],
    )

    def backward(part, acc):
        return backward_call(
            queries, grads, norm_row, term_row, ids_both, kv_parts[part : part + 2], part, acc
        )

    grad_ffn = lax.psum_scatter(
        grad_ffn, ("z_hi", "z_lo"), scatter_dimension=0, tiled=True
    )
    direct, over_y, far = backward(2, None)
    far = swap(far, CORE)
    keep, move = halve(keep, after(came, direct), 0, 4)
    over_y = (over_y.astype(F32) + after(far, move).astype(F32)).astype(BF16)
    ffn_move = swap(ffn_move, X)
    direct = after(direct, over_y, ffn_move)
    over_y = swap(over_y, Y)
    came = swap(move, X)
    direct, grad_kv, over_core = backward(0, direct)
    direct = after(direct, grad_ffn)
    over_core = swap(after(over_core, over_y), CORE)

    send, *grad_rows = call(
        gather_grads_kernel,
        [*map(Far, (direct, queries, norms, normed, grad_kv)), over_core, over_y],
        [shaped(NH, rows, 2 * DH)] + [shaped(NH, own_rows, 2 * DH)] * 4,
        "gather_grads",
        scalars=[place],
        scratch=[pltpu.VMEM((wide_rows, 2 * DH), BF16), pltpu.VMEM((width, 2 * DH), F32)],
    )
    arrived = lax.all_to_all(send, HEAD_AXES, 0, 0, tiled=True)
    grad_rows = call(
        sum_kernel,
        sum_shares(grad_rows),
        [shaped(NH, own_rows, 2 * DH)],
        "sum_rows",
        scalars=[place],
    )
    rows_send = grad_rows[0]
    grad_up, grad_down = call(
        unpack_kernel,
        [Far(after(grad_ffn, rows_send))],
        [shaped(width, own_units, dtype=F32), shaped(own_units, width, dtype=F32)],
        "unpack",
        far_out=(0, 1),
    )
    arrived = after(arrived, rows_send, grad_up)
    grad_rows = lax.all_to_all(after(rows_send, arrived), HEAD_AXES, 0, 0, tiled=True)
    grad_second_half = call(
        last_kernel,
        [arrived, *map(Far, (second_half, grad_second, gain_rows, qv_full))],
        [row_block],
        "last",
        far_out=(0,),
    )[0]

    grad_out = call(
        quarter_kernel,
        [keep, after(came, rows_send)],
        [shaped(own_rows, out_width)] * 4,
        "quarter",
        scalars=[place],
    )
    grad_out = sum(
        after(swap(part, p * Z_LO) if p else part, arrived).astype(F32)
        for p, part in enumerate(grad_out)
    )
    ffn_sum = ffn_sum[0::2] + after(ffn_move, rows_send).astype(F32)
    ffn_sum = ffn_sum[0] + after(swap(ffn_sum[1].astype(BF16), Y), arrived).astype(F32)
    second_out = second_half.astype(F32) + ffn_sum
    grad_qk, grad_value, grad_attn_gain = call(
        own_rows_kernel,
        [after(grad_rows, grad_second_half, grad_up), Far(qk_weight), Far(value_weight), Far(gains)],
        [shaped(own_rows, width, dtype=F32)] * 2 + [shaped(own_rows, 128, dtype=F32)],
        "own_rows",
        far_out=(0, 1),
    )

    return (
        y_first,
        second_out.astype(BF16),
        grad_mid,
        grad_second_half,
        grad_qk,
        grad_value,
        grad_out[:, :width],
        grad_attn_gain[:, 0],
        grad_out[:, width],
        grad_up,
        grad_down,
    )


def solution(mesh):
    if dict(mesh.shape) == {"head": 4, "blk": 8}:
        plan, axes = cube_plan, BITS
        mesh = jax.sharding.Mesh(mesh.devices.reshape((2,) * 5), BITS)
    else:
        plan, axes = ring_plan, ("head", "blk")
    by_row, by_column, vector = P(axes, None), P(None, axes), P(axes)
    return jax.shard_map(
        plan,
        mesh=mesh,
        in_specs=(by_row,) * 7 + (vector, vector, by_column, by_row, P()),
        out_specs=(by_row,) * 7 + (vector, vector, by_column, by_row),
        check_vma=False,
    )
```

```python
import functools

import jax
import jax.numpy as jnp
from jax import lax
from jax.experimental import pallas as pl
from jax.experimental.pallas import tpu as pltpu
from jax.sharding import PartitionSpec as P

NH = 8
DH = 128
STRETCH = 64


def shifted(value, axis, by):
    devices = lax.axis_size(axis)
    return lax.ppermute(value, axis, [(i, (i + by) % devices) for i in range(devices)])


def layer_norm(values, gains):
    average = jnp.mean(values, axis=-1, keepdims=True)
    centred = values - average
    variance = jnp.mean(centred * centred, axis=-1, keepdims=True)
    return centred * lax.rsqrt(variance + 1e-05) * gains


def key_norm(queries):
    return (
        queries
        * lax.rsqrt(jnp.mean(queries * queries, axis=-1, keepdims=True) + 1e-06)
        * queries.shape[-1] ** (-0.5)
    )


def row_norm(queries):
    return jnp.sqrt(jnp.sum(queries * queries, axis=-1) + 1e-06)


def group_ids(stretch_ids, heads_count, cycle_count, local_rows, cycle_index):
    shaped = stretch_ids.reshape(stretch_ids.shape[0], heads_count, cycle_count, local_rows)
    picked = lax.dynamic_slice_in_dim(shaped, cycle_index, 1, 2)
    places = (
        jnp.arange(heads_count, dtype=jnp.int32)[:, None] * cycle_count + cycle_index
    ) * local_rows
    places = places + jnp.arange(local_rows, dtype=jnp.int32)[None, :]
    return (picked.reshape(stretch_ids.shape[0], heads_count * local_rows), places.reshape(-1))


def pair_counts(query_ids, query_places, key_ids, key_places, nchunk):
    previous = (query_ids + nchunk - 1) % nchunk
    same_stretch = key_ids[:, None, :] == query_ids[:, :, None]
    before = key_ids[:, None, :] == previous[:, :, None]
    counts = jnp.sum((same_stretch | before).astype(jnp.float32), axis=0)
    return counts * (query_places[:, None] != key_places[None, :]).astype(jnp.float32)


def forward_block(queries, query_norms, counts, key_block, value_block):
    scores = jnp.einsum("qhd,khd->hqk", queries, key_block, preferred_element_type=jnp.float32)
    weights = counts[None] * jnp.exp(scores - query_norms.T[:, :, None])
    summed = jnp.einsum(
        "hqk,khd->qhd",
        weights.astype(jnp.bfloat16),
        value_block,
        preferred_element_type=jnp.float32,
    )
    return (jnp.sum(weights, axis=-1), summed)


def backward_block(queries, query_norms, counts, key_block, value_block, grad_summed, grad_totals):
    scores = jnp.einsum("qhd,khd->hqk", queries, key_block, preferred_element_type=jnp.float32)
    weights = counts[None] * jnp.exp(scores - query_norms.T[:, :, None])
    grad_weights = jnp.einsum(
        "qhd,khd->hqk", grad_summed, value_block, preferred_element_type=jnp.float32
    )
    grad_scores_f = weights * (grad_weights + grad_totals[:, :, None])
    grad_scores = grad_scores_f.astype(jnp.bfloat16)
    grad_norms = -jnp.sum(grad_scores_f, axis=-1)
    grad_values = jnp.einsum(
        "hqk,qhd->khd",
        weights.astype(jnp.bfloat16),
        grad_summed,
        preferred_element_type=jnp.float32,
    )
    grad_direct = jnp.einsum(
        "hqk,khd->qhd", grad_scores, key_block, preferred_element_type=jnp.float32
    )
    grad_keys = jnp.einsum("hqk,qhd->khd", grad_scores, queries, preferred_element_type=jnp.float32)
    return (grad_norms, grad_direct, grad_keys, grad_values)


def feed_forward(normed_ffn, grad_output, up_part, down_part):
    pre_act = jnp.dot(normed_ffn, up_part, preferred_element_type=jnp.float32)
    hidden_f, gelu_back = jax.vjp(jax.nn.gelu, pre_act)
    hidden = hidden_f.astype(jnp.bfloat16)
    ffn_result = jnp.dot(hidden, down_part, preferred_element_type=jnp.float32)
    grad_hidden = jnp.dot(grad_output, down_part.T, preferred_element_type=jnp.float32)
    grad_pre = gelu_back(grad_hidden)[0].astype(jnp.bfloat16)
    grad_normed = jnp.dot(grad_pre, up_part.T, preferred_element_type=jnp.float32)
    grad_up = jnp.dot(normed_ffn.T, grad_pre, preferred_element_type=jnp.float32)
    grad_down = jnp.dot(hidden.T, grad_output, preferred_element_type=jnp.float32)
    return (ffn_result, grad_normed, grad_up, grad_down)


def ring_plan(
    first_half,
    second_half,
    grad_first,
    grad_second,
    qk_weight,
    value_weight,
    out_weight,
    attn_gain,
    ffn_gain,
    up_weight,
    down_weight,
    stretch_ids,
):
    heads_count = lax.axis_size("head")
    cycle_count = lax.axis_size("blk")
    cycle_index = lax.axis_index("blk")
    local_rows = first_half.shape[0]
    model_width = first_half.shape[1]
    group_rows = local_rows * heads_count
    local_heads = NH // heads_count
    nchunk = stretch_ids.shape[1] // STRETCH
    full_qk, full_value, full_out, full_attn_gain, full_ffn_gain, up_part, down_part = (
        lax.all_gather(qk_weight, ("head", "blk"), axis=0, tiled=True),
        lax.all_gather(value_weight, ("head", "blk"), axis=0, tiled=True),
        lax.all_gather(out_weight, ("head", "blk"), axis=0, tiled=True),
        lax.all_gather(attn_gain, ("head", "blk"), axis=0, tiled=True),
        lax.all_gather(ffn_gain, ("head", "blk"), axis=0, tiled=True),
        lax.all_gather(up_weight, ("head", "blk"), axis=1, tiled=True),
        lax.all_gather(down_weight, ("head", "blk"), axis=0, tiled=True),
    )
    second_f = second_half.astype(jnp.float32)
    normed_f, attn_norm_back = jax.vjp(layer_norm, second_f, full_attn_gain.astype(jnp.float32))
    normed = normed_f.astype(jnp.bfloat16)
    query_tok = jnp.dot(normed, full_qk, preferred_element_type=jnp.float32).astype(jnp.bfloat16)
    value_tok = jnp.dot(normed, full_value, preferred_element_type=jnp.float32).astype(jnp.bfloat16)
    query_heads = query_tok.reshape(local_rows, NH, DH)
    value_heads = value_tok.reshape(local_rows, NH, DH)
    queries, values = (
        lax.all_to_all(query_heads, "head", split_axis=1, concat_axis=0, tiled=True),
        lax.all_to_all(value_heads, "head", split_axis=1, concat_axis=0, tiled=True),
    )
    query_f = queries.astype(jnp.float32)
    key_f, key_back = jax.vjp(key_norm, query_f)
    keys = key_f.astype(jnp.bfloat16)
    query_norms, norm_back = jax.vjp(row_norm, query_f)
    query_ids, query_places = group_ids(
        stretch_ids, heads_count, cycle_count, local_rows, cycle_index
    )

    def counts_for(cycle_step):
        source_index = (cycle_index - cycle_step + cycle_count) % cycle_count
        key_ids, key_places = group_ids(
            stretch_ids, heads_count, cycle_count, local_rows, source_index
        )
        return pair_counts(query_ids, query_places, key_ids, key_places, nchunk)

    def rotate(key_block, value_block):
        return shifted((key_block, value_block), "blk", 1)

    def forward_step(cycle_step, carried):
        key_block, value_block, totals, summed = carried
        part_totals, part_summed = forward_block(
            queries, query_norms, counts_for(cycle_step), key_block, value_block
        )
        key_next, value_next = rotate(key_block, value_block)
        return (key_next, value_next, totals + part_totals, summed + part_summed)

    initial = (
        keys,
        values,
        jnp.zeros((local_heads, group_rows), jnp.float32),
        jnp.zeros((group_rows, local_heads, DH), jnp.float32),
    )
    key_block, value_block, totals, summed = lax.fori_loop(
        0, cycle_count - 1, forward_step, initial
    )
    part_totals, part_summed = forward_block(
        queries, query_norms, counts_for(cycle_count - 1), key_block, value_block
    )
    totals = totals + part_totals
    summed = summed + part_summed
    attended = summed / totals.T[:, :, None]
    attn_tok = lax.all_to_all(
        attended.astype(jnp.bfloat16), "head", split_axis=0, concat_axis=1, tiled=True
    ).reshape(local_rows, model_width)
    first_out = first_half.astype(jnp.float32) + jnp.dot(
        attn_tok, full_out, preferred_element_type=jnp.float32
    )
    normed_ffn_f, ffn_norm_back = jax.vjp(layer_norm, first_out, full_ffn_gain.astype(jnp.float32))
    normed_ffn = normed_ffn_f.astype(jnp.bfloat16)
    ffn_result, grad_normed_ffn, grad_up, grad_down = feed_forward(
        normed_ffn, grad_second, up_part, down_part
    )
    second_out = second_f + ffn_result
    grad_mid_ffn, grad_ffn_gain = ffn_norm_back(grad_normed_ffn)
    grad_mid = grad_first.astype(jnp.float32) + grad_mid_ffn
    grad_mid_low = grad_mid.astype(jnp.bfloat16)
    grad_out = jnp.dot(attn_tok.T, grad_mid_low, preferred_element_type=jnp.float32)
    grad_attn_tok = jnp.dot(grad_mid_low, full_out.T, preferred_element_type=jnp.float32).astype(
        jnp.bfloat16
    )
    grad_attn = lax.all_to_all(
        grad_attn_tok.reshape(local_rows, NH, DH), "head", split_axis=1, concat_axis=0, tiled=True
    )
    grad_attn_f = grad_attn.astype(jnp.float32)
    grad_summed = (grad_attn_f / totals.T[:, :, None]).astype(jnp.bfloat16)
    grad_totals = (-jnp.sum(grad_attn_f * attended, axis=-1) / totals.T).T

    def pass_grads(grad_keys, grad_values):
        return (
            shifted(grad_keys.astype(jnp.bfloat16), "blk", 1).astype(grad_keys.dtype),
            shifted(grad_values.astype(jnp.bfloat16), "blk", 1).astype(grad_values.dtype),
        )

    def backward_step(cycle_step, carried):
        key_block, value_block, grad_keys, grad_values, grad_norms, grad_direct = carried
        pieces = backward_block(
            queries,
            query_norms,
            counts_for(cycle_step),
            key_block,
            value_block,
            grad_summed,
            grad_totals,
        )
        key_next, value_next = rotate(key_block, value_block)
        grad_keys, grad_values = pass_grads(grad_keys + pieces[2], grad_values + pieces[3])
        return (
            key_next,
            value_next,
            grad_keys,
            grad_values,
            grad_norms + pieces[0],
            grad_direct + pieces[1],
        )

    zero_rows = jnp.zeros((group_rows, local_heads, DH), jnp.float32)
    initial = (
        keys,
        values,
        zero_rows,
        zero_rows,
        jnp.zeros((local_heads, group_rows), jnp.float32),
        zero_rows,
    )
    carried = lax.fori_loop(0, cycle_count - 1, backward_step, initial)
    pieces = backward_block(
        queries,
        query_norms,
        counts_for(cycle_count - 1),
        carried[0],
        carried[1],
        grad_summed,
        grad_totals,
    )
    grad_keys, grad_values = pass_grads(carried[2] + pieces[2], carried[3] + pieces[3])
    grad_norms = carried[4] + pieces[0]
    grad_direct = carried[5] + pieces[1]
    grad_queries = grad_direct + norm_back(grad_norms.T)[0] + key_back(grad_keys)[0]
    grad_q_tok, grad_v_tok = (
        lax.all_to_all(
            grad_queries.astype(jnp.bfloat16), "head", split_axis=0, concat_axis=1, tiled=True
        ),
        lax.all_to_all(
            grad_values.astype(jnp.bfloat16), "head", split_axis=0, concat_axis=1, tiled=True
        ),
    )
    grad_q_tok = grad_q_tok.reshape(local_rows, model_width)
    grad_v_tok = grad_v_tok.reshape(local_rows, model_width)
    grad_normed = jnp.dot(grad_q_tok, full_qk.T, preferred_element_type=jnp.float32) + jnp.dot(
        grad_v_tok, full_value.T, preferred_element_type=jnp.float32
    )
    grad_qk = jnp.dot(normed.T, grad_q_tok, preferred_element_type=jnp.float32)
    grad_value = jnp.dot(normed.T, grad_v_tok, preferred_element_type=jnp.float32)
    grad_second_attn, grad_attn_gain = attn_norm_back(grad_normed)
    grad_second_total = grad_second.astype(jnp.float32) + grad_second_attn
    sum_qk, sum_value, sum_out, sum_attn_gain, sum_ffn_gain, sum_up, sum_down = (
        lax.psum_scatter(grad_qk, ("head", "blk"), scatter_dimension=0, tiled=True),
        lax.psum_scatter(grad_value, ("head", "blk"), scatter_dimension=0, tiled=True),
        lax.psum_scatter(grad_out, ("head", "blk"), scatter_dimension=0, tiled=True),
        lax.psum_scatter(grad_attn_gain, ("head", "blk"), scatter_dimension=0, tiled=True),
        lax.psum_scatter(grad_ffn_gain, ("head", "blk"), scatter_dimension=0, tiled=True),
        lax.psum_scatter(grad_up, ("head", "blk"), scatter_dimension=1, tiled=True),
        lax.psum_scatter(grad_down, ("head", "blk"), scatter_dimension=0, tiled=True),
    )
    return (
        first_out.astype(jnp.bfloat16),
        second_out.astype(jnp.bfloat16),
        grad_mid.astype(jnp.bfloat16),
        grad_second_total.astype(jnp.bfloat16),
        sum_qk,
        sum_value,
        sum_out,
        sum_attn_gain,
        sum_ffn_gain,
        sum_up,
        sum_down,
    )


BITS = ("y", "core", "z_hi", "z_lo", "x")
Y, CORE, Z_HI, Z_LO, X = 16, 8, 4, 2, 1
HEAD_AXES = ("z_hi", "z_lo", "x")
PARTS = (0, CORE, Y, Y | CORE)
LOG2E = 1.4426950408889634
HIGH_BITS = -2139062144
NT = (((1,), (1,)), ((), ()))
NN = (((1,), (0,)), ((), ()))
TN = (((0,), (0,)), ((), ()))
F32, BF16, I32 = jnp.float32, jnp.bfloat16, jnp.int32
LONG = pl.CostEstimate(flops=10**11, bytes_accessed=1, transcendentals=0)
SMEM = pl.BlockSpec(memory_space=pltpu.SMEM)


def dot(left, right, dims=NN):
    return lax.dot_general(left, right, dims, preferred_element_type=F32)


def swap(value, mask):
    return lax.ppermute(value, BITS, [(i, i ^ mask) for i in range(32)])


def after(value, *others):
    return lax.optimization_barrier((value, *others))[0]


def shaped(*shape, dtype=BF16):
    return jax.ShapeDtypeStruct(shape, dtype)


class Far:
    def __init__(self, value):
        self.value = value


class Fetched:
    def __init__(self, ref, copy):
        self.ref, self.copy, self.shape = ref, copy, ref.shape

    def wait(self):
        if self.copy is not None:
            self.copy.wait()
            self.copy = None

    def __getitem__(self, place):
        self.wait()
        return self.ref[place]


def call(kernel, inputs, out_shape, name, far_out=(), mib=62, scalars=(), scratch=(), cost=LONG, lazy=False):
    far_in = [i for i, a in enumerate(inputs) if lazy or isinstance(a, Far)]
    arrays = [a.value if isinstance(a, Far) else a for a in inputs]
    first_in, first_out = len(scalars), len(scalars) + len(arrays)
    first_scratch = first_out + len(out_shape)
    staged = [arrays[i] for i in far_in] + [out_shape[i] for i in far_out]

    def body(*refs):
        refs, sems = list(refs[:-1]), refs[-1]
        own = refs[first_scratch : first_scratch + len(scratch)]
        stages = refs[first_scratch + len(scratch) :]
        fetched = []
        for k, i in enumerate(far_in):
            copy = pltpu.make_async_copy(refs[first_in + i], stages[k], sems.at[k])
            copy.start()
            fetched.append(Fetched(stages[k], copy))
            refs[first_in + i] = fetched[-1]
        if not lazy:
            for operand in fetched:
                operand.wait()
        copies = []
        for k, i in enumerate(far_out, len(far_in)):
            copies.append(pltpu.make_async_copy(stages[k], refs[first_out + i], sems.at[k]))
            refs[first_out + i] = stages[k]
        kernel(*refs[:first_scratch], *own)
        for operand in fetched:
            operand.wait()
        for copy in copies:
            copy.start()
        for copy in copies:
            copy.wait()

    near, far = pl.BlockSpec(memory_space=pltpu.VMEM), pl.BlockSpec(memory_space=pl.ANY)
    return pl.pallas_call(
        body,
        in_specs=[SMEM] * len(scalars) + [far if i in far_in else near for i in range(len(arrays))],
        out_specs=[far if i in far_out else near for i in range(len(out_shape))],
        out_shape=out_shape,
        scratch_shapes=[
            *scratch,
            *(pltpu.VMEM(a.shape, a.dtype) for a in staged),
            pltpu.SemaphoreType.DMA((max(len(staged), 1),)),
        ],
        compiler_params=pltpu.CompilerParams(vmem_limit_bytes=mib * 2**20),
        cost_estimate=cost,
        name=name,
    )(*scalars, *arrays)


def with_cores(near):
    return near + [swap(part, CORE) for part in near]


def near_xy(value):
    return [value, swap(value, X), swap(value, Y), swap(value, X | Y)]


def gather_xy(value):
    return with_cores(near_xy(value))


def gather_zx(value):
    low, high = swap(value, Z_LO), swap(value, Z_HI)
    both = swap(high, Z_LO)
    beside_low = swap(low, X)
    beside_high = swap(after(high, beside_low), X)
    beside_both = swap(after(both, beside_high), X)
    return [value, swap(value, X), low, beside_low, high, beside_high, both, beside_both]


def scatter_xy(blocks):
    arrived = [swap(block, CORE) for block in blocks[4:]]
    sums = [
        (near.astype(F32) + far.astype(F32)).astype(BF16)
        for near, far in zip(blocks[1:4], arrived[1:], strict=True)
    ]
    sent = [swap(part, mask) for part, mask in zip(sums, (X, Y, X | Y), strict=True)]
    return [blocks[0], arrived[0], *sent]


def scatter_by_x(blocks):
    arrived = [swap(block, CORE) for block in blocks[4:]]
    own, one, two, both = (
        near.astype(F32) + far.astype(F32) for near, far in zip(blocks[:4], arrived, strict=True)
    )
    own = own + swap(one.astype(BF16), X).astype(F32)
    two = two + swap(both.astype(BF16), X).astype(F32)
    return own + swap(two.astype(BF16), Y).astype(F32)


def shares(value):
    over_y = swap(value, Y)
    return [value, swap(value, CORE), over_y, swap(over_y, CORE)]


def sum_shares(blocks):
    return [blocks[0]] + [swap(b, mask) for b, mask in zip(blocks[1:], PARTS[1:], strict=True)]


def normalised(values):
    centred = values - jnp.mean(values, axis=-1, keepdims=True)
    rstd = lax.rsqrt(jnp.mean(centred * centred, axis=-1, keepdims=True) + 1e-05)
    return centred * rstd, rstd


def norm_back(scaled_grads, xhat, rstd):
    return rstd * (
        scaled_grads
        - jnp.mean(scaled_grads, axis=-1, keepdims=True)
        - xhat * jnp.mean(scaled_grads * xhat, axis=-1, keepdims=True)
    )


def to_row(column_ref, row_ref):
    for i in range(row_ref.shape[1] // 128):
        chunk = slice(i * 128, (i + 1) * 128)
        square = jnp.broadcast_to(column_ref[chunk, :], (128, 128))
        row_ref[:, chunk] = square.T[0:8, :]


def pack_kernel(*refs):
    qk_ref, value_ref, out_ref, up_ref, down_ref, gain_ref, columns_ref, z_ref, qv_ref = refs
    rows, width = qk_ref.shape
    units = down_ref.shape[0]
    for h in range(NH):
        lanes = slice(h * DH, (h + 1) * DH)
        columns_ref[h, :, :DH] = qk_ref[:, lanes]
        columns_ref[h, :, DH : 2 * DH] = value_ref[:, lanes]
        columns_ref[h, :, 2 * DH :] = gain_ref[...]
    z_ref[:units, :width] = up_ref[...].astype(F32).T.astype(BF16)
    z_ref[:units, width:] = down_ref[...]
    z_ref[units:, :width] = out_ref[: rows // 2, :]
    z_ref[units:, width:] = out_ref[rows // 2 :, :]
    qv_ref[:, :width] = qk_ref[...]
    qv_ref[:, width:] = value_ref[...]


def column_kernel(row_ref, column_ref):
    for i in range(row_ref.shape[1] // 128):
        chunk = slice(i * 128, (i + 1) * 128)
        square = jnp.broadcast_to(row_ref[0:1, chunk], (128, 128))
        column_ref[chunk, :] = square.T[:, 0:1]


def project_kernel(place_ref, *refs):
    blocks, parts, outs = refs[:8], refs[8:12], refs[12:18]
    weight_ref = refs[18]
    normed_ref, q_ref, kv_ref, norm_ref, row_ref, gain_ref = outs
    me = place_ref[0]
    rows = parts[0].shape[1]
    for part, mask in zip(parts, PARTS, strict=True):
        for s in range(NH):
            owner = ((me ^ mask) & (Y | CORE)) | s
            weight_ref[pl.ds(pl.multiple_of(owner * rows, rows), rows), :] = part[s]
    for i in range(weight_ref.shape[0] // 128):
        chunk = slice(i * 128, (i + 1) * 128)
        gain_ref[:, chunk] = weight_ref[chunk, 2 * DH :].astype(F32).T[0:8, :]
    weight = weight_ref[:, : 2 * DH]
    gain = gain_ref[0:1, :]
    for i, block in enumerate(blocks):
        rows = pl.ds(i * block.shape[0], block.shape[0])
        normed = (normalised(block[...].astype(F32))[0] * gain).astype(BF16)
        normed_ref[rows, :] = normed
        both = dot(normed, weight)
        queries = both[:, :DH].astype(BF16)
        q_ref[rows, :] = queries
        query_f = queries.astype(F32)
        squares = jnp.sum(query_f * query_f, axis=-1, keepdims=True)
        keys = (query_f * lax.rsqrt(squares / DH + 1e-06) * DH ** (-0.5)).astype(BF16)
        kv_ref[rows, :] = jnp.concatenate([keys, both[:, DH:].astype(BF16)], axis=1)
        norm_ref[rows, :] = jnp.sqrt(squares + 1e-06) * LOG2E
    to_row(norm_ref, row_ref)


def pair_count(one, other, neighbour, diagonal):
    high = jnp.int32(HIGH_BITS)
    match = ((high - (one ^ other)) | (high - (one ^ neighbour))) & high
    counts = lax.population_count(match)
    if diagonal is not None:
        across = lax.broadcasted_iota(I32, counts.shape, 0) - lax.broadcasted_iota(
            I32, counts.shape, 1
        )
        counts = jnp.where(across == diagonal, 0, counts)
    return counts.astype(F32)


def forward_kernel(*refs, tile, parts, own, last):
    q_ref, n_ref, qid_ref, kid_ref = refs[:4]
    kv_refs = refs[4 : 4 + parts]
    acc_in = None if own else refs[4 + parts]
    place_ref = refs[5 + parts] if last else None
    acc_ref = refs[-2] if last else refs[-1]
    step = pl.program_id(0)
    steps = pl.num_programs(0) // parts

    @pl.when(step == 0)
    def _():
        acc_ref[...] = jnp.zeros_like(acc_ref) if own else acc_in[...]

    def part(kv_ref, diagonal_at):
        count = kv_ref.shape[0]
        keys = kv_ref[:, :DH]
        values = jnp.concatenate([kv_ref[:, DH:], jnp.ones((count, DH), BF16)], axis=1)
        for i in range(q_ref.shape[0] // tile):
            rows = slice(i * tile, (i + 1) * tile)
            scores = dot(q_ref[rows, :], keys, NT)
            powers = jnp.exp2(scores * LOG2E - n_ref[rows, :])
            diagonal = None if diagonal_at is None else diagonal_at * count - i * tile
            counts = pair_count(qid_ref[rows, :], kid_ref[0:1, :], kid_ref[2:3, :], diagonal)
            acc_ref[rows, :] += dot((powers * counts).astype(BF16), values)

    for number, kv_ref in enumerate(kv_refs):

        @pl.when(step // steps == number)
        def _(kv_ref=kv_ref, diagonal_at=step if own and number == 0 else None):
            part(kv_ref, diagonal_at)

    if last:
        send_ref = refs[-1]
        rows = send_ref.shape[1]

        @pl.when(step == parts * steps - 1)
        def _():
            for j in range(NH):
                block = acc_ref[j * rows : (j + 1) * rows, :]
                send_ref[place_ref[1] ^ j] = (block[:, :DH] / block[:, DH:]).astype(BF16)


def forward_call(queries, norms, ids, kvs, part, acc, place=None, tk=768, tile=256):
    nq, nk = queries.shape[0], kvs[0].shape[0]
    steps = nk // tk
    column = pl.BlockSpec((nq, 1), lambda j: (0, 0))
    full = pl.BlockSpec((nq, DH), lambda j: (0, 0))
    keyed = [
        pl.BlockSpec((tk, 2 * DH), lambda j, n=n: (jnp.clip(j - n * steps, 0, steps - 1), 0))
        for n in range(len(kvs))
    ]
    wide = pl.BlockSpec((nq, 2 * DH), lambda j: (0, 0))
    listed = pl.BlockSpec((8, tk), lambda j: (0, part * steps + j))
    inputs = [queries, norms, ids[0], ids[1], *kvs]
    specs = [full, column, column, listed, *keyed]
    out_shape, out_specs = [shaped(nq, 2 * DH, dtype=F32)], [wide]
    if acc is not None:
        inputs.append(acc)
        specs.append(wide)
    if place is not None:
        inputs.append(place)
        specs.append(SMEM)
        out_shape.append(shaped(NH, nq // NH, DH))
        out_specs.append(pl.BlockSpec((NH, nq // NH, DH), lambda j: (0, 0, 0)))
    return pl.pallas_call(
        functools.partial(
            forward_kernel, tile=tile, parts=len(kvs), own=acc is None, last=place is not None
        ),
        grid=(len(kvs) * steps,),
        in_specs=specs,
        out_specs=out_specs,
        out_shape=out_shape,
        input_output_aliases={} if acc is None else {4 + len(kvs): 0},
        compiler_params=pltpu.CompilerParams(vmem_limit_bytes=62 * 2**20),
        name="attention_forward",
    )(*inputs)


def backward_kernel(*refs, tile, own):
    q_ref, g_ref, n_ref, t_ref, qid_ref, kid_ref = refs[:6]
    kv_refs = refs[6:8]
    dq_ref, *dkv_refs = refs[-3:]
    step = pl.program_id(0)
    steps = pl.num_programs(0) // 2

    @pl.when(step == 0)
    def _():
        dq_ref[...] = refs[8][...] if own else jnp.zeros_like(dq_ref)

    def part(kv_ref, dkv_ref, diagonal_at):
        keys, values, key_ids = kv_ref[:, :DH], kv_ref[:, DH:], kid_ref[...]
        count = keys.shape[0]
        wide_keys = jnp.concatenate([keys, jnp.ones(keys.shape, BF16)], axis=1)
        grad_keys = jnp.zeros(keys.shape, F32)
        grad_values = jnp.zeros(keys.shape, F32)
        for i in range(q_ref.shape[0] // tile):
            rows = slice(i * tile, (i + 1) * tile)
            queries, grads = q_ref[rows, :], g_ref[rows, :]
            scores = dot(keys, queries, NT)
            powers = jnp.exp2(scores * LOG2E - n_ref[0:1, rows])
            diagonal = None if diagonal_at is None else i * tile - diagonal_at * count
            counts = pair_count(key_ids, qid_ref[0:1, rows], qid_ref[1:2, rows], diagonal)
            weights = powers * counts
            grad_weights = dot(values, grads, NT)
            grad_scores = (weights * (grad_weights + t_ref[0:1, rows])).astype(BF16)
            grad_values = grad_values + dot(weights.astype(BF16), grads)
            grad_keys = grad_keys + dot(grad_scores, queries)
            dq_ref[rows, :] += dot(grad_scores, wide_keys, TN)
        dkv_ref[...] = jnp.concatenate([grad_keys, grad_values], axis=1).astype(BF16)

    @pl.when(step < steps)
    def _():
        part(kv_refs[0], dkv_refs[0], step if own else None)

    @pl.when(step >= steps)
    def _():
        part(kv_refs[1], dkv_refs[1], None)


def backward_call(queries, grads, norms, terms, ids, kv_pair, part, acc, tk=768, tile=256):
    nq, nk = queries.shape[0], kv_pair[0].shape[0]
    steps = nk // tk
    full = pl.BlockSpec((nq, DH), lambda j: (0, 0))
    row = pl.BlockSpec((8, nq), lambda j: (0, 0))
    first = pl.BlockSpec((tk, 2 * DH), lambda j: (jnp.minimum(j, steps - 1), 0))
    second = pl.BlockSpec((tk, 2 * DH), lambda j: (jnp.maximum(j - steps, 0), 0))
    wide = pl.BlockSpec((nq, 2 * DH), lambda j: (0, 0))
    listed = pl.BlockSpec((tk, 1), lambda j: (part * steps + j, 0))
    more = [] if acc is None else [acc]
    return pl.pallas_call(
        functools.partial(backward_kernel, tile=tile, own=acc is not None),
        grid=(2 * steps,),
        in_specs=[full, full, row, row, row, listed, first, second] + [wide] * len(more),
        out_specs=[wide, first, second],
        out_shape=[shaped(nq, 2 * DH, dtype=F32), *[shaped(nk, 2 * DH)] * 2],
        input_output_aliases={8: 0} if more else {},
        compiler_params=pltpu.CompilerParams(vmem_limit_bytes=62 * 2**20),
        cost_estimate=LONG,
        name="attention_backward",
    )(queries, grads, norms, terms, ids[1], ids[0], *kv_pair, *more)


def out_kernel(place_ref, attn_ref, half_ref, gain_ref, *refs):
    parts, (low_ref, out_ref, normed_ref, weight_ref) = refs[:8], refs[8:]
    rows, width = weight_ref.shape[0] // 32, weight_ref.shape[1]
    masks = [core | near for core in (0, CORE) for near in (0, X, Y, X | Y)]
    for part, mask in zip(parts, masks, strict=True):
        for p in range(4):
            start = pl.multiple_of((((place_ref[0] ^ mask) & (Y | CORE | X)) | (p * Z_LO)) * rows, rows)
            weight_ref[pl.ds(start, rows // 2), :] = part[p, :, :width]
            middle = pl.multiple_of(start + rows // 2, rows // 2)
            weight_ref[pl.ds(middle, rows // 2), :] = part[p, :, width:]
    attn = jnp.concatenate([attn_ref[h] for h in range(NH)], axis=1)
    first_out = half_ref[...].astype(F32) + dot(attn, weight_ref[...])
    out_ref[...] = first_out
    low_ref[...] = first_out.astype(BF16)
    normed_ref[...] = (normalised(first_out)[0] * gain_ref[1:2, :]).astype(BF16)


def ffn_part(z_ref, units, down):
    width = z_ref.shape[2] // 2
    lanes = slice(width, None) if down else slice(width)
    return jnp.concatenate([z_ref[p, :units, lanes] for p in range(4)], axis=0)


def hidden_back_kernel(*refs):
    blocks, z_ref, out_ref = refs[:8], refs[8], refs[9]
    down = ffn_part(z_ref, out_ref.shape[1] // 4, True)
    for i, block in enumerate(blocks):
        rows = pl.ds(i * block.shape[0], block.shape[0])
        out_ref[rows, :] = dot(block[...], down, NT)


def ffn_kernel(*refs):
    blocks, back_ref, z_ref, outs = refs[:8], refs[8], refs[9], refs[10:]
    hidden_ref, grad_ref = outs[8:]
    up = ffn_part(z_ref, hidden_ref.shape[1] // 4, False)
    slope = 0.7978845608028654
    for i in (4, 5, 6, 7, 0, 1, 2, 3):
        block = blocks[i]
        rows = pl.ds(i * block.shape[0], block.shape[0])
        v = dot(block[...], up, NT)
        square = v * v
        t = jnp.tanh(slope * v * (1.0 + 0.044715 * square))
        half = 0.5 * (1.0 + t)
        hidden_ref[rows, :] = (v * half).astype(BF16)
        back = half + 0.5 * v * (1.0 - t * t) * slope * (1.0 + 3 * 0.044715 * square)
        grad = (back_ref[rows, :] * back).astype(BF16)
        grad_ref[rows, :] = grad
        outs[i][...] = dot(grad, up).astype(BF16)


def ffn_rest_kernel(*refs):
    blocks, grads, z_ref = refs[:8], refs[8:16], refs[18]
    hidden_ref, grad_ref = refs[16:18]
    near_ref, far_ref, sum_ref = refs[19:]
    width = sum_ref.shape[1] // 2
    units = sum_ref.shape[0] // 4
    down = ffn_part(z_ref, units, True)
    for i in range(8):
        rows = pl.ds(i * blocks[i].shape[0], blocks[i].shape[0])
        out = (near_ref, far_ref)[i // 4]
        out[i % 4] = dot(hidden_ref[rows, :], down).astype(BF16)
    inputs = jnp.concatenate([block[...] for block in blocks], axis=0)
    sum_ref[:, :width] = dot(grad_ref[...], inputs, TN).astype(BF16)
    cotangents = jnp.concatenate([block[...] for block in grads], axis=0)
    sum_ref[:, width:] = dot(hidden_ref[...], cotangents, TN).astype(BF16)


def mid_kernel(place_ref, *refs):
    parts, rest, outs = refs[:5], refs[5:10], refs[10:]
    out_ref, first_ref, gain_ref, weight_ref, attn_ref = rest
    mid_ref, send_ref, keep_ref, move_ref = outs
    xhat, rstd = normalised(out_ref[...])
    grads = sum(part[...].astype(F32) for part in parts)
    gain_sum = jnp.sum(grads * xhat, axis=0, keepdims=True)
    mid = first_ref[...].astype(F32) + norm_back(grads * gain_ref[1:2, :], xhat, rstd)
    mid = mid.astype(BF16)
    mid_ref[...] = mid
    grad_attn = dot(mid, weight_ref[...], NT).astype(BF16)
    for h in range(NH):
        send_ref[h] = grad_attn[:, h * DH : (h + 1) * DH]
    width = mid_ref.shape[1]
    heads = NH // 4
    core = (place_ref[0] >> 3) & 1
    gains = [
        jnp.broadcast_to(gain_sum[:, h * DH : (h + 1) * DH], (DH, DH)).T for h in range(NH)
    ]
    for ref, bit in ((keep_ref, core), (move_ref, 1 - core)):
        for i in range(NH // 2):
            first, k = divmod(i, heads)
            rows = slice(i * DH, (i + 1) * DH)
            attn = attn_ref[(2 * first + bit) * heads + k]
            ref[rows, :width] = dot(attn, mid, TN).astype(BF16)
            low, high = (gains[(2 * first + b) * heads + k] for b in range(2))
            ref[rows, width:] = jnp.where(bit == 0, low, high).astype(BF16)


def turn_kernel(place_ref, arrived_ref, acc_ref, grads_ref, row_ref, column_ref):
    rows = arrived_ref.shape[1]
    for j in range(NH):
        place = slice(j * rows, (j + 1) * rows)
        block = acc_ref[place, :]
        totals = block[:, DH:]
        attended = block[:, :DH] / totals
        grad_attn = arrived_ref[place_ref[1] ^ j].astype(F32)
        grads_ref[place, :] = (grad_attn / totals).astype(BF16)
        column_ref[place, :] = (
            -jnp.sum(grad_attn * attended, axis=-1, keepdims=True) / totals[:, :1]
        )
    to_row(column_ref, row_ref)


def halve_kernel(place_ref, kept_ref, came_ref, keep_ref, send_ref, *, shift, blocks):
    rows = kept_ref.shape[0] // (2 * blocks)
    bit = (place_ref[0] >> shift) & 1
    for i in range(blocks):
        out = slice(i * rows, (i + 1) * rows)
        for ref, half in ((keep_ref, bit), (send_ref, 1 - bit)):
            start = pl.ds(pl.multiple_of((2 * i + half) * rows, rows), rows)
            total = kept_ref[start, :].astype(F32) + came_ref[start, :].astype(F32)
            ref[out, :] = total.astype(BF16)


def quarter_kernel(place_ref, kept_ref, came_ref, *outs):
    rows = outs[0].shape[0]
    for p, out in enumerate(outs):
        start = pl.ds(pl.multiple_of((((place_ref[0] >> 1) & 3) ^ p) * rows, rows), rows)
        total = kept_ref[start, :].astype(F32) + came_ref[start, :].astype(F32)
        out[...] = total.astype(BF16)


def gather_grads_kernel(place_ref, direct_ref, q_ref, n_ref, normed_ref, *refs):
    kv_refs, (send_ref, *outs), (both_ref, sum_ref) = refs[:3], refs[3:8], refs[8:]
    rows = send_ref.shape[1]
    for j in range(NH):
        place = slice(j * rows, (j + 1) * rows)
        grad_kv = sum(ref[place, :].astype(F32) for ref in kv_refs)
        grad_keys, grad_values = grad_kv[:, :DH], grad_kv[:, DH:]
        queries = q_ref[place, :].astype(F32)
        inverse = lax.rsqrt(jnp.mean(queries * queries, axis=-1, keepdims=True) + 1e-06)
        mean_part = jnp.mean(grad_keys * queries, axis=-1, keepdims=True)
        grad_norms = -direct_ref[place, DH:]
        grad_queries = (
            direct_ref[place, :DH]
            + grad_norms * queries * (LOG2E / n_ref[place, :])
            + (inverse * DH ** (-0.5)) * (grad_keys - queries * (inverse * inverse * mean_part))
        )
        both = jnp.concatenate([grad_queries.astype(BF16), grad_values.astype(BF16)], axis=1)
        both_ref[place, :] = both
        send_ref[place_ref[1] ^ j] = both
    sum_ref[...] = dot(normed_ref[...], both_ref[...], TN)
    rows = outs[0].shape[1]
    for out, mask in zip(outs, PARTS, strict=True):
        for j in range(NH):
            start = pl.multiple_of((place_ref[0] ^ mask ^ j) * rows, rows)
            out[j] = sum_ref[pl.ds(start, rows), :].astype(BF16)


def sum_kernel(place_ref, *refs):
    parts, out = refs[:4], refs[4]
    for j in range(NH):
        out[place_ref[1] ^ j] = sum(part[j].astype(F32) for part in parts).astype(BF16)


def own_rows_kernel(rows_ref, qk_ref, value_ref, gain_ref, *outs):
    grad_qk_ref, grad_value_ref, grad_gain_ref = outs
    for h in range(NH):
        lanes = slice(h * DH, (h + 1) * DH)
        grad_qk_ref[:, lanes] = rows_ref[h, :, :DH].astype(F32)
        grad_value_ref[:, lanes] = rows_ref[h, :, DH:].astype(F32)
    total = jnp.sum(
        qk_ref[...].astype(F32) * grad_qk_ref[...]
        + value_ref[...].astype(F32) * grad_value_ref[...],
        axis=-1,
        keepdims=True,
    )
    grad_gain_ref[...] = jnp.broadcast_to(
        total / gain_ref[:, :1].astype(F32), grad_gain_ref.shape
    )


def unpack_kernel(sum_ref, up_ref, down_ref):
    width = sum_ref.shape[1] // 2
    up_ref[...] = sum_ref[:, :width].astype(F32).T
    down_ref[...] = sum_ref[:, width:].astype(F32)


def last_kernel(arrived_ref, half_ref, grad_ref, gain_ref, weight_ref, out_ref):
    width = half_ref.shape[1]
    grad_q = jnp.concatenate([arrived_ref[h][:, :DH] for h in range(NH)], axis=1)
    grad_v = jnp.concatenate([arrived_ref[h][:, DH:] for h in range(NH)], axis=1)
    grads = dot(grad_q, weight_ref[:, :width], NT) + dot(grad_v, weight_ref[:, width:], NT)
    xhat, rstd = normalised(half_ref[...].astype(F32))
    out_ref[...] = (
        grad_ref[...].astype(F32) + norm_back(grads * gain_ref[0:1, :], xhat, rstd)
    ).astype(BF16)


def cube_plan(
    first_half,
    second_half,
    grad_first,
    grad_second,
    qk_weight,
    value_weight,
    out_weight,
    attn_gain,
    ffn_gain,
    up_weight,
    down_weight,
    stretch_ids,
):
    y, core, z_hi, z_lo, x = (lax.axis_index(name) for name in BITS)
    me = y * 16 + core * 8 + z_hi * 4 + z_lo * 2 + x
    place = jnp.stack([me, me & 7]).astype(I32)
    rows, width = first_half.shape
    wide_rows = rows * 8
    own_rows = qk_weight.shape[0]
    own_units = down_weight.shape[0]
    units = own_units * 4
    rounds, tokens = stretch_ids.shape
    nchunk = tokens // STRETCH
    row_block = shaped(rows, width)
    acc_shape = shaped(rows, width, dtype=F32)

    blocks = gather_zx(second_half)
    gains = jnp.pad(jnp.stack([attn_gain, ffn_gain], axis=1), ((0, 0), (0, DH - 2)))
    columns, z_rows, qv_rows = call(
        pack_kernel,
        [Far(a) for a in (qk_weight, value_weight, out_weight, up_weight, down_weight, gains)],
        [
            shaped(NH, own_rows, 3 * DH),
            shaped(own_units + own_rows // 2, 2 * width),
            shaped(own_rows, 2 * width),
        ],
        "pack",
        cost=None,
        far_out=(1, 2),
    )
    columns = shares(lax.all_to_all(columns, HEAD_AXES, 0, 0, tiled=True))
    weights = lax.all_gather(after(z_rows, blocks[4]), ("z_hi", "z_lo"), axis=0)
    cotangent_y = swap(grad_second, Y)

    ids = stretch_ids.reshape(rounds, 2, 2, 2, 2, 2, rows)
    for axis, bit in enumerate((y, core, z_hi, z_lo, x), 1):
        ids = jnp.where(bit == 1, jnp.flip(ids, axis), ids)
    ids = ids.reshape(rounds, tokens)

    def packed(numbers):
        return sum(numbers[r] << (8 * r) for r in range(rounds))

    ids_row = packed(ids)
    ids_rows = jnp.concatenate(
        [
            ids_row[None],
            packed((ids + nchunk - 1) % nchunk)[None],
            packed((ids + 1) % nchunk)[None],
            jnp.zeros((5, tokens), I32),
        ]
    )
    ids_column = call(
        column_kernel, [Far(ids_rows)], [shaped(tokens, 1, dtype=I32)], "ids", far_out=(0,), cost=None
    )[0]
    ids_both = (ids_column, ids_rows)

    columns[0] = after(columns[0], *ids_both, cotangent_y)
    normed, queries, kv, norms, norm_row, gain_rows = call(
        project_kernel,
        [Far(blocks[0]), *blocks[1:], *columns],
        [
            shaped(wide_rows, width),
            shaped(wide_rows, DH),
            shaped(wide_rows, 2 * DH),
            shaped(wide_rows, 1, dtype=F32),
            shaped(8, wide_rows, dtype=F32),
            shaped(8, width, dtype=F32),
        ],
        "project",
        cost=None,
        far_out=range(6),
        scalars=[place],
        scratch=[pltpu.VMEM((width, 3 * DH), BF16)],
    )
    kv_parts = shares(kv)
    near, near_y = after(grad_second, kv), after(cotangent_y, kv)
    cotangents = [near, swap(near, X), near_y, swap(near_y, X)]
    acc, = forward_call(queries, norms, ids_both, kv_parts[:2], 0, None)
    kv_parts[2] = after(kv_parts[2], acc, *cotangents)
    kv_parts[3] = swap(kv_parts[2], CORE)
    qv_full = lax.all_gather(after(qv_rows, kv_parts[2]), BITS, axis=0, tiled=True)
    acc, = forward_call(queries, norms, ids_both, kv_parts[2:3], 2, acc)
    out_near = near_xy(after(weights, acc)[:, own_units:])
    acc, attn_send = forward_call(queries, norms, ids_both, kv_parts[3:], 3, acc, place)
    cotangents = with_cores([after(a, attn_send) for a in cotangents])
    attn_tok = lax.all_to_all(attn_send, HEAD_AXES, 0, 0, tiled=True)
    units = own_units * 4
    hidden_back = call(
        hidden_back_kernel,
        [*map(Far, cotangents), Far(weights)],
        [shaped(wide_rows, units, dtype=F32)],
        "hidden_back",
        cost=None,
        far_out=(0,),
    )[0]
    out_parts = with_cores([after(a, hidden_back) for a in out_near])
    y_first, first_out, normed_ffn, out_full = call(
        out_kernel,
        [attn_tok, Far(first_half), Far(gain_rows), *out_parts],
        [row_block, acc_shape, row_block, shaped(width, width)],
        "project_out",
        cost=None,
        far_out=(0, 1, 3),
        scalars=[place],
    )
    ffn_in = gather_xy(normed_ffn)
    *grad_blocks, hidden, grad_pre = call(
        ffn_kernel,
        [Far(ffn_in[0]), *ffn_in[1:], Far(hidden_back), Far(weights)],
        [row_block] * 8 + [shaped(wide_rows, units)] * 2,
        "feed_forward",
        cost=None,
        mib=44,
        far_out=(8, 9),
    )
    grad_parts = scatter_xy(grad_blocks)
    ffn_near, ffn_far, grad_ffn = call(
        ffn_rest_kernel,
        [Far(ffn_in[0]), *ffn_in[1:], *map(Far, (*cotangents, hidden, grad_pre, weights))],
        [shaped(4, rows, width)] * 2 + [shaped(units, 2 * width)],
        "feed_forward_rest",
        cost=None,
        far_out=range(3),
        mib=48,
    )
    out_width = width + DH
    half = shaped(width // 2, out_width)
    grad_mid, grad_attn, keep, move = call(
        mid_kernel,
        [
            *grad_parts,
            *map(Far, (after(first_out, grad_ffn, qv_full), grad_first, gain_rows, out_full)),
            Far(attn_tok),
        ],
        [row_block, shaped(NH, rows, DH), half, half],
        "mid",
        lazy=True,
        cost=None,
        far_out=(0, 2),
        scalars=[place],
    )

    grad_attn = lax.all_to_all(grad_attn, HEAD_AXES, 0, 0, tiled=True)

    def halve(keep, came, shift, blocks):
        half = shaped(keep.shape[0] // 2, out_width)
        return call(
            functools.partial(halve_kernel, shift=shift, blocks=blocks),
            [Far(keep), came],
            [half, half],
            "halve",
            lazy=True,
            far_out=(0,),
            scalars=[place],
        )

    keep, move = halve(keep, swap(move, CORE), 4, 1)
    ffn_far = swap(after(ffn_far, move), CORE)
    came = swap(move, Y)
    ffn_sum = ffn_near.astype(F32) + ffn_far.astype(F32)
    ffn_move = ffn_sum[1::2].astype(BF16)
    grads, term_row = call(
        turn_kernel,
        [after(grad_attn, move, ffn_move), Far(acc)],
        [shaped(wide_rows, DH), shaped(8, wide_rows, dtype=F32)],
        "turn",
        lazy=True,
        far_out=(0, 1),
        scalars=[place],
        scratch=[pltpu.VMEM((wide_rows, 1), F32)],
    )

    def backward(part, acc):
        return backward_call(
            queries, grads, norm_row, term_row, ids_both, kv_parts[part : part + 2], part, acc
        )

    grad_ffn = lax.psum_scatter(
        grad_ffn, ("z_hi", "z_lo"), scatter_dimension=0, tiled=True
    )
    direct, over_y, far = backward(2, None)
    far = swap(far, CORE)
    keep, move = halve(keep, after(came, direct), 0, 4)
    over_y = (over_y.astype(F32) + after(far, move).astype(F32)).astype(BF16)
    ffn_move = swap(ffn_move, X)
    direct = after(direct, over_y, ffn_move)
    over_y = swap(over_y, Y)
    came = swap(move, X)
    direct, grad_kv, over_core = backward(0, direct)
    direct = after(direct, grad_ffn)
    over_core = swap(after(over_core, over_y), CORE)

    send, *grad_rows = call(
        gather_grads_kernel,
        [*map(Far, (direct, queries, norms, normed, grad_kv)), over_core, over_y],
        [shaped(NH, rows, 2 * DH)] + [shaped(NH, own_rows, 2 * DH)] * 4,
        "gather_grads",
        scalars=[place],
        scratch=[pltpu.VMEM((wide_rows, 2 * DH), BF16), pltpu.VMEM((width, 2 * DH), F32)],
    )
    arrived = lax.all_to_all(send, HEAD_AXES, 0, 0, tiled=True)
    grad_rows = call(
        sum_kernel,
        sum_shares(grad_rows),
        [shaped(NH, own_rows, 2 * DH)],
        "sum_rows",
        scalars=[place],
    )
    rows_send = grad_rows[0]
    grad_up, grad_down = call(
        unpack_kernel,
        [Far(after(grad_ffn, rows_send))],
        [shaped(width, own_units, dtype=F32), shaped(own_units, width, dtype=F32)],
        "unpack",
        far_out=(0, 1),
    )
    arrived = after(arrived, rows_send, grad_up)
    grad_rows = lax.all_to_all(after(rows_send, arrived), HEAD_AXES, 0, 0, tiled=True)
    grad_second_half = call(
        last_kernel,
        [arrived, *map(Far, (second_half, grad_second, gain_rows, qv_full))],
        [row_block],
        "last",
        lazy=True,
        far_out=(0,),
    )[0]

    grad_out = call(
        quarter_kernel,
        [keep, after(came, rows_send)],
        [shaped(own_rows, out_width)] * 4,
        "quarter",
        scalars=[place],
    )
    grad_out = sum(
        after(swap(part, p * Z_LO) if p else part, arrived).astype(F32)
        for p, part in enumerate(grad_out)
    )
    ffn_sum = ffn_sum[0::2] + after(ffn_move, rows_send).astype(F32)
    ffn_sum = ffn_sum[0] + after(swap(ffn_sum[1].astype(BF16), Y), arrived).astype(F32)
    second_out = second_half.astype(F32) + ffn_sum
    grad_qk, grad_value, grad_attn_gain = call(
        own_rows_kernel,
        [after(grad_rows, grad_second_half, grad_up), Far(qk_weight), Far(value_weight), Far(gains)],
        [shaped(own_rows, width, dtype=F32)] * 2 + [shaped(own_rows, 128, dtype=F32)],
        "own_rows",
        lazy=True,
        far_out=(0, 1),
    )

    return (
        y_first,
        second_out.astype(BF16),
        grad_mid,
        grad_second_half,
        grad_qk,
        grad_value,
        grad_out[:, :width],
        grad_attn_gain[:, 0],
        grad_out[:, width],
        grad_up,
        grad_down,
    )


def solution(mesh):
    if dict(mesh.shape) == {"head": 4, "blk": 8}:
        plan, axes = cube_plan, BITS
        mesh = jax.sharding.Mesh(mesh.devices.reshape((2,) * 5), BITS)
    else:
        plan, axes = ring_plan, ("head", "blk")
    by_row, by_column, vector = P(axes, None), P(None, axes), P(axes)
    return jax.shard_map(
        plan,
        mesh=mesh,
        in_specs=(by_row,) * 7 + (vector, vector, by_column, by_row, P()),
        out_specs=(by_row,) * 7 + (vector, vector, by_column, by_row),
        check_vma=False,
    )
```
